128 devices in a mesh: dp: 64 (over y, z, x), blk: 2 (over core).
Axes of the slice: x: 4, y: 4, z: 4, core: 2. Of those that a mesh axis runs over, the one named last changes fastest.
Arguments:
- segment: bfloat16 [64, 512, 1024], P('dp', 'blk'), may hold values from -6 to 6
- memory: bfloat16 [64, 384, 1024], P('dp', 'blk'), may hold values from -6 to 6
- compressed: bfloat16 [64, 512, 1024], P('dp', 'blk'), may hold values from -6 to 6
- mem_count: int32 [64], P('dp'), may hold values from 0 to 384, as said below
- comp_count: int32 [64], P('dp'), may hold values from 0 to 512, as said below
- attn_gain: bfloat16 [1024], P(('dp', 'blk')), may hold values from 0.5 to 1.5
- w_query: bfloat16 [1024, 1024], P(('dp', 'blk')), may hold values from -0.1875 to 0.1875
- w_key: bfloat16 [1024, 1024], P(('dp', 'blk')), may hold values from -0.1875 to 0.1875
- w_value: bfloat16 [1024, 1024], P(('dp', 'blk')), may hold values from -0.1875 to 0.1875
- u_bias: bfloat16 [1024], P(('dp', 'blk')), may hold values from -3 to 3
- v_bias: bfloat16 [1024], P(('dp', 'blk')), may hold values from -3 to 3
- w_rel: bfloat16 [1024, 1024], P(('dp', 'blk')), may hold values from -0.1875 to 0.1875
- w_proj: bfloat16 [1024, 1024], P(('dp', 'blk')), may hold values from -1.5 to 1.5
- ffn_gain: bfloat16 [1024], P(('dp', 'blk')), may hold values from 0.5 to 1.5
- w_in: bfloat16 [1024, 4096], P(('dp', 'blk')), may hold values from -0.1875 to 0.1875
- b_in: bfloat16 [4096], P(('dp', 'blk')), may hold values from -3 to 3
- w_out: bfloat16 [4096, 1024], P(('dp', 'blk')), may hold values from -0.09375 to 0.09375
- b_out: bfloat16 [1024], P(('dp', 'blk')), may hold values from -2 to 2
- w_comp: bfloat16 [3072, 1024], P(('dp', 'blk')), may hold values from -0.109375 to 0.109375
- b_comp: bfloat16 [1024], P(('dp', 'blk')), may hold values from -2 to 2
- out_grad: bfloat16 [64, 512, 1024], P('dp', 'blk'), may hold values from -6 to 6
- comp_grad: bfloat16 [64, 128, 1024], P('dp', 'blk'), may hold values from -6 to 6
Outputs:
- output: bfloat16 [64, 512, 1024], P('dp', 'blk')
- new_compressed: bfloat16 [64, 128, 1024], P('dp', 'blk')
- d_segment: float32 [64, 512, 1024], P('dp', 'blk')
- d_attn_gain: float32 [1024], P('blk')
- d_query: float32 [1024, 1024], P('blk')
- d_key: float32 [1024, 1024], P('blk')
- d_value: float32 [1024, 1024], P('blk')
- d_u_bias: float32 [1024], P('blk')
- d_v_bias: float32 [1024], P('blk')
- d_rel: float32 [1024, 1024], P('blk')
- d_proj: float32 [1024, 1024], P('blk')
- d_ffn_gain: float32 [1024], P('blk')
- d_in: float32 [1024, 4096], P('blk')
- d_b_in: float32 [4096], P('blk')
- d_out: float32 [4096, 1024], P('blk')
- d_b_out: float32 [1024], P('blk')
- d_comp: float32 [3072, 1024], P('blk')
- d_b_comp: float32 [1024], P('blk')
The draws below stay inside these ranges and needn't reach their ends.
Inputs may be any that keep to these rules, and one draw needn't show every extreme that they name: mem_count is the number of valid memory slots of a sequence, which are its last ones; some sequence has all 384. comp_count is the number of valid compressed slots of a sequence, which are its last ones; some sequence has all 512.
All inputs are finite; a program needn't handle non-finite values.
Results may differ from the reference program's by a relative error of at most 0.017.
Values may be sent and summed in bfloat16 or wider, within the bound.
No kernel may reach another device: no remote copies, remote signals or barrier semaphores. Data moves between devices by JAX's collectives and lax.ppermute only.
A program may use at most 256 MiB of HBM per device.

```python
import math
import jax
import jax.numpy as jnp
from jax import lax

D = 1024
HEAD_DIM = 128
FF = 4096
SEG = 512
MEM = 384
COMP = 512
RATE = 3
SEQS = 64
KTOT = 1408
NEWC = 128


def full_somewhere(key, upper):
    key_counts, key_pick = jax.random.split(key)
    counts = jax.random.randint(key_counts, (SEQS,), 0, upper + 1)
    chosen = jax.random.randint(key_pick, (), 0, SEQS)
    return jnp.where(jnp.arange(SEQS) == chosen, upper, counts).astype(jnp.int32)


def draw_mem_count(key, part):
    key = jax.random.fold_in(key, 11)
    return full_somewhere(key, MEM)


def draw_comp_count(key, part):
    key = jax.random.fold_in(key, 23)
    return full_somewhere(key, COMP)


def block_levels(own_key, dims, cuts, low, largest):
    loudness, own = 1.0, jax.random.fold_in(own_key, 6)
    for axis_at, parts in cuts:
        draws = jnp.exp(jax.random.uniform(jax.random.fold_in(own, axis_at), (parts,), jnp.float32, low / len(cuts), largest / len(cuts)))
        loudness = loudness * jnp.repeat(draws, dims[axis_at] // parts).reshape([-1 if axis == axis_at else 1 for axis in range(len(dims))])
    return loudness


def gaussian(own_key, extent, width, limit, cuts=(), kind=jnp.bfloat16):
    loudness = block_levels(own_key, extent, cuts, -0.22, 0.18) if cuts else 1.0
    array = jax.random.normal(own_key, extent, jnp.float32) * width * loudness
    return jnp.minimum(jnp.maximum(array, -limit), limit).astype(kind)


def setup_inputs(seed: int = 0) -> dict:
    arg_keys = jax.random.split(jax.random.key(seed), 23)
    segment = gaussian(arg_keys[0], (SEQS, SEG, D), 1.0, 6.0, ((0, 64), (1, 2)))
    memory = gaussian(arg_keys[1], (SEQS, MEM, D), 1.0, 6.0, ((0, 64), (1, 2)))
    compressed = gaussian(arg_keys[2], (SEQS, COMP, D), 1.0, 6.0, ((0, 64), (1, 2)))
    mem_count = draw_mem_count(jax.random.fold_in(arg_keys[22], 71), 0)
    comp_count = draw_comp_count(jax.random.fold_in(arg_keys[22], 71), 0)
    attn_gain = jnp.clip(1.0 + 0.1 * jax.random.normal(arg_keys[5], (D,), jnp.float32), 0.5, 1.5).astype(jnp.bfloat16)
    w_query = gaussian(arg_keys[6], (D, D), D ** -0.5, 0.1875, ((0, 128),))
    w_key = gaussian(arg_keys[7], (D, D), D ** -0.5, 0.1875, ((0, 128),))
    w_value = gaussian(arg_keys[8], (D, D), D ** -0.5, 0.1875, ((0, 128),))
    u_bias = gaussian(arg_keys[9], (D,), 0.5, 3.0, ((0, 128),))
    v_bias = gaussian(arg_keys[10], (D,), 0.5, 3.0, ((0, 128),))
    w_rel = gaussian(arg_keys[11], (D, D), D ** -0.5, 0.1875, ((0, 128),))
    w_proj = gaussian(arg_keys[12], (D, D), (D // 64) ** -0.5, 1.5, ((0, 128),))
    ffn_gain = jnp.clip(1.0 + 0.1 * jax.random.normal(arg_keys[13], (D,), jnp.float32), 0.5, 1.5).astype(jnp.bfloat16)
    w_in = gaussian(arg_keys[14], (D, FF), D ** -0.5, 0.1875, ((0, 128),))
    b_in = gaussian(arg_keys[15], (FF,), 0.5, 3.0, ((0, 128),))
    w_out = gaussian(arg_keys[16], (FF, D), FF ** -0.5, 0.09375, ((0, 128),))
    b_out = gaussian(arg_keys[17], (D,), 0.3, 2.0, ((0, 128),))
    w_comp = gaussian(arg_keys[18], (RATE * D, D), (RATE * D) ** -0.5, 0.109375, ((0, 128),))
    b_comp = gaussian(arg_keys[19], (D,), 0.3, 2.0, ((0, 128),))
    out_grad = gaussian(arg_keys[20], (SEQS, SEG, D), 1.0, 6.0, ((0, 64), (1, 2)))
    comp_grad = gaussian(arg_keys[21], (SEQS, NEWC, D), 1.0, 6.0, ((0, 64), (1, 2)))
    return dict(segment=segment, memory=memory, compressed=compressed, mem_count=mem_count, comp_count=comp_count, attn_gain=attn_gain, w_query=w_query, w_key=w_key, w_value=w_value, u_bias=u_bias, v_bias=v_bias, w_rel=w_rel, w_proj=w_proj, ffn_gain=ffn_gain, w_in=w_in, b_in=b_in, w_out=w_out, b_out=b_out, w_comp=w_comp, b_comp=b_comp, out_grad=out_grad, comp_grad=comp_grad)


@jax.custom_vjp
def low(v):
    return lax.optimization_barrier(v.astype(jnp.bfloat16)).astype(jnp.float32)

@jax.custom_vjp
def low_back(v):
    return v

def low_keep(v):
    return (low(v), None)

def low_pass(kept, grad):
    return (grad,)

def back_keep(v):
    return (v, None)

def back_low(kept, grad):
    return (low(grad),)
low.defvjp(low_keep, low_pass)
low_back.defvjp(back_keep, back_low)
EPSILON = 1e-05
NEG_FILL = -1e+30
PRECISE = lax.Precision.HIGHEST

def norm_rows(row_vals, gain_vec):
    average = lax.optimization_barrier(jnp.mean(row_vals, axis=-1, keepdims=True))
    centred = row_vals - average
    variance = lax.optimization_barrier(jnp.mean(centred * centred, axis=-1, keepdims=True))
    return centred * lax.rsqrt(variance + EPSILON) * gain_vec

def key_mask(query_pos, mem_valid, comp_valid):
    key_pos = jnp.arange(KTOT, dtype=jnp.int32)
    in_comp = (key_pos < COMP) & (key_pos >= COMP - comp_valid)
    in_mem = (key_pos >= COMP) & (key_pos < COMP + MEM) & (key_pos >= COMP + MEM - mem_valid)
    in_seg = (key_pos[None, :] >= COMP + MEM) & (key_pos[None, :] <= query_pos[:, None])
    return (in_comp | in_mem)[None, :] | in_seg

def attend(rel_rows, members):
    query_u, query_v, key_rows, value_rows, mem_valid, comp_valid = members
    head_count = D // HEAD_DIM
    query_pos = COMP + MEM + jnp.arange(SEG, dtype=jnp.int32)
    key_pos = jnp.arange(KTOT, dtype=jnp.int32)
    visible = key_mask(query_pos, mem_valid, comp_valid)
    qu_heads = query_u.reshape(SEG, head_count, HEAD_DIM)
    qv_heads = query_v.reshape(SEG, head_count, HEAD_DIM)
    key_heads = key_rows.reshape(KTOT, head_count, HEAD_DIM)
    value_heads = value_rows.reshape(KTOT, head_count, HEAD_DIM)
    rel_heads = rel_rows.reshape(-1, head_count, HEAD_DIM)
    content = jnp.einsum('qhd,khd->hqk', qu_heads, key_heads, precision=PRECISE)
    wide_pos = jnp.einsum('qhd,rhd->hqr', qv_heads, rel_heads, precision=PRECISE)
    rel_index = (query_pos[:, None] - key_pos[None, :] + SEG).astype(jnp.int32)
    placed = jnp.take_along_axis(wide_pos, jnp.broadcast_to(rel_index[None], (head_count, SEG, KTOT)), axis=2)
    scores = low_back((content + placed) * (1.0 / math.sqrt(HEAD_DIM)))
    scores = jnp.where(visible[None], scores, NEG_FILL)
    row_max = lax.optimization_barrier(jnp.max(scores, axis=-1, keepdims=True))
    shifted = jnp.exp(scores - row_max)
    prob_low = low(shifted / lax.optimization_barrier(jnp.sum(shifted, axis=-1, keepdims=True)))
    mixed_rows = jnp.einsum('hqk,khd->qhd', prob_low, value_heads, precision=PRECISE)
    return mixed_rows.reshape(SEG, D)

def project(left_side, right_side):
    return jnp.einsum('skd,de->ske', left_side, right_side, precision=PRECISE)

def reference(segment, memory, compressed, mem_count, comp_count, attn_gain, w_query, w_key, w_value, u_bias, v_bias, w_rel, w_proj, ffn_gain, w_in, b_in, w_out, b_out, w_comp, b_comp, out_grad, comp_grad):
    mem_rows = memory.astype(jnp.float32)
    comp_rows = compressed.astype(jnp.float32)
    frequency = jnp.exp(jnp.arange(D // 2, dtype=jnp.float32) * (-2.0 * math.log(10000.0) / D))
    distance = jnp.arange(KTOT + SEG, dtype=jnp.float32) - SEG
    angles = distance[:, None] * frequency[None, :]
    pos_table = jnp.concatenate([jnp.sin(angles), jnp.cos(angles)], axis=1)
    pos_table = low(jnp.where(distance[:, None] >= 0.0, pos_table, jnp.zeros_like(pos_table)))
    slot_pos = jnp.arange(MEM, dtype=jnp.int32)
    kept_slots = (slot_pos[None, :] >= MEM - mem_count[:, None]).astype(jnp.float32)
    windows = (mem_rows * kept_slots[:, :, None]).reshape(SEQS, NEWC, RATE * D)

    def forward(seg_rows, gain_attn, proj_query, proj_key, proj_value, bias_u, bias_v, proj_rel, proj_out, gain_ffn, ffn_in, ffn_bias, ffn_out, out_bias, comp_proj, comp_bias):
        raw_rows = jnp.concatenate([comp_rows, mem_rows, seg_rows], axis=1)
        joined = low(norm_rows(raw_rows, gain_attn))
        act_seg = joined[:, COMP + MEM:]
        query_rows = low_back(project(act_seg, proj_query))
        key_rows = low_back(low(project(joined, proj_key)))
        value_rows = low_back(low(project(joined, proj_value)))
        query_u = low(query_rows + bias_u)
        query_v = low(query_rows + bias_v)
        rel_rows = low_back(low(jnp.dot(pos_table, proj_rel, precision=PRECISE)))
        mixed = lax.map(lambda members: jax.checkpoint(attend)(rel_rows, members), (query_u, query_v, key_rows, value_rows, mem_count, comp_count))
        attended = low_back(low(mixed))
        hidden = seg_rows + low_back(project(attended, proj_out))
        act_two = low(norm_rows(hidden, gain_ffn))
        pre_act = low_back(project(act_two, ffn_in) + ffn_bias)
        act_ffn = low(jax.nn.gelu(pre_act, approximate=True))
        result = hidden + low_back(project(act_ffn, ffn_out) + out_bias)
        new_comp = project(windows, comp_proj) + comp_bias
        return (result, new_comp)
    primals = (segment.astype(jnp.float32), attn_gain.astype(jnp.float32), w_query.astype(jnp.float32), w_key.astype(jnp.float32), w_value.astype(jnp.float32), u_bias.astype(jnp.float32), v_bias.astype(jnp.float32), w_rel.astype(jnp.float32), w_proj.astype(jnp.float32), ffn_gain.astype(jnp.float32), w_in.astype(jnp.float32), b_in.astype(jnp.float32), w_out.astype(jnp.float32), b_out.astype(jnp.float32), w_comp.astype(jnp.float32), b_comp.astype(jnp.float32))
    (result, new_comp), backward = jax.vjp(forward, *primals)
    grads = backward((out_grad.astype(jnp.float32), comp_grad.astype(jnp.float32)))
    return (result.astype(jnp.bfloat16), new_comp.astype(jnp.bfloat16), grads[0], grads[1], grads[2], grads[3], grads[4], grads[5], grads[6], grads[7], grads[8], grads[9], grads[10], grads[11], grads[12], grads[13], grads[14], grads[15])
```

```python
import math, functools
import jax, jax.numpy as jnp
from jax import lax
from jax.sharding import PartitionSpec as P
from jax.experimental import pallas as pl
from jax.experimental.pallas import tpu as pltpu
D=1024
FF=4096
HEAD_DIM=128
SEG=512
MEM=384
COMP=512
RATE=3
KTOT=1408
RELN=1536
QB=128
EPSILON=1e-05
SCALE=1.0/math.sqrt(HEAD_DIM); NEG=-1e30
def tdot(a,b):
    return lax.dot_general(a,b,(((1,),(1,)),((),())),preferred_element_type=jnp.float32)
def ndot(a,b):
    return lax.dot_general(a,b,(((1,),(0,)),((),())),preferred_element_type=jnp.float32)
def cdot(a,b):
    return lax.dot_general(a,b,(((0,),(0,)),((),())),preferred_element_type=jnp.float32)

def attn_fwd_kernel(cnt_ref, qu_ref, qv_ref, k_ref, v_ref, r_ref, att_ref, p_ref):
    mc = cnt_ref[0]; cc = cnt_ref[1]
    kp = lax.broadcasted_iota(jnp.int32,(1,COMP+MEM),1)
    ok = ((kp < COMP) & (kp >= COMP-cc)) | ((kp>=COMP)&(kp>=COMP+MEM-mc))
    old_bias = jnp.where(ok, 0.0, NEG)
    tri = jnp.where(lax.broadcasted_iota(jnp.int32,(QB,QB),1) <= lax.broadcasted_iota(jnp.int32,(QB,QB),0), 0.0, NEG)
    for b in range(SEG//QB):
        i0=QB*b; nk=COMP+MEM+QB*(b+1); c0=SEG-QB-QB*b; wl=nk+QB
        s = tdot(qu_ref[pl.ds(i0,QB),:], k_ref[pl.ds(0,nk),:])
        w = tdot(qv_ref[pl.ds(i0,QB),:], r_ref[pl.ds(c0,wl),:])
        w = pltpu.roll(w, wl-(QB-1), 1, stride=1, stride_axis=0)[:,:nk]
        s = (s+w)*SCALE
        parts=[s[:,:COMP+MEM]+old_bias]
        if b: parts.append(s[:,COMP+MEM:nk-QB])
        parts.append(s[:,nk-QB:]+tri)
        s=jnp.concatenate(parts,axis=1)
        m=jnp.max(s,axis=1,keepdims=True)
        e=jnp.exp(s-m)
        l=jnp.sum(e,axis=1,keepdims=True)
        p=(e*(1.0/l)).astype(jnp.bfloat16)
        p_ref[0,pl.ds(i0,QB),pl.ds(0,nk)]=p
        if nk<KTOT: p_ref[0,pl.ds(i0,QB),pl.ds(nk,KTOT-nk)]=jnp.zeros((QB,KTOT-nk),jnp.bfloat16)
        att_ref[pl.ds(i0,QB),:]=ndot(p,v_ref[pl.ds(0,nk),:]).astype(jnp.bfloat16)

def attn_fwd(cnt,qu,qv,k,v,r):
    nh=qu.shape[1]//HEAD_DIM
    col=lambda n: pl.BlockSpec((n,HEAD_DIM),lambda h:(0,h))
    return pl.pallas_call(attn_fwd_kernel, grid=(nh,),
        in_specs=[pl.BlockSpec(memory_space=pltpu.SMEM),col(SEG),col(SEG),col(KTOT),col(KTOT),col(RELN)],
        out_specs=[col(SEG),pl.BlockSpec((1,SEG,KTOT),lambda h:(h,0,0))],
        out_shape=[jax.ShapeDtypeStruct((SEG,nh*HEAD_DIM),jnp.bfloat16),jax.ShapeDtypeStruct((nh,SEG,KTOT),jnp.bfloat16)],
        compiler_params=pltpu.CompilerParams(vmem_limit_bytes=48<<20),
        cost_estimate=pl.CostEstimate(flops=6*nh*SEG*KTOT*HEAD_DIM,bytes_accessed=12<<20,transcendentals=nh*SEG*KTOT),
        name="attention_forward")(cnt,qu,qv,k,v,r)

def attn_bwd_kernel(p_ref, ga_ref, qu_ref, qv_ref, k_ref, v_ref, r_ref, dq_ref, du_ref, dv_ref, dk_ref, dval_ref, dr_ref, ds_s, dw_s, qvr_s):
    flip=((lax.broadcasted_iota(jnp.int32,(QB,QB),0)+lax.broadcasted_iota(jnp.int32,(QB,QB),1))==QB-1).astype(jnp.float32).astype(jnp.bfloat16)
    du=jnp.zeros((1,HEAD_DIM),jnp.float32); dv=du
    for b in range(SEG//QB):
        i0=QB*b; nk=COMP+MEM+QB*(b+1); c0=SEG-QB-QB*b; wl=nk+QB
        rows=pl.ds(i0,QB)
        p=p_ref[0,rows,pl.ds(0,nk)].astype(jnp.float32)
        dp=tdot(ga_ref[rows,:],v_ref[pl.ds(0,nk),:])
        pd=p*dp
        delta=jnp.sum(pd,axis=1,keepdims=True)
        ds=(pd-p*delta).astype(jnp.bfloat16)
        ds_s[rows,pl.ds(0,nk)]=ds
        if nk<KTOT: ds_s[rows,pl.ds(nk,KTOT-nk)]=jnp.zeros((QB,KTOT-nk),jnp.bfloat16)
        wide=jnp.concatenate([ndot(flip,ds),jnp.zeros((QB,QB),jnp.float32)],axis=1)
        wide=pltpu.roll(wide,0,1,stride=1,stride_axis=0).astype(jnp.bfloat16)
        qvr_s[rows,:]=ndot(flip,qv_ref[rows,:]).astype(jnp.bfloat16)
        dw_s[rows,pl.ds(c0,wl)]=wide
        if c0: dw_s[rows,pl.ds(0,c0)]=jnp.zeros((QB,c0),jnp.bfloat16)
        dqu=ndot(ds,k_ref[pl.ds(0,nk),:])*SCALE
        dqr=ndot(wide,r_ref[pl.ds(c0,wl),:])*SCALE
        hi=dqr.astype(jnp.bfloat16); lo=(dqr-hi.astype(jnp.float32)).astype(jnp.bfloat16)
        dqv=ndot(flip,hi)+ndot(flip,lo)
        du+=jnp.sum(dqu,axis=0,keepdims=True); dv+=jnp.sum(dqv,axis=0,keepdims=True)
        dq_ref[rows,:]=(dqu+dqv).astype(jnp.bfloat16)
    du_ref[...]=du; dv_ref[...]=dv
    dk_ref[...]=(cdot(ds_s[...],qu_ref[...])*SCALE).astype(jnp.bfloat16)
    dr_ref[...]=(cdot(dw_s[...],qvr_s[...])*SCALE).astype(jnp.bfloat16)
    dval_ref[...]=cdot(p_ref[0],ga_ref[...]).astype(jnp.bfloat16)

def attn_bwd(p,ga,qu,qv,k,v,r):
    nh=qu.shape[1]//HEAD_DIM
    col=lambda n: pl.BlockSpec((n,HEAD_DIM),lambda h:(0,h))
    sd=lambda n,dt=jnp.bfloat16: jax.ShapeDtypeStruct((n,nh*HEAD_DIM),dt)
    return pl.pallas_call(attn_bwd_kernel, grid=(nh,),
        in_specs=[pl.BlockSpec((1,SEG,KTOT),lambda h:(h,0,0)),col(SEG),col(SEG),col(SEG),col(KTOT),col(KTOT),col(RELN)],
        out_specs=[col(SEG),col(1),col(1),col(KTOT),col(KTOT),col(RELN)],
        out_shape=[sd(SEG),sd(1,jnp.float32),sd(1,jnp.float32),sd(KTOT),sd(KTOT),sd(RELN)],
        scratch_shapes=[pltpu.VMEM((SEG,KTOT),jnp.bfloat16),pltpu.VMEM((SEG,RELN),jnp.bfloat16),pltpu.VMEM((SEG,HEAD_DIM),jnp.bfloat16)],
        compiler_params=pltpu.CompilerParams(vmem_limit_bytes=48<<20),
        cost_estimate=pl.CostEstimate(flops=12*nh*SEG*KTOT*HEAD_DIM,bytes_accessed=20<<20,transcendentals=0),
        name="attention_backward")(p,ga,qu,qv,k,v,r)


ROWS = 136


def swap(array):
    return lax.ppermute(array, "blk", [(0, 1), (1, 0)])


def on_device(
    segment, memory, compressed, mem_count, comp_count, attn_gain, w_query, w_key, w_value, u_bias, v_bias,
    w_rel, w_proj, ffn_gain, w_in, b_in, w_out, b_out, w_comp, b_comp, out_grad, comp_grad,
):
    f32, bf16 = jnp.float32, jnp.bfloat16
    core = lax.axis_index("blk")
    first = core == 0

    def both(own, other, axis=0):
        return jnp.where(first, jnp.concatenate([own, other], axis), jnp.concatenate([other, own], axis))

    def half(array, which, axis):
        size = array.shape[axis] // 2
        return lax.dynamic_slice_in_dim(array, which * size, size, axis)

    vectors = jnp.concatenate([attn_gain, u_bias, v_bias, ffn_gain, b_in, b_out, b_comp])
    vectors = jnp.pad(vectors[None], ((0, 7), (0, D - vectors.shape[0])))
    shard = jnp.concatenate(
        [w_query, w_key, w_value, w_rel, w_proj]
        + [w_in[:, D * c : D * (c + 1)] for c in range(4)]
        + [w_out, w_comp, vectors]
    )
    every = lax.all_gather(shard, ("dp", "blk"), axis=0, tiled=False)

    def columns(at):
        return half(every[:, at : at + 8].reshape(D, D), core, 1)

    proj_query, proj_key, proj_value, proj_rel = (columns(8 * n) for n in range(4))
    proj_out = every[:, 32:40].reshape(D, D)
    ffn_in = [
        lax.dynamic_slice_in_dim(every, 40 + 16 * core + 8 * c, 8, 1).reshape(D, D) for c in range(2)
    ]
    ffn_out = half(every[:, 72:104].reshape(FF, D), core, 0)
    comp_proj = every[:, 104:128].reshape(RATE * D, D)

    def vector(at, size):
        return every[:, 128, at : at + size].reshape(-1).astype(f32)

    gain_one, bias_u, bias_v, gain_two = (vector(8 * n, 8) for n in range(4))
    ffn_bias, out_bias, comp_bias = vector(32, 32), vector(64, 8), vector(72, 8)

    own_rows = jnp.concatenate([compressed[0], memory[0], segment[0], out_grad[0], comp_grad[0]])
    other_rows = swap(own_rows)
    edges = [0, 256, 448, 704, 960, 1024]
    pieces = [both(own_rows[a:b], other_rows[a:b]) for a, b in zip(edges[:-1], edges[1:])]
    raw_rows = jnp.concatenate(pieces[:3]).astype(f32)
    seg_rows = raw_rows[COMP + MEM :]
    grad_res, comp_flat = pieces[3], pieces[4]

    def stats(rows):
        centred = rows - jnp.mean(rows, axis=-1, keepdims=True)
        inverse = lax.rsqrt(jnp.mean(centred * centred, axis=-1, keepdims=True) + EPSILON)
        return centred * inverse, inverse

    normed, inverse = stats(raw_rows)
    joined = (normed * gain_one).astype(bf16)

    distance = (KTOT - 1) - jnp.arange(RELN, dtype=f32)
    frequency = jnp.exp(jnp.arange(D // 2, dtype=f32) * (-2.0 * math.log(10000.0) / D))
    angles = distance[:, None] * frequency[None, :]
    table = jnp.concatenate([jnp.sin(angles), jnp.cos(angles)], axis=1)
    table = jnp.where(distance[:, None] >= 0.0, table, 0.0).astype(bf16)

    slot = jnp.arange(MEM, dtype=jnp.int32)
    masked = jnp.where((slot >= MEM - mem_count[0])[:, None], pieces[1], jnp.zeros_like(pieces[1]))
    windows = masked.reshape(MEM // RATE, RATE * D)
    d_comp = cdot(half(windows, core, 1), comp_flat)
    new_compressed = (ndot(half(windows, core, 0), comp_proj) + comp_bias).astype(bf16)

    query_rows = ndot(joined[COMP + MEM :], proj_query)
    key_rows = ndot(joined, proj_key).astype(bf16)
    value_rows = ndot(joined, proj_value).astype(bf16)
    rel_rows = ndot(table, proj_rel).astype(bf16)
    query_u = (query_rows + half(bias_u, core, 0)).astype(bf16)
    query_v = (query_rows + half(bias_v, core, 0)).astype(bf16)
    counts = jnp.concatenate([mem_count, comp_count])
    attended, probs = attn_fwd(counts, query_u, query_v, key_rows, value_rows, rel_rows)

    hidden = seg_rows + ndot(both(attended, swap(attended), 1), proj_out)
    normed_two, inverse_two = stats(hidden)
    act_two = (normed_two * gain_two).astype(bf16)
    pre_act = jnp.concatenate([ndot(act_two, part) for part in ffn_in], axis=1) + half(ffn_bias, core, 0)
    inner = math.sqrt(2.0 / math.pi)
    tanh = jnp.tanh(inner * (pre_act + 0.044715 * pre_act * pre_act * pre_act))
    act_ffn = (0.5 * pre_act * (1.0 + tanh)).astype(bf16)
    slope = 0.5 * (1.0 + tanh) + (0.5 * inner) * pre_act * (1.0 - tanh * tanh) * (
        1.0 + (3.0 * 0.044715) * pre_act * pre_act
    )
    grad_pre = tdot(grad_res, ffn_out) * slope
    grad_pre = grad_pre.astype(bf16)
    back = tdot(grad_pre, jnp.concatenate(ffn_in, axis=1))
    back = back + swap(back)
    scaled = back * gain_two
    grad_hidden = grad_res.astype(f32) + inverse_two * (
        scaled
        - jnp.mean(scaled, axis=-1, keepdims=True)
        - normed_two * jnp.mean(scaled * normed_two, axis=-1, keepdims=True)
    )
    grad_branch = grad_hidden.astype(bf16)
    grad_att = tdot(grad_branch, half(proj_out, core, 0)).astype(bf16)

    partial = ndot(act_ffn, ffn_out)
    result = half(hidden, core, 0) + half(partial, core, 0) + swap(half(partial, 1 - core, 0)) + out_bias
    output = result.astype(bf16)[None]

    def rows_of(left, right):
        keep = cdot(half(left, core, 1), right)
        send = cdot(half(left, 1 - core, 1), right)
        return keep, send

    def turned(keep, send):
        return both(keep.astype(bf16), swap(send.astype(bf16)), 1)

    d_in = turned(*rows_of(act_two, grad_pre))
    d_out = cdot(act_ffn, grad_res)
    d_proj = cdot(attended, grad_branch)
    early = jnp.concatenate(
        [d_in[:, D * c : D * (c + 1)] for c in range(4)] + [d_out.astype(bf16), d_comp.astype(bf16), d_proj.astype(bf16)]
    )
    early = lax.psum(early, "dp")

    grad_query, d_u, d_v, grad_keys, grad_values, grad_rel = attn_bwd(
        probs, grad_att, query_u, query_v, key_rows, value_rows, rel_rows
    )
    pair_query = rows_of(joined[COMP + MEM :], grad_query)
    pair_key = rows_of(joined, grad_keys)
    pair_value = rows_of(joined, grad_values)
    pair_rel = rows_of(table, grad_rel)

    def gain_share(which, at):
        total = sum(
            jnp.sum(pair[which] * half(weight, at, 0).astype(f32), axis=1)
            for pair, weight in (
                (pair_query, proj_query),
                (pair_key, proj_key),
                (pair_value, proj_value),
            )
        )
        return total / half(gain_one, at, 0)

    d_gain_one = gain_share(0, core) + swap(gain_share(1, 1 - core))
    d_gain_two = jnp.sum(half(back, core, 1) * half(normed_two, core, 1), axis=0)
    d_b_in = jnp.sum(grad_pre.astype(f32), axis=0)
    d_b_out = jnp.sum(half(grad_res, core, 1).astype(f32), axis=0)
    d_b_comp = jnp.sum(half(comp_flat, core, 1).astype(f32), axis=0)
    small = jnp.concatenate([d_gain_one, d_u[0], d_v[0], d_gain_two, d_b_in, d_b_out, d_b_comp])
    small = jnp.pad(small, (0, 8 * D - small.shape[0])).reshape(8, D)
    late = jnp.concatenate(
        [turned(*pair) for pair in (pair_query, pair_key, pair_value, pair_rel)] + [small.astype(bf16)]
    )
    late, early = lax.optimization_barrier((late, early))
    late = lax.psum(late, "dp")

    seg_at = COMP + MEM
    grad_seg = (
        tdot(grad_query, proj_query) + tdot(grad_keys[seg_at:], proj_key) + tdot(grad_values[seg_at:], proj_value)
    )
    grad_seg = half(grad_seg, core, 0) + swap(half(grad_seg, 1 - core, 0))
    scaled_one = grad_seg * gain_one
    normed_seg, inverse_seg = half(normed[seg_at:], core, 0), half(inverse[seg_at:], core, 0)
    d_segment = half(grad_hidden, core, 0) + inverse_seg * (
        scaled_one
        - jnp.mean(scaled_one, axis=-1, keepdims=True)
        - normed_seg * jnp.mean(scaled_one * normed_seg, axis=-1, keepdims=True)
    )

    early, late = early.astype(f32), late.astype(f32)
    d_in = jnp.concatenate([early[512 * c : 512 * (c + 1)] for c in range(4)], axis=1)
    small = late[2048:].reshape(-1)
    return (
        output,
        new_compressed[None],
        d_segment[None],
        small[:512],
        late[:512],
        late[512:1024],
        late[1024:1536],
        small[512:1024],
        small[1024:1536],
        late[1536:2048],
        early[5632:6144],
        small[1536:2048],
        d_in,
        small[2048:4096],
        early[2048:4096],
        small[4096:4608],
        early[4096:5632],
        small[4608:5120],
    )


def solution(mesh):
    rows, weight, vector = P("dp", "blk", None), P(("dp", "blk"), None), P(("dp", "blk"))
    placed = (
        rows, rows, rows, P("dp"), P("dp"), vector, weight, weight, weight, vector, vector,
        weight, weight, vector, weight, vector, weight, vector, weight, vector, rows, rows,
    )
    half_one, half_two = P("blk"), P("blk", None)
    return jax.shard_map(
        on_device,
        mesh=mesh,
        in_specs=placed,
        out_specs=(
            rows, rows, rows, half_one, half_two, half_two, half_two, half_one, half_one,
            half_two, half_two, half_one, half_two, half_one, half_two, half_one, half_two, half_one,
        ),
        check_vma=False,
    )
```

```python
import math, functools
import jax, jax.numpy as jnp
from jax import lax
from jax.sharding import PartitionSpec as P
from jax.experimental import pallas as pl
from jax.experimental.pallas import tpu as pltpu
D=1024
FF=4096
HEAD_DIM=128
SEG=512
MEM=384
COMP=512
RATE=3
KTOT=1408
RELN=1536
QB=128
EPSILON=1e-05
SCALE=1.0/math.sqrt(HEAD_DIM); NEG=-1e30
def tdot(a,b):
    return lax.dot_general(a,b,(((1,),(1,)),((),())),preferred_element_type=jnp.float32)
def ndot(a,b):
    return lax.dot_general(a,b,(((1,),(0,)),((),())),preferred_element_type=jnp.float32)
def cdot(a,b):
    return lax.dot_general(a,b,(((0,),(0,)),((),())),preferred_element_type=jnp.float32)

def attn_fwd_kernel(cnt_ref, qu_ref, qv_ref, k_ref, v_ref, r_ref, att_ref, p_ref):
    mc = cnt_ref[0]; cc = cnt_ref[1]
    kp = lax.broadcasted_iota(jnp.int32,(1,COMP+MEM),1)
    ok = ((kp < COMP) & (kp >= COMP-cc)) | ((kp>=COMP)&(kp>=COMP+MEM-mc))
    old_bias = jnp.where(ok, 0.0, NEG)
    tri = jnp.where(lax.broadcasted_iota(jnp.int32,(QB,QB),1) <= lax.broadcasted_iota(jnp.int32,(QB,QB),0), 0.0, NEG)
    for b in range(SEG//QB):
        i0=QB*b; nk=COMP+MEM+QB*(b+1); c0=SEG-QB-QB*b; wl=nk+QB
        s = tdot(qu_ref[pl.ds(i0,QB),:], k_ref[pl.ds(0,nk),:])
        w = tdot(qv_ref[pl.ds(i0,QB),:], r_ref[pl.ds(c0,wl),:])
        w = pltpu.roll(w, wl-(QB-1), 1, stride=1, stride_axis=0)[:,:nk]
        s = (s+w)*SCALE
        parts=[s[:,:COMP+MEM]+old_bias]
        if b: parts.append(s[:,COMP+MEM:nk-QB])
        parts.append(s[:,nk-QB:]+tri)
        s=jnp.concatenate(parts,axis=1)
        m=jnp.max(s,axis=1,keepdims=True)
        e=jnp.exp(s-m)
        l=jnp.sum(e,axis=1,keepdims=True)
        p=(e*(1.0/l)).astype(jnp.bfloat16)
        p_ref[0,pl.ds(i0,QB),pl.ds(0,nk)]=p
        if nk<KTOT: p_ref[0,pl.ds(i0,QB),pl.ds(nk,KTOT-nk)]=jnp.zeros((QB,KTOT-nk),jnp.bfloat16)
        att_ref[pl.ds(i0,QB),:]=ndot(p,v_ref[pl.ds(0,nk),:]).astype(jnp.bfloat16)

def attn_fwd(cnt,qu,qv,k,v,r):
    nh=qu.shape[1]//HEAD_DIM
    col=lambda n: pl.BlockSpec((n,HEAD_DIM),lambda h:(0,h))
    return pl.pallas_call(attn_fwd_kernel, grid=(nh,),
        in_specs=[pl.BlockSpec(memory_space=pltpu.SMEM),col(SEG),col(SEG),col(KTOT),col(KTOT),col(RELN)],
        out_specs=[col(SEG),pl.BlockSpec((1,SEG,KTOT),lambda h:(h,0,0))],
        out_shape=[jax.ShapeDtypeStruct((SEG,nh*HEAD_DIM),jnp.bfloat16),jax.ShapeDtypeStruct((nh,SEG,KTOT),jnp.bfloat16)],
        compiler_params=pltpu.CompilerParams(vmem_limit_bytes=60<<20),
        cost_estimate=pl.CostEstimate(flops=6*nh*SEG*KTOT*HEAD_DIM,bytes_accessed=12<<20,transcendentals=nh*SEG*KTOT),
        name="attention_forward")(cnt,qu,qv,k,v,r)

def attn_bwd_kernel(p_ref, ga_ref, qu_ref, qv_ref, k_ref, v_ref, r_ref, dq_ref, du_ref, dv_ref, dk_ref, dval_ref, dr_ref, ds_s, dw_s, qvr_s):
    flip=((lax.broadcasted_iota(jnp.int32,(QB,QB),0)+lax.broadcasted_iota(jnp.int32,(QB,QB),1))==QB-1).astype(jnp.float32).astype(jnp.bfloat16)
    du=jnp.zeros((1,HEAD_DIM),jnp.float32); dv=du
    for b in range(SEG//QB):
        i0=QB*b; nk=COMP+MEM+QB*(b+1); c0=SEG-QB-QB*b; wl=nk+QB
        rows=pl.ds(i0,QB)
        p=p_ref[0,rows,pl.ds(0,nk)].astype(jnp.float32)
        dp=tdot(ga_ref[rows,:],v_ref[pl.ds(0,nk),:])
        pd=p*dp
        delta=jnp.sum(pd,axis=1,keepdims=True)
        ds=(pd-p*delta).astype(jnp.bfloat16)
        ds_s[rows,pl.ds(0,nk)]=ds
        if nk<KTOT: ds_s[rows,pl.ds(nk,KTOT-nk)]=jnp.zeros((QB,KTOT-nk),jnp.bfloat16)
        wide=jnp.concatenate([ndot(flip,ds),jnp.zeros((QB,QB),jnp.float32)],axis=1)
        wide=pltpu.roll(wide,0,1,stride=1,stride_axis=0).astype(jnp.bfloat16)
        qvr_s[rows,:]=ndot(flip,qv_ref[rows,:]).astype(jnp.bfloat16)
        dw_s[rows,pl.ds(c0,wl)]=wide
        if c0: dw_s[rows,pl.ds(0,c0)]=jnp.zeros((QB,c0),jnp.bfloat16)
        dqu=ndot(ds,k_ref[pl.ds(0,nk),:])*SCALE
        dqr=ndot(wide,r_ref[pl.ds(c0,wl),:])*SCALE
        hi=dqr.astype(jnp.bfloat16); lo=(dqr-hi.astype(jnp.float32)).astype(jnp.bfloat16)
        dqv=ndot(flip,hi)+ndot(flip,lo)
        du+=jnp.sum(dqu,axis=0,keepdims=True); dv+=jnp.sum(dqv,axis=0,keepdims=True)
        dq_ref[rows,:]=(dqu+dqv).astype(jnp.bfloat16)
    du_ref[...]=du; dv_ref[...]=dv
    dk_ref[...]=(cdot(ds_s[...],qu_ref[...])*SCALE).astype(jnp.bfloat16)
    dr_ref[...]=(cdot(dw_s[...],qvr_s[...])*SCALE).astype(jnp.bfloat16)
    dval_ref[...]=cdot(p_ref[0],ga_ref[...]).astype(jnp.bfloat16)

def attn_bwd(p,ga,qu,qv,k,v,r):
    nh=qu.shape[1]//HEAD_DIM
    col=lambda n: pl.BlockSpec((n,HEAD_DIM),lambda h:(0,h))
    sd=lambda n,dt=jnp.bfloat16: jax.ShapeDtypeStruct((n,nh*HEAD_DIM),dt)
    return pl.pallas_call(attn_bwd_kernel, grid=(nh,),
        in_specs=[pl.BlockSpec((1,SEG,KTOT),lambda h:(h,0,0)),col(SEG),col(SEG),col(SEG),col(KTOT),col(KTOT),col(RELN)],
        out_specs=[col(SEG),col(1),col(1),col(KTOT),col(KTOT),col(RELN)],
        out_shape=[sd(SEG),sd(1,jnp.float32),sd(1,jnp.float32),sd(KTOT),sd(KTOT),sd(RELN)],
        scratch_shapes=[pltpu.VMEM((SEG,KTOT),jnp.bfloat16),pltpu.VMEM((SEG,RELN),jnp.bfloat16),pltpu.VMEM((SEG,HEAD_DIM),jnp.bfloat16)],
        compiler_params=pltpu.CompilerParams(vmem_limit_bytes=60<<20),
        cost_estimate=pl.CostEstimate(flops=12*nh*SEG*KTOT*HEAD_DIM,bytes_accessed=20<<20,transcendentals=0),
        name="attention_backward")(p,ga,qu,qv,k,v,r)


PATHS = {"A": ("x", "z", "y"), "B": ("y", "x", "z"), "C": ("z", "y", "x")}
SPOT = {"A": (0, 0, 0), "B": (0, 1, 1), "C": (0, 0, 2)}
STRIDE = {"y": 16, "z": 4, "x": 1}
ALL_AXES = ("dp", "blk")
BUFFER = 5648
ANY = pl.BlockSpec(memory_space=pl.ANY)
SMEM = pl.BlockSpec(memory_space=pltpu.SMEM)
VMEM = pl.BlockSpec(memory_space=pltpu.VMEM)
HBM = pl.BlockSpec(memory_space=pltpu.HBM)


def params(mib=40):
    return pltpu.CompilerParams(vmem_limit_bytes=mib << 20)


def shape_of(shape, dtype=jnp.float32):
    return jax.ShapeDtypeStruct(shape, dtype)


def swap(array):
    return lax.ppermute(array, "blk", [(0, 1), (1, 0)])


def step_pairs(chain, phase, delta):
    pairs = []
    for chip in range(64):
        for core in range(2):
            stride = STRIDE[PATHS[chain[core]][phase]]
            at = (chip // stride) % 4
            pairs.append((2 * chip + core, 2 * (chip + ((at + delta) % 4 - at) * stride) + core))
    return pairs


def send(array, chain, phase, delta):
    return lax.ppermute(array, ALL_AXES, step_pairs(chain, phase, delta))


def run_copies(copies):
    for copy in copies:
        copy.start()
    for copy in copies:
        copy.wait()


def spot_of(chain, core, phase, index):
    return (slice(None),) * SPOT[chain[core]][phase] + (index,)


def place_kernel(chain, phase, moves, deps, at_ref, own_ref, next_ref, across_ref, prev_ref, *rest):
    outs, sems = rest[deps:-1], rest[-1]
    pieces = (own_ref, next_ref, across_ref, prev_ref)
    lead = (slice(None),) * phase
    for core in range(2):
        @pl.when(at_ref[4] == core)
        def _():
            copies = []
            for k, piece in enumerate(pieces):
                where = spot_of(chain, core, phase, at_ref[k])
                for n, (start, size, out, head, to) in enumerate(moves):
                    source = piece.at[lead + (pl.ds(start, size),)]
                    target = outs[out].at[head + where]
                    if to is not None:
                        target = target.at[lead + (pl.ds(to, size),)]
                    copies.append(pltpu.make_async_copy(source, target, sems.at[k * len(moves) + n]))
            run_copies(copies)


def place(chain, phase, at, pieces, shapes, moves, deps=()):
    out = pl.pallas_call(
        functools.partial(place_kernel, chain, phase, moves, len(deps)),
        in_specs=[SMEM] + [ANY] * (4 + len(deps)),
        out_specs=[VMEM] * len(shapes),
        out_shape=[shape_of(shape, jnp.bfloat16) for shape in shapes],
        scratch_shapes=[pltpu.SemaphoreType.DMA((4 * len(moves),))],
        compiler_params=params(32),
        name="place_pieces",
    )(at, *pieces, *deps)
    return out if len(shapes) > 1 else out[0]


def grow(chain, phase, at, pieces):
    rows, lanes = pieces[0].shape[-2:]
    return place(chain, phase, at, pieces, [(4,) * (phase + 1) + (rows, lanes)], ((0, rows, 0, (), None),))


def send_pieces(chain, phase, at_ref, held, pieces, sems):
    for core in range(2):
        @pl.when(at_ref[4] == core)
        def _():
            copies = []
            for k, piece in enumerate(pieces):
                where = spot_of(chain, core, phase, at_ref[k])
                copies.append(pltpu.make_async_copy(held.at[where], piece, sems.at[k]))
            run_copies(copies)


def split_kernel(chain, phase, at_ref, own_in, one_in, two_in, three_in, own_ref, next_ref, across_ref, prev_ref, held, sems):
    held[...] = sum(ref[...].astype(jnp.float32) for ref in (own_in, one_in, two_in, three_in)).astype(jnp.bfloat16)
    send_pieces(chain, phase, at_ref, held, (own_ref, next_ref, across_ref, prev_ref), sems)


def add_split(chain, phase, at, parts):
    shape = parts[0].shape
    return pl.pallas_call(
        functools.partial(split_kernel, chain, phase),
        in_specs=[SMEM] + [VMEM] * 4,
        out_specs=[ANY] * 4,
        out_shape=[shape_of(shape[1:], jnp.bfloat16)] * 4,
        scratch_shapes=[pltpu.VMEM(shape, jnp.bfloat16), pltpu.SemaphoreType.DMA((4,))],
        compiler_params=params(32),
        name="add_pieces",
    )(at, *parts)


def finish_kernel(chain, at_ref, own_ref, next_ref, across_ref, prev_ref, *rest):
    outs, proj_ref, extra_ref, held, sems = rest[:4], rest[4], rest[5], rest[6], rest[7]
    for core in range(2):
        @pl.when(at_ref[4] == core)
        def _():
            copies = []
            for k, piece in enumerate((own_ref, next_ref, across_ref, prev_ref)):
                where = spot_of(chain, core, 2, at_ref[k])
                copies.append(pltpu.make_async_copy(piece, held.at[where], sems.at[k]))
            run_copies(copies)
    extra_ref[...] = held[0, 0, 0, 80:, :].astype(jnp.float32)
    for chip in range(64):
        y, z, x = chip // 16, (chip // 4) % 4, chip % 4
        for h in range(2):
            block = held[y, z, x, 32 * h : 32 * h + 32, :].astype(jnp.float32)
            outs[y][pl.ds(32 * (chip % 16), 32), pl.ds(512 * h, 512)] = block
            block = held[y, z, x, 64 + 8 * h : 72 + 8 * h, :].astype(jnp.float32)
            proj_ref[pl.ds(8 * chip, 8), pl.ds(512 * h, 512)] = block


def finish(chain, at, pieces):
    return pl.pallas_call(
        functools.partial(finish_kernel, chain),
        in_specs=[SMEM] + [ANY] * 4,
        out_specs=[VMEM] * 6,
        out_shape=[shape_of((512, D))] * 5 + [shape_of((8, 512))],
        scratch_shapes=[pltpu.VMEM((4, 4, 4, 88, 512), jnp.bfloat16), pltpu.SemaphoreType.DMA((4,))],
        compiler_params=params(60),
        name="finish_gradients",
    )(at, *pieces)


def three_ways(chain, phase, chunk):
    prev, nxt, across = send(chunk, chain, phase, 1), send(chunk, chain, phase, -1), send(chunk, chain, phase, 2)
    return chunk, nxt, across, prev


MATS = (4, 4, 4, 4, 16, 512)


def gather_steps(chain, chunk, spots, deps):
    chunk = grow(chain, 0, spots[0], three_ways(chain, 0, chunk))
    pieces = three_ways(chain, 1, chunk)
    near = place(chain, 1, spots[1], pieces, [(4, 4, 72, 512)], ((0, 64, 0, (), 0), (128, 8, 0, (), 64)))
    each = tuple((16 * m, 16, 0, (m,), None) for m in range(4))
    mats, vecs = place(
        chain, 2, spots[2], three_ways(chain, 2, near), [MATS, (4, 4, 4, 8, 512)], each + ((64, 8, 1, (), None),), deps
    )
    far = place(chain, 1, spots[1], pieces, [(4, 4, 64, 512)], ((64, 64, 0, (), None),), (mats,))
    panels = place(chain, 2, spots[2], three_ways(chain, 2, far), [MATS], each)
    return mats.reshape(4, D, 512), vecs, panels.reshape(4, D, 512)


def scatter_steps(chain, pieces, spots):
    for phase in (2, 1, 0):
        own, nxt, across, prev = pieces
        parts = (own, send(nxt, chain, phase, 1), send(prev, chain, phase, -1), send(across, chain, phase, 2))
        if phase:
            pieces = add_split(chain, phase - 1, spots[phase - 1], parts)
    return sum(part.astype(jnp.float32) for part in parts)


def regather_steps(chain, chunk, spots):
    for phase in range(2):
        chunk = grow(chain, phase, spots[phase], three_ways(chain, phase, chunk))
    return finish(chain, spots[2], three_ways(chain, 2, chunk))


PACKED = ((8, D),) * 4 + ((8, FF), (8, D), (24, D), (32, D)) + ((1, 8),) * 4 + ((1, 32), (1, 8), (1, 8))


def pack_kernel(at_ref, *refs):
    f32, bf16 = jnp.float32, jnp.bfloat16
    count = len(PACKED)
    sources, (blocks_ref, keep_ref, give_ref), held, sems = refs[:count], refs[count : count + 3], refs[count + 3 : -1], refs[-1]
    run_copies([pltpu.make_async_copy(source, place, sems.at[k]) for k, (source, place) in enumerate(zip(sources, held))])
    wq, wk, wv, wr, win, wp, wc, wo, ga, ub, vb, gf, bi, bo, bc = held
    first = at_ref[0] == 0
    where = at_ref[1]

    def spread(ref, size, width):
        row = lax.broadcasted_iota(jnp.int32, (size, width), 0)
        lane = lax.broadcasted_iota(jnp.int32, (size, width), 1)
        hot = (lane == size * where + row).astype(f32).astype(bf16)
        return ndot(ref[...], hot)

    for n, ref in enumerate((wq, wk, wv, wr)):
        left, right = ref[:, :512].astype(f32), ref[:, 512:].astype(f32)
        keep_ref[8 * n : 8 * n + 8, :] = jnp.where(first, left, right).astype(bf16)
        give_ref[8 * n : 8 * n + 8, :] = jnp.where(first, right, left).astype(bf16)
    for n in range(4):
        left, right = (win[:, 2048 * h + 512 * n : 2048 * h + 512 * n + 512].astype(f32) for h in range(2))
        keep_ref[32 + 8 * n : 40 + 8 * n, :] = jnp.where(first, left, right).astype(bf16)
        give_ref[32 + 8 * n : 40 + 8 * n, :] = jnp.where(first, right, left).astype(bf16)
    rows = []
    for ref in (ga, ub, vb, gf):
        wide = spread(ref, 8, D)
        rows += [wide[:, :512], wide[:, 512:]]
    vectors = jnp.concatenate(rows, axis=0).astype(bf16)
    keep_ref[64:72, :] = vectors
    give_ref[64:72, :] = vectors
    blocks_ref[0] = wp[...]
    for q in range(3):
        blocks_ref[1 + q] = wc[8 * q : 8 * q + 8, :]
    for q in range(4):
        blocks_ref[4 + q] = wo[8 * q : 8 * q + 8, :]
    wide = spread(bi, 32, 4 * D)
    rows = [wide[:, D * c : D * c + D] for c in range(4)] + [spread(bo, 8, D), spread(bc, 8, D), jnp.zeros((2, D), f32)]
    blocks_ref[8] = jnp.concatenate(rows, axis=0).astype(bf16)


def pack(at, *arrays):
    return pl.pallas_call(
        pack_kernel,
        in_specs=[SMEM] + [HBM] * len(arrays),
        out_specs=[VMEM] * 3,
        out_shape=[shape_of((9, 8, D), jnp.bfloat16)] + [shape_of((72, 512), jnp.bfloat16)] * 2,
        scratch_shapes=[pltpu.VMEM(shape, jnp.bfloat16) for shape in PACKED] + [pltpu.SemaphoreType.DMA((len(PACKED),))],
        compiler_params=params(60),
        name="pack_weights",
    )(at, *arrays)


def start_kernel(taps_ref, grad_ref, out_ref, stage, sem):
    stage[...] = cdot(taps_ref[...], grad_ref[...]).astype(jnp.bfloat16)
    run_copies([pltpu.make_async_copy(stage, out_ref.at[pl.ds(4096, 1536)], sem)])


def start_buffer(taps, grads):
    return pl.pallas_call(
        start_kernel,
        in_specs=[VMEM, VMEM],
        out_specs=HBM,
        out_shape=shape_of((BUFFER, D), jnp.bfloat16),
        scratch_shapes=[pltpu.VMEM((1536, D), jnp.bfloat16), pltpu.SemaphoreType.DMA],
        compiler_params=params(60),
        name="compression_gradient",
    )(taps, grads)


def normalize(rows):
    centred = rows - jnp.mean(rows, axis=1, keepdims=True)
    inverse = lax.rsqrt(jnp.mean(centred * centred, axis=1, keepdims=True) + EPSILON)
    return centred * inverse, inverse


def mix_kernel(core_ref, att_ref, got_ref, proj_ref, seg_ref, gain_ref, hidden_ref, act_ref):
    core = core_ref[0]
    mine = proj_ref[0, pl.ds(pl.multiple_of(512 * core, 512), 512), :]
    other = proj_ref[0, pl.ds(pl.multiple_of(512 - 512 * core, 512), 512), :]
    hidden = seg_ref[...].astype(jnp.float32) + ndot(att_ref[...], mine) + ndot(got_ref[...], other)
    hidden_ref[...] = hidden
    act_ref[...] = (normalize(hidden)[0] * gain_ref[...]).astype(jnp.bfloat16)


def mix(core, att, got, large, seg, gain):
    whole = lambda *shape: pl.BlockSpec(shape, lambda i: (0,) * len(shape))
    return pl.pallas_call(
        mix_kernel,
        grid=(1,),
        in_specs=[SMEM, whole(512, 512), whole(512, 512), whole(1, D, D), whole(512, D), whole(1, D)],
        out_specs=[whole(512, D), whole(512, D)],
        out_shape=[shape_of((512, D)), shape_of((512, D), jnp.bfloat16)],
        compiler_params=params(60),
        name="hidden_rows",
    )(core, att, got, large, seg, gain)


def middle_kernel(core_ref, back_ref, got_ref, hidden_ref, gain_ref, gr_ref, proj_ref, hid_ref, branch_ref, att_ref, sum_ref):
    del core_ref
    back = back_ref[...] + got_ref[...]
    normed, inverse = normalize(hidden_ref[...])
    sum_ref[...] = jnp.sum(back * normed, axis=0, keepdims=True)
    scaled = back * gain_ref[...]
    along = jnp.mean(scaled * normed, axis=1, keepdims=True)
    grad = gr_ref[...].astype(jnp.float32) + inverse * (
        scaled - jnp.mean(scaled, axis=1, keepdims=True) - normed * along
    )
    hid_ref[...] = grad
    branch = grad.astype(jnp.bfloat16)
    branch_ref[...] = branch
    att_ref[...] = tdot(branch, proj_ref[0]).astype(jnp.bfloat16)


def middle(core, back, got, hidden, gain, grad_res, large):
    whole = lambda *shape: pl.BlockSpec(shape, lambda i, c: (0,) * len(shape))
    return pl.pallas_call(
        middle_kernel,
        grid_spec=pltpu.PrefetchScalarGridSpec(
            num_scalar_prefetch=1,
            grid=(1,),
            in_specs=[
                whole(512, D), whole(512, D), whole(512, D), whole(1, D), whole(512, D),
                pl.BlockSpec((1, 512, D), lambda i, c: (0, c[0], 0)),
            ],
            out_specs=[whole(512, D), whole(512, D), whole(512, 512), whole(1, D)],
        ),
        out_shape=[
            shape_of((512, D)), shape_of((512, D), jnp.bfloat16), shape_of((512, 512), jnp.bfloat16), shape_of((1, D)),
        ],
        compiler_params=params(60),
        name="hidden_gradient",
    )(core, back, got, hidden, gain, grad_res, large)


LATE = ((512, 512), (512, D), (KTOT, D), (512, 512), (3, D, 512), (KTOT, 512), (KTOT, 512), (RELN, D), (RELN, 512))


def late_kernel(at_ref, *refs):
    f32, bf16 = jnp.float32, jnp.bfloat16
    count = len(LATE)
    sources, (gain_ref, small_ref), pieces = refs[:count], refs[count : count + 2], refs[count + 2 : count + 6]
    places, held, sems = refs[count + 6 : -2], refs[-2], refs[-1]
    loads = []
    for k, (source, to) in enumerate(zip(sources, places)):
        source = source.at[pl.ds(0, 3)] if k == 4 else source
        loads.append(pltpu.make_async_copy(source, to, sems.at[4 + k]))
        loads[-1].start()
    att_ref, branch_ref, joined_ref, gq_ref, mats_ref, gk_ref, gv_ref, table_ref, gr_ref = places
    loads[0].wait()
    loads[1].wait()
    proj = cdot(att_ref[...], branch_ref[...]).astype(bf16).reshape(4, 4, 4, 8, D)
    for h in range(2):
        held[:, :, :, 64 + 8 * h : 72 + 8 * h, :] = proj[..., 512 * h : 512 * h + 512]
    ones = jnp.ones((8, 512), bf16)
    total = jnp.zeros((8, D), f32)
    sides = (
        (lambda: joined_ref[pl.ds(COMP + MEM, SEG), :], gq_ref, (2, 3, 4)),
        (lambda: joined_ref[...], gk_ref, (5,)),
        (lambda: joined_ref[...], gv_ref, (6,)),
        (lambda: table_ref[...], gr_ref, (7, 8)),
    )
    for m, (left, right, needs) in enumerate(sides):
        for k in needs:
            loads[k].wait()
        grad = cdot(left(), right[...])
        low = grad.astype(bf16)
        for h in range(2):
            held[m, :, :, 32 * h : 32 * h + 32, :] = low[512 * h : 512 * h + 512].reshape(4, 4, 32, 512)
        if m < 3:
            product = grad * mats_ref[m].astype(f32)
            high = product.astype(bf16)
            total += tdot(ones, high) + tdot(ones, (product - high.astype(f32)).astype(bf16))
    total = total[:1] / gain_ref[...]
    extra = jnp.concatenate([total[:, :512], total[:, 512:], small_ref[2:, :]], axis=0)
    held[:, :, :, 80:, :] = jnp.zeros((4, 4, 4, 8, 512), bf16)
    held[0, 0, 0, 80:, :] = extra.astype(bf16)
    send_pieces("AB", 2, at_ref, held, pieces, sems)


def late_gradients(*arrays):
    bf16 = jnp.bfloat16
    return pl.pallas_call(
        late_kernel,
        in_specs=[SMEM] + [HBM] * len(LATE) + [VMEM] * 2,
        out_specs=[ANY] * 4,
        out_shape=[shape_of((4, 4, 88, 512), bf16)] * 4,
        scratch_shapes=[pltpu.VMEM(shape, bf16) for shape in LATE]
        + [pltpu.VMEM((4, 4, 4, 88, 512), bf16), pltpu.SemaphoreType.DMA((4 + len(LATE),))],
        compiler_params=params(60),
        cost_estimate=pl.CostEstimate(flops=2 * 5400 * 512 * 1024, bytes_accessed=24 << 20, transcendentals=0),
        name="late_gradients",
    )(*arrays)


def ffn_kernel(core_ref, act_ref, gr_ref, win_ref, *rest):
    del core_ref
    quarters, bias_ref, out_ref, back_ref, part_ref = rest[:4], rest[4], rest[6], rest[7], rest[8]
    natural, stage_in, stage_out, sums, sems = rest[9:]
    p = pl.program_id(0)
    slot = lax.rem(p, 2)

    def sending(step, buffer):
        rows = pl.ds(pl.multiple_of(1024 * (step // 2), 1024), 1024)
        lanes = pl.ds(pl.multiple_of(512 * lax.rem(step, 2), 512), 512)
        below = pl.ds(pl.multiple_of(2048 + 512 * step, 512), 512)
        return [
            pltpu.make_async_copy(stage_in.at[buffer], out_ref.at[rows, lanes], sems.at[buffer]),
            pltpu.make_async_copy(stage_out.at[buffer], out_ref.at[below], sems.at[2 + buffer]),
        ]

    @pl.when(p >= 2)
    def _():
        for copy in sending(p - 2, slot):
            copy.wait()

    act, grad, w_one = act_ref[...], gr_ref[...], win_ref[0]
    for q in range(4):
        for shard in range(16):
            natural[32 * shard + 8 * q : 32 * shard + 8 * q + 8, :] = quarters[q][0, 8 * shard : 8 * shard + 8, :]
    w_two = natural[...]
    pre = ndot(act, w_one) + bias_ref[0]
    inner = math.sqrt(2.0 / math.pi)
    square = pre * pre
    tanh = jnp.tanh(inner * pre * (1.0 + 0.044715 * square))
    act_low = (0.5 * pre * (1.0 + tanh)).astype(jnp.bfloat16)
    slope = 0.5 * (1.0 + tanh) + (0.5 * inner) * pre * (1.0 - tanh * tanh) * (1.0 + (3.0 * 0.044715) * square)
    grad_act = tdot(grad, w_two)
    grad_pre = (grad_act * slope).astype(jnp.bfloat16)
    stage_in[slot] = cdot(act, grad_pre).astype(jnp.bfloat16)
    stage_out[slot] = cdot(act_low, grad).astype(jnp.bfloat16)
    for copy in sending(p, slot):
        copy.start()
    total = jnp.sum(grad_pre.astype(jnp.float32), axis=0, keepdims=True)
    total = jnp.concatenate([total, total], axis=1)
    row = lax.broadcasted_iota(jnp.int32, (16, D), 0)
    lane = lax.broadcasted_iota(jnp.int32, (16, D), 1)
    mine = (row == p // 2) & (lane // 512 == lax.rem(p, 2))

    @pl.when(p == 0)
    def _():
        sums[...] = jnp.zeros_like(sums)
        back_ref[...] = tdot(grad_pre, w_one)
        part_ref[...] = ndot(act_low, w_two)

    @pl.when(p > 0)
    def _():
        back_ref[...] += tdot(grad_pre, w_one)
        part_ref[...] += ndot(act_low, w_two)

    sums[...] = jnp.where(mine, total, sums[...].astype(jnp.float32)).astype(jnp.bfloat16)

    @pl.when(p == 3)
    def _():
        last = pltpu.make_async_copy(sums, out_ref.at[pl.ds(5632, 16)], sems.at[4])
        last.start()
        for copy in sending(p - 1, 1 - slot) + sending(p, slot):
            copy.wait()
        last.wait()


def ffn(core, act, grad, w_one, large, bias, buffer):
    f32, bf16 = jnp.float32, jnp.bfloat16
    whole = pl.BlockSpec((512, D), lambda p, c: (0, 0))
    quarter = lambda q: pl.BlockSpec((1, 128, D), lambda p, c: (4 + q, 4 * c[0] + p, 0))
    return pl.pallas_call(
        ffn_kernel,
        grid_spec=pltpu.PrefetchScalarGridSpec(
            num_scalar_prefetch=1,
            grid=(4,),
            in_specs=[
                whole,
                whole,
                pl.BlockSpec((1, D, 512), lambda p, c: (p, 0, 0)),
                *(quarter(q) for q in range(4)),
                pl.BlockSpec((1, 1, 512), lambda p, c: (p, 0, 0)),
                HBM,
            ],
            out_specs=[HBM, whole, whole],
            scratch_shapes=[
                pltpu.VMEM((512, D), bf16),
                pltpu.VMEM((2, D, 512), bf16),
                pltpu.VMEM((2, 512, D), bf16),
                pltpu.VMEM((16, D), bf16),
                pltpu.SemaphoreType.DMA((5,)),
            ],
        ),
        out_shape=[shape_of((BUFFER, D), bf16), shape_of((512, D)), shape_of((512, D))],
        input_output_aliases={9: 0},
        compiler_params=params(60),
        cost_estimate=pl.CostEstimate(flops=12 * 512 * 1024 * 2048, bytes_accessed=24 << 20, transcendentals=512 * 2048),
        name="feed_forward",
    )(core, act, grad, w_one, large, large, large, large, bias, buffer)


def hold_kernel(*refs):
    del refs


def hold(array, deps):
    return pl.pallas_call(
        hold_kernel,
        in_specs=[HBM] + [ANY] * len(deps),
        out_specs=HBM,
        out_shape=shape_of(array.shape, array.dtype),
        input_output_aliases={0: 0},
        compiler_params=params(60),
        name="after_others",
    )(array, *deps)


def pick_kernel(core_ref, source_ref, out_ref):
    del core_ref
    out_ref[...] = source_ref[...]


def pick_halves(core, buffer):
    return pl.pallas_call(
        pick_kernel,
        grid_spec=pltpu.PrefetchScalarGridSpec(
            num_scalar_prefetch=1,
            grid=(2,),
            in_specs=[pl.BlockSpec((512, D), lambda q, c: (2 * q + 1 - c[0], 0))],
            out_specs=pl.BlockSpec((512, D), lambda q, c: (q, 0)),
        ),
        out_shape=shape_of((D, D), jnp.bfloat16),
        compiler_params=params(60),
        name="other_half",
    )(core, buffer)


def on_device(
    segment, memory, compressed, mem_count, comp_count, attn_gain, w_query, w_key, w_value, u_bias, v_bias,
    w_rel, w_proj, ffn_gain, w_in, b_in, w_out, b_out, w_comp, b_comp, out_grad, comp_grad,
):
    f32, bf16 = jnp.float32, jnp.bfloat16
    core, chip = lax.axis_index("blk"), lax.axis_index("dp")
    first = core == 0
    core_at = core.reshape(1).astype(jnp.int32)
    coords = {"y": chip // 16, "z": (chip // 4) % 4, "x": chip % 4}
    spots = {}
    for chain in ("AB",):
        spots[chain] = []
        for phase in range(3):
            at = jnp.where(first, coords[PATHS[chain[0]][phase]], coords[PATHS[chain[1]][phase]])
            spots[chain].append(jnp.stack([(at + k) % 4 for k in range(4)] + [core]).astype(jnp.int32))

    def both(own, other, axis=0):
        return jnp.where(first, jnp.concatenate([own, other], axis), jnp.concatenate([other, own], axis))

    def half(array, which, axis):
        size = array.shape[axis] // 2
        return lax.dynamic_slice_in_dim(array, which * size, size, axis)

    where_at = jnp.stack([core, 2 * chip + core]).astype(jnp.int32)
    row = lambda vector: vector.reshape(1, -1)
    blocks, keep, give = pack(
        where_at, w_query, w_key, w_value, w_rel, w_in, w_proj, w_comp, w_out,
        row(attn_gain), row(u_bias), row(v_bias), row(ffn_gain), row(b_in), row(b_out), row(b_comp),
    )
    large = lax.all_gather(blocks, ALL_AXES, axis=1, tiled=True)
    got = swap(give)
    chunk = jnp.concatenate(
        [both(keep[8 * n : 8 * n + 8], got[8 * n : 8 * n + 8]) for n in range(8)] + [keep[64:] + got[64:]]
    )

    pieces = [both(array[0], swap(array[0])) for array in (compressed, memory, segment, out_grad, comp_grad)]
    seg_at = COMP + MEM
    grad_res, comp_flat = pieces[3], pieces[4]
    all_rows = jnp.concatenate(pieces[:3])

    def centre(rows):
        mean = jnp.mean(rows, axis=-1, keepdims=True)
        centred = rows - mean
        return mean, lax.rsqrt(jnp.mean(centred * centred, axis=-1, keepdims=True) + EPSILON)

    mean_one, inverse_one = centre(all_rows.astype(f32))

    distance = (KTOT - 1) - jnp.arange(RELN, dtype=f32)
    frequency = jnp.exp(jnp.arange(D // 2, dtype=f32) * (-2.0 * math.log(10000.0) / D))
    coarse = distance[::32, None] * frequency[None, :]
    fine = jnp.arange(32, dtype=f32)[:, None] * frequency[None, :]
    sin_a, cos_a = (trig(coarse)[:, None, :] for trig in (jnp.sin, jnp.cos))
    sin_b, cos_b = (trig(fine)[None, :, :] for trig in (jnp.sin, jnp.cos))
    sines, cosines = sin_a * cos_b - cos_a * sin_b, cos_a * cos_b + sin_a * sin_b
    table = jnp.concatenate([sines.reshape(RELN, 512), cosines.reshape(RELN, 512)], axis=1)
    table = jnp.where(distance[:, None] >= 0.0, table, 0.0).astype(bf16)

    slot = jnp.arange(MEM, dtype=jnp.int32)
    masked = jnp.where((slot >= MEM - mem_count[0])[:, None], pieces[1], jnp.zeros_like(pieces[1]))
    windows = masked.reshape(MEM // RATE, RATE * D)
    buffer = start_buffer(half(windows, core, 1), comp_flat)

    mats, vecs, w_one = gather_steps("AB", chunk, spots["AB"], (mean_one, inverse_one, all_rows, table, buffer))
    vecs = jnp.sum(vecs.astype(f32), axis=(0, 1, 2))
    gain_one, gain_two = vecs[:2].reshape(1, D), vecs[6:8].reshape(1, D)
    bias_u = jnp.where(first, vecs[2], vecs[3])
    bias_v = jnp.where(first, vecs[4], vecs[5])
    joined = ((all_rows.astype(f32) - mean_one) * inverse_one * gain_one).astype(bf16)
    query_rows = ndot(joined[seg_at:], mats[0])
    key_rows = ndot(joined, mats[1]).astype(bf16)
    value_rows = ndot(joined, mats[2]).astype(bf16)
    rel_rows = ndot(table, mats[3]).astype(bf16)
    query_u = (query_rows + bias_u).astype(bf16)
    query_v = (query_rows + bias_v).astype(bf16)
    counts = jnp.concatenate([mem_count, comp_count])
    attended, probs = attn_fwd(counts, query_u, query_v, key_rows, value_rows, rel_rows)

    others = jnp.sum(large[8].reshape(128, 8, D).astype(f32), axis=0)
    ffn_bias = half(others[:4], core, 0).reshape(4, 1, 512)
    out_bias, comp_bias = others[4], others[5]
    hidden, act_two = mix(core_at, attended, swap(attended), large, pieces[2], gain_two)
    buffer, back, partial = ffn(core_at, act_two, grad_res, w_one, large, ffn_bias, buffer)
    buffer = lax.psum(buffer, "dp")
    grad_hidden, grad_branch, grad_att, d_gain_two = middle(
        core_at, back, swap(back), hidden, gain_two, grad_res, large
    )

    grad_query, d_u, d_v, grad_keys, grad_values, grad_rel = attn_bwd(
        probs, grad_att, query_u, query_v, key_rows, value_rows, rel_rows
    )
    d_b_out = jnp.sum(half(grad_res, core, 1).astype(f32), axis=0, keepdims=True)
    d_b_comp = jnp.sum(half(comp_flat, core, 1).astype(f32), axis=0, keepdims=True)
    small = jnp.concatenate(
        [jnp.zeros((2, 512), f32), d_u, d_v, half(d_gain_two, core, 1), d_b_out, d_b_comp, jnp.zeros((1, 512), f32)]
    )
    pieces_late = late_gradients(
        spots["AB"][2], attended, grad_branch, joined, grad_query, mats, grad_keys, grad_values, table, grad_rel, gain_one, small
    )
    share = scatter_steps("AB", pieces_late, spots["AB"])
    keep = half(share[:64], core, 0).astype(bf16)
    mail = swap(jnp.concatenate([half(share[:64], 1 - core, 0), share[80:]]).astype(bf16))
    gains = jnp.where(jnp.arange(8)[:, None] < 2, share[80:] + mail[32:].astype(f32), share[80:])
    late = jnp.concatenate([both(keep, mail[:32]), share[64:80].astype(bf16), gains.astype(bf16)])
    *late, d_proj, extra = regather_steps("AB", late, spots["AB"])

    result = half(hidden, core, 0) + half(partial, core, 0) + swap(half(partial, 1 - core, 0)) + out_bias
    output = result.astype(bf16)

    comp_proj = large[1:4].reshape(3, 128, 8, D).transpose(1, 0, 2, 3).reshape(RATE * D, D)
    new_compressed = (ndot(half(windows, core, 0), comp_proj) + comp_bias).astype(bf16)

    grad_seg = (
        tdot(grad_query, mats[0]) + tdot(grad_keys[seg_at:], mats[1]) + tdot(grad_values[seg_at:], mats[2])
    )
    grad_seg = half(grad_seg, core, 0) + swap(half(grad_seg, 1 - core, 0))
    scaled_one = grad_seg * gain_one
    own_segment = segment[0].astype(f32)
    mean_seg, inverse_seg = centre(own_segment)
    normed_seg = (own_segment - mean_seg) * inverse_seg
    d_segment = half(grad_hidden, core, 0) + inverse_seg * (
        scaled_one
        - jnp.mean(scaled_one, axis=-1, keepdims=True)
        - normed_seg * jnp.mean(scaled_one * normed_seg, axis=-1, keepdims=True)
    )

    buffer = hold(buffer, (late[0], output, new_compressed, d_segment))
    others = swap(pick_halves(core_at, buffer))
    d_out = buffer[2048:4096].astype(f32)
    d_comp = buffer[4096:5632].astype(f32)
    mine = [lax.dynamic_slice_in_dim(buffer, D * q + 512 * core, 512, 0) for q in range(2)]
    d_in = both(jnp.concatenate(mine, axis=1), jnp.concatenate([others[:512], others[512:]], axis=1), 1).astype(f32)
    d_b_in = buffer[5632:5634].astype(f32).reshape(2048)
    return (
        output[None],
        new_compressed[None],
        d_segment[None],
        jnp.where(first, extra[0], extra[1]),
        late[0],
        late[1],
        late[2],
        extra[2],
        extra[3],
        late[3],
        d_proj,
        extra[4],
        d_in,
        d_b_in,
        d_out,
        extra[5],
        d_comp,
        extra[6],
    )


def solution(mesh):
    rows, weight, vector = P("dp", "blk", None), P(("dp", "blk"), None), P(("dp", "blk"))
    placed = (
        rows, rows, rows, P("dp"), P("dp"), vector, weight, weight, weight, vector, vector,
        weight, weight, vector, weight, vector, weight, vector, weight, vector, rows, rows,
    )
    half_one, half_two = P("blk"), P("blk", None)
    return jax.shard_map(
        on_device,
        mesh=mesh,
        in_specs=placed,
        out_specs=(
            rows, rows, rows, half_one, half_two, half_two, half_two, half_one, half_one,
            half_two, half_two, half_one, half_two, half_one, half_two, half_one, half_two, half_one,
        ),
        check_vma=False,
    )
```

```python
import math, functools
import jax, jax.numpy as jnp
from jax import lax
from jax.sharding import PartitionSpec as P
from jax.experimental import pallas as pl
from jax.experimental.pallas import tpu as pltpu
D=1024
FF=4096
HEAD_DIM=128
SEG=512
MEM=384
COMP=512
RATE=3
KTOT=1408
RELN=1536
QB=128
EPSILON=1e-05
SCALE=1.0/math.sqrt(HEAD_DIM); NEG=-1e30
def tdot(a,b):
    return lax.dot_general(a,b,(((1,),(1,)),((),())),preferred_element_type=jnp.float32)
def ndot(a,b):
    return lax.dot_general(a,b,(((1,),(0,)),((),())),preferred_element_type=jnp.float32)
def cdot(a,b):
    return lax.dot_general(a,b,(((0,),(0,)),((),())),preferred_element_type=jnp.float32)

def attn_fwd_kernel(cnt_ref, qu_ref, qv_ref, k_ref, v_ref, r_ref, att_ref, p_ref):
    mc = cnt_ref[0]; cc = cnt_ref[1]
    kp = lax.broadcasted_iota(jnp.int32,(1,COMP+MEM),1)
    ok = ((kp < COMP) & (kp >= COMP-cc)) | ((kp>=COMP)&(kp>=COMP+MEM-mc))
    old_bias = jnp.where(ok, 0.0, NEG)
    tri = jnp.where(lax.broadcasted_iota(jnp.int32,(QB,QB),1) <= lax.broadcasted_iota(jnp.int32,(QB,QB),0), 0.0, NEG)
    for b in range(SEG//QB):
        i0=QB*b; nk=COMP+MEM+QB*(b+1); c0=SEG-QB-QB*b; wl=nk+QB
        s = tdot(qu_ref[pl.ds(i0,QB),:], k_ref[pl.ds(0,nk),:])
        w = tdot(qv_ref[pl.ds(i0,QB),:], r_ref[pl.ds(c0,wl),:])
        w = pltpu.roll(w, wl-(QB-1), 1, stride=1, stride_axis=0)[:,:nk]
        s = (s+w)*SCALE
        parts=[s[:,:COMP+MEM]+old_bias]
        if b: parts.append(s[:,COMP+MEM:nk-QB])
        parts.append(s[:,nk-QB:]+tri)
        s=jnp.concatenate(parts,axis=1)
        m=jnp.max(s,axis=1,keepdims=True)
        e=jnp.exp(s-m)
        l=jnp.sum(e,axis=1,keepdims=True)
        p=(e*(1.0/l)).astype(jnp.bfloat16)
        p_ref[0,pl.ds(i0,QB),pl.ds(0,nk)]=p
        if nk<KTOT: p_ref[0,pl.ds(i0,QB),pl.ds(nk,KTOT-nk)]=jnp.zeros((QB,KTOT-nk),jnp.bfloat16)
        att_ref[pl.ds(i0,QB),:]=ndot(p,v_ref[pl.ds(0,nk),:]).astype(jnp.bfloat16)

def attn_fwd(cnt,qu,qv,k,v,r):
    nh=qu.shape[1]//HEAD_DIM
    col=lambda n: pl.BlockSpec((n,HEAD_DIM),lambda h:(0,h))
    return pl.pallas_call(attn_fwd_kernel, grid=(nh,),
        in_specs=[pl.BlockSpec(memory_space=pltpu.SMEM),col(SEG),col(SEG),col(KTOT),col(KTOT),col(RELN)],
        out_specs=[col(SEG),pl.BlockSpec((1,SEG,KTOT),lambda h:(h,0,0))],
        out_shape=[jax.ShapeDtypeStruct((SEG,nh*HEAD_DIM),jnp.bfloat16),jax.ShapeDtypeStruct((nh,SEG,KTOT),jnp.bfloat16)],
        compiler_params=pltpu.CompilerParams(vmem_limit_bytes=40<<20),
        cost_estimate=pl.CostEstimate(flops=6*nh*SEG*KTOT*HEAD_DIM,bytes_accessed=12<<20,transcendentals=nh*SEG*KTOT),
        name="attention_forward")(cnt,qu,qv,k,v,r)


PATHS = {"A": ("x", "z", "y"), "B": ("y", "x", "z"), "C": ("z", "y", "x")}
SPOT = {
    name: tuple(sorted(path[: phase + 1], key="yzx".index).index(path[phase]) for phase in range(3))
    for name, path in PATHS.items()
}
STRIDE = {"y": 16, "z": 4, "x": 1}
ALL_AXES = ("dp", "blk")
BUFFER = 5648
ANY = pl.BlockSpec(memory_space=pl.ANY)
SMEM = pl.BlockSpec(memory_space=pltpu.SMEM)
VMEM = pl.BlockSpec(memory_space=pltpu.VMEM)
HBM = pl.BlockSpec(memory_space=pltpu.HBM)


def params(mib=40):
    return pltpu.CompilerParams(vmem_limit_bytes=mib << 20)


def shape_of(shape, dtype=jnp.float32):
    return jax.ShapeDtypeStruct(shape, dtype)


def swap(array):
    return lax.ppermute(array, "blk", [(0, 1), (1, 0)])


def step_pairs(chain, phase, delta):
    pairs = []
    for chip in range(64):
        for core in range(2):
            stride = STRIDE[PATHS[chain[core]][phase]]
            at = (chip // stride) % 4
            pairs.append((2 * chip + core, 2 * (chip + ((at + delta) % 4 - at) * stride) + core))
    return pairs


def send(array, chain, phase, delta):
    return lax.ppermute(array, ALL_AXES, step_pairs(chain, phase, delta))


def run_copies(copies):
    for copy in copies:
        copy.start()
    for copy in copies:
        copy.wait()


def spot_of(chain, core, phase, index):
    return (slice(None),) * SPOT[chain[core]][phase] + (index,)


def place_kernel(chain, phase, moves, deps, at_ref, own_ref, next_ref, across_ref, prev_ref, *rest):
    outs, sems = rest[deps:-1], rest[-1]
    pieces = (own_ref, next_ref, across_ref, prev_ref)
    lead = (slice(None),) * phase
    for core in range(2):
        @pl.when(at_ref[4] == core)
        def _():
            copies = []
            for k, piece in enumerate(pieces):
                where = spot_of(chain, core, phase, at_ref[k])
                for n, (start, size, out, head, to) in enumerate(moves):
                    source = piece.at[lead + (pl.ds(start, size),)]
                    target = outs[out].at[head + where]
                    if to is not None:
                        target = target.at[lead + (pl.ds(to, size),)]
                    copies.append(pltpu.make_async_copy(source, target, sems.at[k * len(moves) + n]))
            run_copies(copies)


def place(chain, phase, at, pieces, shapes, moves, deps=(), mib=32):
    out = pl.pallas_call(
        functools.partial(place_kernel, chain, phase, moves, len(deps)),
        in_specs=[SMEM] + [ANY] * (4 + len(deps)),
        out_specs=[VMEM] * len(shapes),
        out_shape=[shape_of(shape, jnp.bfloat16) for shape in shapes],
        scratch_shapes=[pltpu.SemaphoreType.DMA((4 * len(moves),))],
        compiler_params=params(mib),
        name="place_pieces",
    )(at, *pieces, *deps)
    return out if len(shapes) > 1 else out[0]


def grow(chain, phase, at, pieces):
    rows, lanes = pieces[0].shape[-2:]
    return place(chain, phase, at, pieces, [(4,) * (phase + 1) + (rows, lanes)], ((0, rows, 0, (), None),))


def send_pieces(chain, phase, at_ref, held, pieces, sems):
    for core in range(2):
        @pl.when(at_ref[4] == core)
        def _():
            copies = []
            for k, piece in enumerate(pieces):
                where = spot_of(chain, core, phase, at_ref[k])
                copies.append(pltpu.make_async_copy(held.at[where], piece, sems.at[k]))
            run_copies(copies)


def split_kernel(chain, phase, at_ref, own_in, one_in, two_in, three_in, own_ref, next_ref, across_ref, prev_ref, held, sems):
    held[...] = sum(ref[...].astype(jnp.float32) for ref in (own_in, one_in, two_in, three_in)).astype(jnp.bfloat16)
    send_pieces(chain, phase, at_ref, held, (own_ref, next_ref, across_ref, prev_ref), sems)


def add_split(chain, phase, at, parts):
    shape = parts[0].shape
    return pl.pallas_call(
        functools.partial(split_kernel, chain, phase),
        in_specs=[SMEM] + [VMEM] * 4,
        out_specs=[ANY] * 4,
        out_shape=[shape_of(shape[1:], jnp.bfloat16)] * 4,
        scratch_shapes=[pltpu.VMEM(shape, jnp.bfloat16), pltpu.SemaphoreType.DMA((4,))],
        compiler_params=params(32),
        name="add_pieces",
    )(at, *parts)


def finish_kernel(chain, at_ref, own_ref, next_ref, across_ref, prev_ref, *rest):
    outs, proj_ref, extra_ref, held, sems = rest[:4], rest[4], rest[5], rest[6], rest[7]
    for core in range(2):
        @pl.when(at_ref[4] == core)
        def _():
            copies = []
            for k, piece in enumerate((own_ref, next_ref, across_ref, prev_ref)):
                where = spot_of(chain, core, 2, at_ref[k])
                copies.append(pltpu.make_async_copy(piece, held.at[where], sems.at[k]))
            run_copies(copies)
    extra_ref[...] = held[0, 0, 0, 80:, :].astype(jnp.float32)
    for chip in range(64):
        y, z, x = chip // 16, (chip // 4) % 4, chip % 4
        for h in range(2):
            block = held[y, z, x, 32 * h : 32 * h + 32, :].astype(jnp.float32)
            outs[y][pl.ds(32 * (chip % 16), 32), pl.ds(512 * h, 512)] = block
            block = held[y, z, x, 64 + 8 * h : 72 + 8 * h, :].astype(jnp.float32)
            proj_ref[pl.ds(8 * chip, 8), pl.ds(512 * h, 512)] = block


def finish(chain, at, pieces):
    return pl.pallas_call(
        functools.partial(finish_kernel, chain),
        in_specs=[SMEM] + [ANY] * 4,
        out_specs=[VMEM] * 6,
        out_shape=[shape_of((512, D))] * 5 + [shape_of((8, 512))],
        scratch_shapes=[pltpu.VMEM((4, 4, 4, 88, 512), jnp.bfloat16), pltpu.SemaphoreType.DMA((4,))],
        compiler_params=params(60),
        name="finish_gradients",
    )(at, *pieces)


def three_ways(chain, phase, chunk):
    prev, nxt, across = send(chunk, chain, phase, 1), send(chunk, chain, phase, -1), send(chunk, chain, phase, 2)
    return chunk, nxt, across, prev


MATS = (4, 4, 4, 4, 16, 512)


def gather_steps(chain, chunk, spots, deps):
    chunk = grow(chain, 0, spots[0], three_ways(chain, 0, chunk))
    pieces = three_ways(chain, 1, chunk)
    near = place(chain, 1, spots[1], pieces, [(4, 4, 80, 512)], ((0, 64, 0, (), 0), (128, 16, 0, (), 64)))
    each = tuple((16 * m, 16, 0, (m,), None) for m in range(4))
    mats, vecs = place(
        chain, 2, spots[2], three_ways(chain, 2, near), [MATS, (4, 4, 4, 16, 512)], each + ((64, 16, 1, (), None),), deps
    )
    far = place(chain, 1, spots[1], pieces, [(4, 4, 64, 512)], ((64, 64, 0, (), None),), (mats,))
    return mats.reshape(4, D, 512), vecs, three_ways(chain, 2, far)


def scatter_steps(chain, pieces, spots):
    for phase in (2, 1, 0):
        own, nxt, across, prev = pieces
        parts = (own, send(nxt, chain, phase, 1), send(prev, chain, phase, -1), send(across, chain, phase, 2))
        if phase:
            pieces = add_split(chain, phase - 1, spots[phase - 1], parts)
    return sum(part.astype(jnp.float32) for part in parts)


def regather_steps(chain, chunk, spots):
    for phase in range(2):
        chunk = grow(chain, phase, spots[phase], three_ways(chain, phase, chunk))
    return finish(chain, spots[2], three_ways(chain, 2, chunk))


PACKED = ((8, D),) * 4 + ((8, FF), (8, D), (24, D), (32, D)) + ((1, 8),) * 4 + ((1, 32), (1, 8), (1, 8))


def pack_kernel(at_ref, *refs):
    f32, bf16 = jnp.float32, jnp.bfloat16
    count = len(PACKED)
    sources, (blocks_ref, keep_ref, give_ref), held, sems = refs[:count], refs[count : count + 3], refs[count + 3 : -1], refs[-1]
    run_copies([pltpu.make_async_copy(source, place, sems.at[k]) for k, (source, place) in enumerate(zip(sources, held))])
    wq, wk, wv, wr, win, wp, wc, wo, ga, ub, vb, gf, bi, bo, bc = held
    first = at_ref[0] == 0
    where = at_ref[1]

    def spread(ref, size, width):
        row = lax.broadcasted_iota(jnp.int32, (size, width), 0)
        lane = lax.broadcasted_iota(jnp.int32, (size, width), 1)
        hot = (lane == size * where + row).astype(f32).astype(bf16)
        return ndot(ref[...], hot)

    for n, ref in enumerate((wq, wk, wv, wr)):
        left, right = ref[:, :512].astype(f32), ref[:, 512:].astype(f32)
        keep_ref[8 * n : 8 * n + 8, :] = jnp.where(first, left, right).astype(bf16)
        give_ref[8 * n : 8 * n + 8, :] = jnp.where(first, right, left).astype(bf16)
    for n in range(4):
        left, right = (win[:, 2048 * h + 512 * n : 2048 * h + 512 * n + 512].astype(f32) for h in range(2))
        keep_ref[32 + 8 * n : 40 + 8 * n, :] = jnp.where(first, left, right).astype(bf16)
        give_ref[32 + 8 * n : 40 + 8 * n, :] = jnp.where(first, right, left).astype(bf16)
    rows = []
    for ref in (ga, ub, vb, gf):
        wide = spread(ref, 8, D)
        rows += [wide[:, :512], wide[:, 512:]]
    wide = spread(bi, 32, 4 * D)
    halves = [jnp.concatenate([wide[:, 2048 * h + 512 * n : 2048 * h + 512 * n + 512] for n in range(4)], axis=0) for h in range(2)]
    tail = []
    for ref in (bo, bc):
        wide = spread(ref, 8, D)
        tail += [wide[:, :512], wide[:, 512:]]
    keep_ref[64:80, :] = jnp.concatenate(rows + [jnp.where(first, halves[0], halves[1])] + tail, axis=0).astype(bf16)
    give_ref[64:80, :] = jnp.concatenate(rows + [jnp.where(first, halves[1], halves[0])] + tail, axis=0).astype(bf16)
    blocks_ref[0] = wp[...]
    for q in range(3):
        blocks_ref[1 + q] = wc[8 * q : 8 * q + 8, :]
    for q in range(4):
        blocks_ref[4 + q] = wo[8 * q : 8 * q + 8, :]


def pack(at, *arrays):
    return pl.pallas_call(
        pack_kernel,
        in_specs=[SMEM] + [HBM] * len(arrays),
        out_specs=[VMEM] * 3,
        out_shape=[shape_of((8, 8, D), jnp.bfloat16)] + [shape_of((80, 512), jnp.bfloat16)] * 2,
        scratch_shapes=[pltpu.VMEM(shape, jnp.bfloat16) for shape in PACKED] + [pltpu.SemaphoreType.DMA((len(PACKED),))],
        compiler_params=params(60),
        name="pack_weights",
    )(at, *arrays)


def start_kernel(taps_ref, grad_ref, out_ref, stage, sem):
    stage[...] = cdot(taps_ref[...], grad_ref[...]).astype(jnp.bfloat16)
    run_copies([pltpu.make_async_copy(stage, out_ref.at[pl.ds(4096, 1536)], sem)])


def start_buffer(taps, grads):
    return pl.pallas_call(
        start_kernel,
        in_specs=[VMEM, VMEM],
        out_specs=HBM,
        out_shape=shape_of((BUFFER, D), jnp.bfloat16),
        scratch_shapes=[pltpu.VMEM((1536, D), jnp.bfloat16), pltpu.SemaphoreType.DMA],
        compiler_params=params(60),
        name="compression_gradient",
    )(taps, grads)


def normalize(rows):
    centred = rows - jnp.mean(rows, axis=1, keepdims=True)
    inverse = lax.rsqrt(jnp.mean(centred * centred, axis=1, keepdims=True) + EPSILON)
    return centred * inverse, inverse


ROWS = 256


def whole_spec(*shape):
    return pl.BlockSpec(shape, lambda i, c: (0,) * len(shape))


def rows_spec(lanes):
    return pl.BlockSpec((ROWS, lanes), lambda i, c: (i, 0))


def middle_kernel(core_ref, back_ref, got_ref, hidden_ref, gain_ref, gr_ref, proj_ref, hid_ref, branch_ref, att_ref, sum_ref):
    del core_ref
    back = back_ref[...].astype(jnp.float32) + got_ref[...].astype(jnp.float32)
    normed, inverse = normalize(hidden_ref[...])
    total = jnp.sum(back * normed, axis=0, keepdims=True)

    @pl.when(pl.program_id(0) == 0)
    def _():
        sum_ref[...] = total

    @pl.when(pl.program_id(0) > 0)
    def _():
        sum_ref[...] += total

    scaled = back * gain_ref[...]
    along = jnp.mean(scaled * normed, axis=1, keepdims=True)
    grad = gr_ref[...].astype(jnp.float32) + inverse * (
        scaled - jnp.mean(scaled, axis=1, keepdims=True) - normed * along
    )
    hid_ref[...] = grad
    branch = grad.astype(jnp.bfloat16)
    branch_ref[...] = branch
    att_ref[...] = tdot(branch, proj_ref[0]).astype(jnp.bfloat16)


def middle(core, back, got, hidden, gain, grad_res, large):
    return pl.pallas_call(
        middle_kernel,
        grid_spec=pltpu.PrefetchScalarGridSpec(
            num_scalar_prefetch=1,
            grid=(512 // ROWS,),
            in_specs=[
                rows_spec(D), rows_spec(D), rows_spec(D), whole_spec(1, D), rows_spec(D),
                pl.BlockSpec((1, 512, D), lambda i, c: (0, c[0], 0)),
            ],
            out_specs=[rows_spec(D), rows_spec(D), rows_spec(512), whole_spec(1, D)],
        ),
        out_shape=[
            shape_of((512, D)), shape_of((512, D), jnp.bfloat16), shape_of((512, 512), jnp.bfloat16), shape_of((1, D)),
        ],
        compiler_params=params(60),
        name="hidden_gradient",
    )(core, back, got, hidden, gain, grad_res, large)


LATE = ((512, 512), (512, D), (KTOT, D), (3, D, 512), (RELN, D))


def late_kernel(
    at_ref, p_ref, ga_ref, qu_ref, qv_ref, k_ref, v_ref, r_ref, gain_ref, small_ref, *rest
):
    f32, bf16 = jnp.float32, jnp.bfloat16
    count = len(LATE)
    sources, pieces, (gq_out, gk_out, gv_out) = rest[:count], rest[count : count + 4], rest[count + 4 : count + 7]
    ds_s, dw_s, qvr_s, gq_s, both_s, gr_s, sums_s = rest[count + 7 : count + 14]
    att_ref, branch_ref, joined_ref, mats_ref, table_ref = places = rest[count + 14 : -2]
    held, sems = rest[-2:]
    head = pl.program_id(0)

    def loads():
        out = []
        for k, (source, to) in enumerate(zip(sources, places)):
            source = source.at[pl.ds(0, 3)] if k == 3 else source
            out.append(pltpu.make_async_copy(source, to, sems.at[4 + k]))
        return out

    @pl.when(head == 0)
    def _():
        for load in loads():
            load.start()

    flip = (
        lax.broadcasted_iota(jnp.int32, (QB, QB), 0) + lax.broadcasted_iota(jnp.int32, (QB, QB), 1) == QB - 1
    ).astype(f32).astype(bf16)
    du = jnp.zeros((1, HEAD_DIM), f32)
    dv = du
    for b in range(SEG // QB):
        i0, nk, c0 = QB * b, COMP + MEM + QB * (b + 1), SEG - QB - QB * b
        wl = nk + QB
        rows = pl.ds(i0, QB)
        p = p_ref[0, rows, pl.ds(0, nk)].astype(f32)
        dp = tdot(ga_ref[rows, :], v_ref[pl.ds(0, nk), :])
        pd = p * dp
        delta = jnp.sum(pd, axis=1, keepdims=True)
        ds = (pd - p * delta).astype(bf16)
        ds_s[rows, pl.ds(0, nk)] = ds
        if nk < KTOT:
            ds_s[rows, pl.ds(nk, KTOT - nk)] = jnp.zeros((QB, KTOT - nk), bf16)
        wide = jnp.concatenate([ndot(flip, ds), jnp.zeros((QB, QB), f32)], axis=1)
        wide = pltpu.roll(wide, 0, 1, stride=1, stride_axis=0).astype(bf16)
        qvr_s[rows, :] = ndot(flip, qv_ref[rows, :]).astype(bf16)
        dw_s[rows, pl.ds(c0, wl)] = wide
        if c0:
            dw_s[rows, pl.ds(0, c0)] = jnp.zeros((QB, c0), bf16)
        dqu = ndot(ds, k_ref[pl.ds(0, nk), :]) * SCALE
        dqr = ndot(wide, r_ref[pl.ds(c0, wl), :]) * SCALE
        hi = dqr.astype(bf16)
        lo = (dqr - hi.astype(f32)).astype(bf16)
        dqv = ndot(flip, hi) + ndot(flip, lo)
        du += jnp.sum(dqu, axis=0, keepdims=True)
        dv += jnp.sum(dqv, axis=0, keepdims=True)
        gq_out[rows, :] = (dqu + dqv).astype(bf16)
    lanes = pl.ds(pl.multiple_of(HEAD_DIM * head, HEAD_DIM), HEAD_DIM)
    above = pl.ds(pl.multiple_of(512 + HEAD_DIM * head, HEAD_DIM), HEAD_DIM)
    sums_s[0:1, lanes] = du
    sums_s[1:2, lanes] = dv
    gq_s[:, lanes] = gq_out[...]
    grad = (cdot(ds_s[...], qu_ref[...]) * SCALE).astype(bf16)
    both_s[:, lanes] = grad
    gk_out[...] = grad[COMP + MEM :]
    grad = cdot(p_ref[0], ga_ref[...]).astype(bf16)
    both_s[:, above] = grad
    gv_out[...] = grad[COMP + MEM :]
    gr_s[:, lanes] = (cdot(dw_s[...], qvr_s[...]) * SCALE).astype(bf16)

    @pl.when(head == 3)
    def _():
        for load in loads():
            load.wait()
        proj = cdot(att_ref[...], branch_ref[...]).astype(bf16).reshape(4, 4, 4, 8, D)
        for h in range(2):
            held[:, :, :, 64 + 8 * h : 72 + 8 * h, :] = proj[..., 512 * h : 512 * h + 512]
        ones = jnp.ones((8, 512), bf16)

        def keep(m, grad):
            low = grad.astype(bf16)
            for h in range(2):
                held[m, :, :, 32 * h : 32 * h + 32, :] = low[512 * h : 512 * h + 512].reshape(4, 4, 32, 512)
            if m == 3:
                return jnp.zeros((8, D), f32)
            product = grad * mats_ref[m].astype(f32)
            high = product.astype(bf16)
            return tdot(ones, high) + tdot(ones, (product - high.astype(f32)).astype(bf16))

        keep(3, cdot(table_ref[...], gr_s[...]))
        total = keep(0, cdot(joined_ref[pl.ds(COMP + MEM, SEG), :], gq_s[...]))
        pair = cdot(joined_ref[...], both_s[...])
        total += keep(1, pair[:, :512])
        total += keep(2, pair[:, 512:])
        total = total[:1] / gain_ref[...]
        extra = jnp.concatenate([total[:, :512], total[:, 512:], sums_s[0:2, :], small_ref[4:, :]], axis=0)
        held[:, :, :, 80:, :] = jnp.zeros((4, 4, 4, 8, 512), bf16)
        held[0, 0, 0, 80:, :] = extra.astype(bf16)
        send_pieces("AB", 2, at_ref, held, pieces, sems)


def late_gradients(at, probs, grad_att, query_u, query_v, keys, values, rel, gain, small, *arrays):
    f32, bf16 = jnp.float32, jnp.bfloat16
    col = lambda n: pl.BlockSpec((n, HEAD_DIM), lambda h: (0, h))
    const = lambda *shape: pl.BlockSpec(shape, lambda h: (0, 0))
    return pl.pallas_call(
        late_kernel,
        grid=(4,),
        in_specs=[
            SMEM, pl.BlockSpec((1, SEG, KTOT), lambda h: (h, 0, 0)),
            col(SEG), col(SEG), col(SEG), col(KTOT), col(KTOT), col(RELN), const(1, D), const(8, 512),
        ] + [HBM] * len(LATE),
        out_specs=[ANY] * 4 + [col(SEG)] * 3,
        out_shape=[shape_of((4, 4, 88, 512), bf16)] * 4 + [shape_of((SEG, 512), bf16)] * 3,
        scratch_shapes=[
            pltpu.VMEM((SEG, KTOT), bf16),
            pltpu.VMEM((SEG, RELN), bf16),
            pltpu.VMEM((SEG, HEAD_DIM), bf16),
            pltpu.VMEM((SEG, 512), bf16),
            pltpu.VMEM((KTOT, D), bf16),
            pltpu.VMEM((RELN, 512), bf16),
            pltpu.VMEM((8, 512), f32),
        ]
        + [pltpu.VMEM(shape, bf16) for shape in LATE]
        + [pltpu.VMEM((4, 4, 4, 88, 512), bf16), pltpu.SemaphoreType.DMA((4 + len(LATE),))],
        compiler_params=params(60),
        cost_estimate=pl.CostEstimate(flops=20 << 30, bytes_accessed=30 << 20, transcendentals=0),
        name="attention_backward",
    )(at, probs, grad_att, query_u, query_v, keys, values, rel, gain, small, *arrays)


def ffn_kernel(at_ref, att_ref, got_ref, proj_ref, seg_ref, gain_ref, gr_ref, *rest):
    pieces, quarters, bias_ref, out_ref, back_ref, part_ref, hidden_ref = rest[:4], rest[4:8], rest[8], *rest[10:14]
    panels, act_ref, turned_ref, natural, stage_in, stage_out, sums, back_sum, part_sum, arrived, sems = rest[14:]
    p = pl.program_id(0)
    slot = lax.rem(p, 2)

    def panel_copies(core, m):
        rows = pl.ds(16 * m if isinstance(m, int) else pl.multiple_of(16 * m, 16), 16)
        return [
            pltpu.make_async_copy(
                pieces[k].at[:, :, rows], panels.at[(m,) + spot_of("AB", core, 2, at_ref[k])], arrived.at[4 * m + k]
            )
            for k in range(4)
        ]

    for core in range(2):
        @pl.when((p == 0) & (at_ref[4] == core))
        def _():
            for m in range(4):
                for copy in panel_copies(core, m):
                    copy.start()

    @pl.when(p == 0)
    def _():
        core = at_ref[4]
        mine = proj_ref[0, pl.ds(pl.multiple_of(512 * core, 512), 512), :]
        other = proj_ref[0, pl.ds(pl.multiple_of(512 - 512 * core, 512), 512), :]
        hidden = seg_ref[...].astype(jnp.float32) + ndot(att_ref[...], mine) + ndot(got_ref[...], other)
        hidden_ref[...] = hidden
        act = (normalize(hidden)[0] * gain_ref[...]).astype(jnp.bfloat16)
        act_ref[...] = act
        turned_ref[...] = act.T

    for core in range(2):
        @pl.when(at_ref[4] == core)
        def _():
            for copy in panel_copies(core, p):
                copy.wait()

    def sending(step, buffer):
        rows = pl.ds(pl.multiple_of(1024 * (step // 2), 1024), 1024)
        lanes = pl.ds(pl.multiple_of(512 * lax.rem(step, 2), 512), 512)
        below = pl.ds(pl.multiple_of(2048 + 512 * step, 512), 512)
        return [
            pltpu.make_async_copy(stage_in.at[buffer], out_ref.at[rows, lanes], sems.at[buffer]),
            pltpu.make_async_copy(stage_out.at[buffer], out_ref.at[below], sems.at[2 + buffer]),
        ]

    @pl.when(p >= 2)
    def _():
        for copy in sending(p - 2, slot):
            copy.wait()

    act, grad, w_one = act_ref[...], gr_ref[...], panels[p].reshape(D, 512)
    for q in range(4):
        for shard in range(16):
            natural[32 * shard + 8 * q : 32 * shard + 8 * q + 8, :] = quarters[q][0, 8 * shard : 8 * shard + 8, :]
    w_two = natural[...]
    pre = ndot(act, w_one) + bias_ref[0]
    inner = math.sqrt(2.0 / math.pi)
    square = pre * pre
    tanh = jnp.tanh(inner * pre * (1.0 + 0.044715 * square))
    act_low = (0.5 * pre * (1.0 + tanh)).astype(jnp.bfloat16)
    slope = 0.5 * (1.0 + tanh) + (0.5 * inner) * pre * (1.0 - tanh * tanh) * (1.0 + (3.0 * 0.044715) * square)
    grad_act = tdot(grad, w_two)
    grad_pre = (grad_act * slope).astype(jnp.bfloat16)
    stage_in[slot] = ndot(turned_ref[...], grad_pre).astype(jnp.bfloat16)
    stage_out[slot] = cdot(act_low, grad).astype(jnp.bfloat16)
    for copy in sending(p, slot):
        copy.start()
    total = jnp.sum(grad_pre.astype(jnp.float32), axis=0, keepdims=True)
    total = jnp.concatenate([total, total], axis=1)
    row = lax.broadcasted_iota(jnp.int32, (16, D), 0)
    lane = lax.broadcasted_iota(jnp.int32, (16, D), 1)
    mine = (row == p // 2) & (lane // 512 == lax.rem(p, 2))

    @pl.when(p == 0)
    def _():
        sums[...] = jnp.zeros_like(sums)
        back_sum[...] = tdot(grad_pre, w_one)
        part_sum[...] = ndot(act_low, w_two)

    @pl.when((p > 0) & (p < 3))
    def _():
        back_sum[...] += tdot(grad_pre, w_one)
        part_sum[...] += ndot(act_low, w_two)

    @pl.when(p == 3)
    def _():
        back_ref[...] = (back_sum[...] + tdot(grad_pre, w_one)).astype(jnp.bfloat16)
        part_ref[...] = (part_sum[...] + ndot(act_low, w_two)).astype(jnp.bfloat16)

    sums[...] = jnp.where(mine, total, sums[...].astype(jnp.float32)).astype(jnp.bfloat16)

    @pl.when(p == 3)
    def _():
        last = pltpu.make_async_copy(sums, out_ref.at[pl.ds(5632, 16)], sems.at[4])
        last.start()
        for copy in sending(p - 1, 1 - slot) + sending(p, slot):
            copy.wait()
        last.wait()


def ffn(at, att, got, seg, gain, grad, pieces, large, bias, buffer):
    f32, bf16 = jnp.float32, jnp.bfloat16
    whole = pl.BlockSpec((512, D), lambda p, c: (0, 0))
    quarter = lambda q: pl.BlockSpec((1, 128, D), lambda p, c: (4 + q, 4 * c[4] + p, 0))
    return pl.pallas_call(
        ffn_kernel,
        grid_spec=pltpu.PrefetchScalarGridSpec(
            num_scalar_prefetch=1,
            grid=(4,),
            in_specs=[
                whole_spec(512, 512),
                whole_spec(512, 512),
                whole_spec(1, D, D),
                whole,
                whole_spec(1, D),
                whole,
                *([ANY] * 4),
                *(quarter(q) for q in range(4)),
                pl.BlockSpec((1, 1, 512), lambda p, c: (p, 0, 0)),
                HBM,
            ],
            out_specs=[HBM, whole, whole, whole],
            scratch_shapes=[
                pltpu.VMEM(MATS, bf16),
                pltpu.VMEM((512, D), bf16),
                pltpu.VMEM((D, 512), bf16),
                pltpu.VMEM((512, D), bf16),
                pltpu.VMEM((2, D, 512), bf16),
                pltpu.VMEM((2, 512, D), bf16),
                pltpu.VMEM((16, D), bf16),
                pltpu.VMEM((512, D), f32),
                pltpu.VMEM((512, D), f32),
                pltpu.SemaphoreType.DMA((16,)),
                pltpu.SemaphoreType.DMA((5,)),
            ],
        ),
        out_shape=[shape_of((BUFFER, D), bf16), shape_of((512, D), bf16), shape_of((512, D), bf16), shape_of((512, D))],
        input_output_aliases={16: 0},
        compiler_params=params(60),
        cost_estimate=pl.CostEstimate(flops=12 * 512 * 1024 * 2048, bytes_accessed=24 << 20, transcendentals=512 * 2048),
        name="feed_forward",
    )(at, att, got, large, seg, gain, grad, *pieces, large, large, large, large, bias, buffer)


STEP = 256
SLOTS = 4


def widen_kernel(core_ref, second, deps, *refs):
    core = core_ref[0]
    source, outs = refs[0], refs[1 + deps : -4]
    low, high, loads, stores = refs[-4:]
    jobs = []
    if second:
        for q in range(2):
            for r in range(512 // STEP):
                rows = pl.ds(512 * q + STEP * r, STEP)
                lanes = pl.ds(pl.multiple_of(D * (2 * (1 - core) + q), D), D)
                jobs.append((rows, outs[0].at[pl.ds(STEP * r, STEP), lanes]))
    else:
        for r in range(2048 // STEP):
            jobs.append((pl.ds(2048 + STEP * r, STEP), outs[1].at[pl.ds(STEP * r, STEP)]))
        for r in range(1536 // STEP):
            jobs.append((pl.ds(4096 + STEP * r, STEP), outs[2].at[pl.ds(STEP * r, STEP)]))
        for q in range(2):
            for r in range(512 // STEP):
                rows = pl.ds(pl.multiple_of(D * q + 512 * core + STEP * r, STEP), STEP)
                lanes = pl.ds(pl.multiple_of(D * (2 * core + q), D), D)
                jobs.append((rows, outs[0].at[pl.ds(STEP * r, STEP), lanes]))

    def load(k):
        return pltpu.make_async_copy(source.at[jobs[k][0]], low.at[k % SLOTS], loads.at[k % SLOTS])

    def store(k):
        return pltpu.make_async_copy(high.at[k % SLOTS], jobs[k][1], stores.at[k % SLOTS])

    for k in range(SLOTS):
        load(k).start()
    for k in range(len(jobs)):
        load(k).wait()
        if k >= SLOTS:
            store(k - SLOTS).wait()
        high[k % SLOTS] = low[k % SLOTS].astype(jnp.float32)
        store(k).start()
        if k + SLOTS < len(jobs):
            load(k + SLOTS).start()
    for k in range(len(jobs) - SLOTS, len(jobs)):
        store(k).wait()
    if not second:
        run_copies([pltpu.make_async_copy(source.at[pl.ds(5632, 16)], low.at[0, pl.ds(0, 16)], loads.at[0])])
        high[0, :16, :] = low[0, :16, :].astype(jnp.float32)
        run_copies([pltpu.make_async_copy(high.at[0, pl.ds(0, 16)], outs[3], stores.at[0])])


def widen(core, source, deps, into=None):
    shapes = [(512, FF)] if into is not None else [(512, FF), (2048, D), (1536, D), (16, D)]
    deps = tuple(deps) + (() if into is None else (into,))

    def body(core_ref, *refs):
        widen_kernel(core_ref, into is not None, len(deps), *refs)

    return pl.pallas_call(
        body,
        in_specs=[SMEM, HBM] + [ANY] * len(deps),
        out_specs=[HBM] * len(shapes),
        out_shape=[shape_of(shape) for shape in shapes],
        input_output_aliases={} if into is None else {1 + len(deps): 0},
        scratch_shapes=[
            pltpu.VMEM((SLOTS, STEP, D), jnp.bfloat16),
            pltpu.VMEM((SLOTS, STEP, D), jnp.float32),
            pltpu.SemaphoreType.DMA((SLOTS,)),
            pltpu.SemaphoreType.DMA((SLOTS,)),
        ],
        compiler_params=params(60),
        name="widen_gradients",
    )(core, source, *deps)


def pick_kernel(core_ref, source_ref, *rest):
    del core_ref
    rest[-1][...] = source_ref[...]


def pick_halves(core, buffer, deps):
    return pl.pallas_call(
        pick_kernel,
        grid_spec=pltpu.PrefetchScalarGridSpec(
            num_scalar_prefetch=1,
            grid=(2,),
            in_specs=[pl.BlockSpec((512, D), lambda q, c: (2 * q + 1 - c[0], 0))] + [ANY] * len(deps),
            out_specs=pl.BlockSpec((512, D), lambda q, c: (q, 0)),
        ),
        out_shape=shape_of((D, D), jnp.bfloat16),
        compiler_params=params(60),
        name="other_half",
    )(core, buffer, *deps)


def on_device(
    segment, memory, compressed, mem_count, comp_count, attn_gain, w_query, w_key, w_value, u_bias, v_bias,
    w_rel, w_proj, ffn_gain, w_in, b_in, w_out, b_out, w_comp, b_comp, out_grad, comp_grad,
):
    f32, bf16 = jnp.float32, jnp.bfloat16
    core, chip = lax.axis_index("blk"), lax.axis_index("dp")
    first = core == 0
    core_at = core.reshape(1).astype(jnp.int32)
    coords = {"y": chip // 16, "z": (chip // 4) % 4, "x": chip % 4}
    spots = {}
    for chain in ("AB",):
        spots[chain] = []
        for phase in range(3):
            at = jnp.where(first, coords[PATHS[chain[0]][phase]], coords[PATHS[chain[1]][phase]])
            spots[chain].append(jnp.stack([(at + k) % 4 for k in range(4)] + [core]).astype(jnp.int32))

    def both(own, other, axis=0):
        return jnp.where(first, jnp.concatenate([own, other], axis), jnp.concatenate([other, own], axis))

    def half(array, which, axis):
        size = array.shape[axis] // 2
        return lax.dynamic_slice_in_dim(array, which * size, size, axis)

    where_at = jnp.stack([core, 2 * chip + core]).astype(jnp.int32)
    row = lambda vector: vector.reshape(1, -1)
    blocks, keep, give = pack(
        where_at, w_query, w_key, w_value, w_rel, w_in, w_proj, w_comp, w_out,
        row(attn_gain), row(u_bias), row(v_bias), row(ffn_gain), row(b_in), row(b_out), row(b_comp),
    )
    large = lax.all_gather(blocks, ALL_AXES, axis=1, tiled=True)
    got = swap(give)
    chunk = jnp.concatenate(
        [both(keep[8 * n : 8 * n + 8], got[8 * n : 8 * n + 8]) for n in range(8)] + [keep[64:] + got[64:]]
    )

    pieces = [both(array[0], swap(array[0])) for array in (compressed, memory, segment, out_grad, comp_grad)]
    seg_at = COMP + MEM
    grad_res, comp_flat = pieces[3], pieces[4]
    all_rows = jnp.concatenate(pieces[:3])

    def centre(rows):
        mean = jnp.mean(rows, axis=-1, keepdims=True)
        centred = rows - mean
        return mean, lax.rsqrt(jnp.mean(centred * centred, axis=-1, keepdims=True) + EPSILON)

    mean_one, inverse_one = centre(all_rows.astype(f32))

    distance = (KTOT - 1) - jnp.arange(RELN, dtype=f32)
    frequency = jnp.exp(jnp.arange(D // 2, dtype=f32) * (-2.0 * math.log(10000.0) / D))
    coarse = distance[::32, None] * frequency[None, :]
    fine = jnp.arange(32, dtype=f32)[:, None] * frequency[None, :]
    sin_a, cos_a = (trig(coarse)[:, None, :] for trig in (jnp.sin, jnp.cos))
    sin_b, cos_b = (trig(fine)[None, :, :] for trig in (jnp.sin, jnp.cos))
    sines, cosines = sin_a * cos_b - cos_a * sin_b, cos_a * cos_b + sin_a * sin_b
    table = jnp.concatenate([sines.reshape(RELN, 512), cosines.reshape(RELN, 512)], axis=1)
    table = jnp.where(distance[:, None] >= 0.0, table, 0.0).astype(bf16)

    slot = jnp.arange(MEM, dtype=jnp.int32)
    masked = jnp.where((slot >= MEM - mem_count[0])[:, None], pieces[1], jnp.zeros_like(pieces[1]))
    windows = masked.reshape(MEM // RATE, RATE * D)
    buffer = start_buffer(half(windows, core, 1), comp_flat)

    mats, vecs, panels = gather_steps("AB", chunk, spots["AB"], (mean_one, inverse_one, all_rows, table, buffer))
    vecs = jnp.sum(vecs.astype(f32), axis=(0, 1, 2))
    gain_one, gain_two = vecs[:2].reshape(1, D), vecs[6:8].reshape(1, D)
    bias_u = jnp.where(first, vecs[2], vecs[3])
    bias_v = jnp.where(first, vecs[4], vecs[5])
    joined = ((all_rows.astype(f32) - mean_one) * inverse_one * gain_one).astype(bf16)
    query_rows = ndot(joined[seg_at:], mats[0])
    key_rows = ndot(joined, mats[1]).astype(bf16)
    value_rows = ndot(joined, mats[2]).astype(bf16)
    rel_rows = ndot(table, mats[3]).astype(bf16)
    query_u = (query_rows + bias_u).astype(bf16)
    query_v = (query_rows + bias_v).astype(bf16)
    counts = jnp.concatenate([mem_count, comp_count])
    attended, probs = attn_fwd(counts, query_u, query_v, key_rows, value_rows, rel_rows)

    ffn_bias = vecs[8:12].reshape(4, 1, 512)
    out_bias, comp_bias = vecs[12:14].reshape(1, D), vecs[14:16].reshape(1, D)
    buffer, back, partial, hidden = ffn(
        spots["AB"][2], attended, swap(attended), pieces[2], gain_two, grad_res, panels, large, ffn_bias, buffer
    )
    buffer = lax.psum(buffer, "dp")
    grad_hidden, grad_branch, grad_att, d_gain_two = middle(
        core_at, back, swap(back), hidden, gain_two, grad_res, large
    )

    d_b_out = jnp.sum(half(grad_res, core, 1).astype(f32), axis=0, keepdims=True)
    d_b_comp = jnp.sum(half(comp_flat, core, 1).astype(f32), axis=0, keepdims=True)
    small = jnp.concatenate(
        [jnp.zeros((4, 512), f32), half(d_gain_two, core, 1), d_b_out, d_b_comp, jnp.zeros((1, 512), f32)]
    )
    *pieces_late, grad_query, grad_keys, grad_values = late_gradients(
        spots["AB"][2], probs, grad_att, query_u, query_v, key_rows, value_rows, rel_rows, gain_one, small,
        attended, grad_branch, joined, mats, table,
    )
    share = scatter_steps("AB", pieces_late, spots["AB"])
    keep = half(share[:64], core, 0).astype(bf16)
    mail = swap(jnp.concatenate([half(share[:64], 1 - core, 0), share[80:]]).astype(bf16))
    gains = jnp.where(jnp.arange(8)[:, None] < 2, share[80:] + mail[32:].astype(f32), share[80:])
    late = jnp.concatenate([both(keep, mail[:32]), share[64:80].astype(bf16), gains.astype(bf16)])
    *late, d_proj, extra = regather_steps("AB", late, spots["AB"])

    partial_sum = half(partial, core, 0).astype(f32) + swap(half(partial, 1 - core, 0)).astype(f32)
    result = half(hidden, core, 0) + partial_sum + out_bias
    output = result.astype(bf16)

    comp_proj = large[1:4].reshape(3, 128, 8, D).transpose(1, 0, 2, 3).reshape(RATE * D, D)
    new_compressed = (ndot(half(windows, core, 0), comp_proj) + comp_bias).astype(bf16)

    grad_seg = (
        tdot(grad_query, mats[0]) + tdot(grad_keys, mats[1]) + tdot(grad_values, mats[2])
    )
    grad_seg = half(grad_seg, core, 0) + swap(half(grad_seg, 1 - core, 0))
    scaled_one = grad_seg * gain_one
    own_segment = segment[0].astype(f32)
    mean_seg, inverse_seg = centre(own_segment)
    normed_seg = (own_segment - mean_seg) * inverse_seg
    d_segment = half(grad_hidden, core, 0) + inverse_seg * (
        scaled_one
        - jnp.mean(scaled_one, axis=-1, keepdims=True)
        - normed_seg * jnp.mean(scaled_one * normed_seg, axis=-1, keepdims=True)
    )

    deps = (late[0], output, new_compressed, d_segment)
    others = pick_halves(core_at, buffer, deps)
    d_in, d_out, d_comp, sums = widen(core_at, buffer, deps + (others,))
    (d_in,) = widen(core_at, swap(others), (), d_in)
    d_b_in = sums[:2].reshape(2048)
    return (
        output[None],
        new_compressed[None],
        d_segment[None],
        jnp.where(first, extra[0], extra[1]),
        late[0],
        late[1],
        late[2],
        extra[2],
        extra[3],
        late[3],
        d_proj,
        extra[4],
        d_in,
        d_b_in,
        d_out,
        extra[5],
        d_comp,
        extra[6],
    )


def solution(mesh):
    rows, weight, vector = P("dp", "blk", None), P(("dp", "blk"), None), P(("dp", "blk"))
    placed = (
        rows, rows, rows, P("dp"), P("dp"), vector, weight, weight, weight, vector, vector,
        weight, weight, vector, weight, vector, weight, vector, weight, vector, rows, rows,
    )
    half_one, half_two = P("blk"), P("blk", None)
    return jax.shard_map(
        on_device,
        mesh=mesh,
        in_specs=placed,
        out_specs=(
            rows, rows, rows, half_one, half_two, half_two, half_two, half_one, half_one,
            half_two, half_two, half_one, half_two, half_one, half_two, half_one, half_two, half_one,
        ),
        check_vma=False,
    )
```

```python
import math, functools
import jax, jax.numpy as jnp
from jax import lax
from jax.sharding import PartitionSpec as P
from jax.experimental import pallas as pl
from jax.experimental.pallas import tpu as pltpu
D=1024
FF=4096
HEAD_DIM=128
SEG=512
MEM=384
COMP=512
RATE=3
KTOT=1408
RELN=1536
QB=128
EPSILON=1e-05
SCALE=1.0/math.sqrt(HEAD_DIM); NEG=-1e30
def tdot(a,b):
    return lax.dot_general(a,b,(((1,),(1,)),((),())),preferred_element_type=jnp.float32)
def ndot(a,b):
    return lax.dot_general(a,b,(((1,),(0,)),((),())),preferred_element_type=jnp.float32)
def cdot(a,b):
    return lax.dot_general(a,b,(((0,),(0,)),((),())),preferred_element_type=jnp.float32)

def attn_fwd_kernel(cnt_ref, qu_ref, qv_ref, k_ref, v_ref, r_ref, att_ref, p_ref):
    mc = cnt_ref[0]; cc = cnt_ref[1]
    kp = lax.broadcasted_iota(jnp.int32,(1,COMP+MEM),1)
    ok = ((kp < COMP) & (kp >= COMP-cc)) | ((kp>=COMP)&(kp>=COMP+MEM-mc))
    old_bias = jnp.where(ok, 0.0, NEG)
    tri = jnp.where(lax.broadcasted_iota(jnp.int32,(QB,QB),1) <= lax.broadcasted_iota(jnp.int32,(QB,QB),0), 0.0, NEG)
    for b in range(SEG//QB):
        i0=QB*b; nk=COMP+MEM+QB*(b+1); c0=SEG-QB-QB*b; wl=nk+QB
        s = tdot(qu_ref[pl.ds(i0,QB),:], k_ref[pl.ds(0,nk),:])
        w = tdot(qv_ref[pl.ds(i0,QB),:], r_ref[pl.ds(c0,wl),:])
        w = pltpu.roll(w, wl-(QB-1), 1, stride=1, stride_axis=0)[:,:nk]
        s = (s+w)*SCALE
        parts=[s[:,:COMP+MEM]+old_bias]
        if b: parts.append(s[:,COMP+MEM:nk-QB])
        parts.append(s[:,nk-QB:]+tri)
        s=jnp.concatenate(parts,axis=1)
        m=jnp.max(s,axis=1,keepdims=True)
        e=jnp.exp(s-m)
        l=jnp.sum(e,axis=1,keepdims=True)
        p=(e*(1.0/l)).astype(jnp.bfloat16)
        p_ref[0,pl.ds(i0,QB),pl.ds(0,nk)]=p
        if nk<KTOT: p_ref[0,pl.ds(i0,QB),pl.ds(nk,KTOT-nk)]=jnp.zeros((QB,KTOT-nk),jnp.bfloat16)
        att_ref[pl.ds(i0,QB),:]=ndot(p,v_ref[pl.ds(0,nk),:]).astype(jnp.bfloat16)

def attn_fwd(cnt,qu,qv,k,v,r):
    nh=qu.shape[1]//HEAD_DIM
    col=lambda n: pl.BlockSpec((n,HEAD_DIM),lambda h:(0,h))
    return pl.pallas_call(attn_fwd_kernel, grid=(nh,),
        in_specs=[pl.BlockSpec(memory_space=pltpu.SMEM),col(SEG),col(SEG),col(KTOT),col(KTOT),col(RELN)],
        out_specs=[col(SEG),pl.BlockSpec((1,SEG,KTOT),lambda h:(h,0,0))],
        out_shape=[jax.ShapeDtypeStruct((SEG,nh*HEAD_DIM),jnp.bfloat16),jax.ShapeDtypeStruct((nh,SEG,KTOT),jnp.bfloat16)],
        compiler_params=pltpu.CompilerParams(vmem_limit_bytes=40<<20),
        cost_estimate=pl.CostEstimate(flops=6*nh*SEG*KTOT*HEAD_DIM,bytes_accessed=12<<20,transcendentals=nh*SEG*KTOT),
        name="attention_forward")(cnt,qu,qv,k,v,r)


PATHS = {"A": ("x", "z", "y"), "B": ("y", "x", "z"), "C": ("z", "y", "x")}
SPOT = {
    name: tuple(sorted(path[: phase + 1], key="yzx".index).index(path[phase]) for phase in range(3))
    for name, path in PATHS.items()
}
STRIDE = {"y": 16, "z": 4, "x": 1}
ALL_AXES = ("dp", "blk")
BUFFER = 5648
ANY = pl.BlockSpec(memory_space=pl.ANY)
SMEM = pl.BlockSpec(memory_space=pltpu.SMEM)
VMEM = pl.BlockSpec(memory_space=pltpu.VMEM)
HBM = pl.BlockSpec(memory_space=pltpu.HBM)


def params(mib=40):
    return pltpu.CompilerParams(vmem_limit_bytes=mib << 20)


def shape_of(shape, dtype=jnp.float32):
    return jax.ShapeDtypeStruct(shape, dtype)


def swap(array):
    return lax.ppermute(array, "blk", [(0, 1), (1, 0)])


def step_pairs(chain, phase, delta):
    pairs = []
    for chip in range(64):
        for core in range(2):
            stride = STRIDE[PATHS[chain[core]][phase]]
            at = (chip // stride) % 4
            pairs.append((2 * chip + core, 2 * (chip + ((at + delta) % 4 - at) * stride) + core))
    return pairs


def send(array, chain, phase, delta):
    return lax.ppermute(array, ALL_AXES, step_pairs(chain, phase, delta))


def run_copies(copies):
    for copy in copies:
        copy.start()
    for copy in copies:
        copy.wait()


def spot_of(chain, core, phase, index, part=None):
    where = [slice(None)] * phase
    if part is not None:
        where[0] = pl.ds(2 * part, 2)
    where.insert(SPOT[chain[core]][phase], index)
    return tuple(where)


DIRECT = ((0, None), (1, None), (2, None), (3, None))
RING = ((0, None), (1, None), (2, 0), (2, 1), (3, None))


def place_kernel(chain, phase, moves, deps, ways, at_ref, *rest):
    pieces, outs, sems = rest[: len(ways)], rest[len(ways) + deps : -1], rest[-1]
    lead = (slice(None),) * phase
    for core in range(2):
        @pl.when(at_ref[4] == core)
        def _():
            copies = []
            for j, ((k, part), piece) in enumerate(zip(ways, pieces)):
                where = spot_of(chain, core, phase, at_ref[k], part)
                for n, (start, size, out, head, to) in enumerate(moves):
                    source = piece.at[lead + (pl.ds(start, size),)]
                    target = outs[out].at[head + where]
                    if to is not None:
                        target = target.at[lead + (pl.ds(to, size),)]
                    copies.append(pltpu.make_async_copy(source, target, sems.at[j * len(moves) + n]))
            run_copies(copies)


def place(chain, phase, at, pieces, shapes, moves, deps=(), mib=32):
    ways = RING if len(pieces) == 5 else DIRECT
    out = pl.pallas_call(
        functools.partial(place_kernel, chain, phase, moves, len(deps), ways),
        in_specs=[SMEM] + [ANY] * (len(ways) + len(deps)),
        out_specs=[VMEM] * len(shapes),
        out_shape=[shape_of(shape, jnp.bfloat16) for shape in shapes],
        scratch_shapes=[pltpu.SemaphoreType.DMA((len(ways) * len(moves),))],
        compiler_params=params(mib),
        name="place_pieces",
    )(at, *pieces, *deps)
    return out if len(shapes) > 1 else out[0]


def grow(chain, phase, at, pieces):
    rows, lanes = pieces[0].shape[-2:]
    return place(chain, phase, at, pieces, [(4,) * (phase + 1) + (rows, lanes)], ((0, rows, 0, (), None),))


def send_pieces(chain, phase, ways, at_ref, held, pieces, sems):
    for core in range(2):
        @pl.when(at_ref[4] == core)
        def _():
            copies = []
            for j, ((k, part), piece) in enumerate(zip(ways, pieces)):
                where = spot_of(chain, core, phase, at_ref[k], part)
                copies.append(pltpu.make_async_copy(held.at[where], piece, sems.at[j]))
            run_copies(copies)


def split_kernel(chain, phase, count, at_ref, *rest):
    parts, pieces, held, sems = rest[:count], rest[count : count + 4], rest[-2], rest[-1]
    held[...] = sum(ref[...].astype(jnp.float32) for ref in parts).astype(jnp.bfloat16)
    send_pieces(chain, phase, DIRECT, at_ref, held, pieces, sems)


def add_split(chain, phase, at, parts):
    shape = parts[0].shape
    return pl.pallas_call(
        functools.partial(split_kernel, chain, phase, len(parts)),
        in_specs=[SMEM] + [VMEM] * len(parts),
        out_specs=[ANY] * 4,
        out_shape=[shape_of(shape[1:], jnp.bfloat16)] * 4,
        scratch_shapes=[pltpu.VMEM(shape, jnp.bfloat16), pltpu.SemaphoreType.DMA((4,))],
        compiler_params=params(32),
        name="add_pieces",
    )(at, *parts)


def halves_kernel(next_ref, prev_ref, low_ref, high_ref, next_out, prev_out):
    f32, bf16 = jnp.float32, jnp.bfloat16
    next_out[:2] = (next_ref[:2].astype(f32) + low_ref[...].astype(f32)).astype(bf16)
    next_out[2:] = next_ref[2:]
    prev_out[:2] = prev_ref[:2]
    prev_out[2:] = (prev_ref[2:].astype(f32) + high_ref[...].astype(f32)).astype(bf16)


def add_halves(*arrays):
    return pl.pallas_call(
        halves_kernel,
        in_specs=[VMEM] * 4,
        out_specs=[VMEM] * 2,
        out_shape=[shape_of(arrays[0].shape, jnp.bfloat16)] * 2,
        compiler_params=params(32),
        name="add_halves",
    )(*arrays)


def finish_kernel(chain, at_ref, *rest):
    received, (*outs, proj_ref, extra_ref, held, sems) = rest[:5], rest[6:]
    for core in range(2):
        @pl.when(at_ref[4] == core)
        def _():
            copies = []
            for j, ((k, part), piece) in enumerate(zip(RING, received)):
                where = spot_of(chain, core, 2, at_ref[k], part)
                copies.append(pltpu.make_async_copy(piece, held.at[where], sems.at[j]))
            run_copies(copies)
    extra_ref[...] = held[0, 0, 0, 80:, :].astype(jnp.float32)
    for chip in range(64):
        y, z, x = chip // 16, (chip // 4) % 4, chip % 4
        for h in range(2):
            block = held[y, z, x, 32 * h : 32 * h + 32, :].astype(jnp.float32)
            outs[y][pl.ds(32 * (chip % 16), 32), pl.ds(512 * h, 512)] = block
            block = held[y, z, x, 64 + 8 * h : 72 + 8 * h, :].astype(jnp.float32)
            proj_ref[pl.ds(8 * chip, 8), pl.ds(512 * h, 512)] = block


def finish(chain, at, pieces, after):
    return pl.pallas_call(
        functools.partial(finish_kernel, chain),
        in_specs=[SMEM] + [ANY] * 6,
        out_specs=[VMEM] * 6,
        out_shape=[shape_of((512, D))] * 5 + [shape_of((8, 512))],
        scratch_shapes=[pltpu.VMEM((4, 4, 4, 88, 512), jnp.bfloat16), pltpu.SemaphoreType.DMA((5,))],
        compiler_params=params(60),
        name="finish_gradients",
    )(at, *pieces, after)


def three_ways(chain, phase, chunk):
    prev, nxt, across = send(chunk, chain, phase, 1), send(chunk, chain, phase, -1), send(chunk, chain, phase, 2)
    return chunk, nxt, across, prev


def ring_ways(chain, chunk):
    prev, nxt = send(chunk, chain, 2, 1), send(chunk, chain, 2, -1)
    return chunk, nxt, send(nxt[:2], chain, 2, -1), send(prev[2:], chain, 2, 1), prev


MATS = (4, 4, 4, 4, 16, 512)


def gather_steps(chain, chunk, spots, deps):
    chunk = grow(chain, 0, spots[0], three_ways(chain, 0, chunk))
    pieces = three_ways(chain, 1, chunk)
    near = place(chain, 1, spots[1], pieces, [(4, 4, 80, 512)], ((0, 64, 0, (), 0), (128, 16, 0, (), 64)))
    each = tuple((16 * m, 16, 0, (m,), None) for m in range(4))
    mats, vecs = place(
        chain, 2, spots[2], three_ways(chain, 2, near), [MATS, (4, 4, 4, 16, 512)], each + ((64, 16, 1, (), None),), deps
    )
    far = place(chain, 1, spots[1], pieces, [(4, 4, 64, 512)], ((64, 64, 0, (), None),), (mats,))
    return mats.reshape(4, D, 512), vecs, three_ways(chain, 2, far)


def scatter_steps(chain, pieces, spots):
    own, nxt, low, high, prev = pieces
    nxt, prev = add_halves(nxt, prev, send(low, chain, 2, 1), send(high, chain, 2, -1))
    parts = (own, send(nxt, chain, 2, 1), send(prev, chain, 2, -1))
    for phase in (1, 0):
        own, nxt, across, prev = add_split(chain, phase, spots[phase], parts)
        parts = (own, send(nxt, chain, phase, 1), send(prev, chain, phase, -1), send(across, chain, phase, 2))
    return sum(part.astype(jnp.float32) for part in parts)


def regather_steps(chain, chunk, spots):
    for phase in range(2):
        chunk = grow(chain, phase, spots[phase], three_ways(chain, phase, chunk))
    return ring_ways(chain, chunk)


PACKED = ((8, D),) * 4 + ((8, FF), (8, D), (24, D), (32, D)) + ((1, 8),) * 4 + ((1, 32), (1, 8), (1, 8))


def pack_kernel(at_ref, *refs):
    f32, bf16 = jnp.float32, jnp.bfloat16
    count = len(PACKED)
    sources, (blocks_ref, keep_ref, give_ref), held, sems = refs[:count], refs[count : count + 3], refs[count + 3 : -1], refs[-1]
    run_copies([pltpu.make_async_copy(source, place, sems.at[k]) for k, (source, place) in enumerate(zip(sources, held))])
    wq, wk, wv, wr, win, wp, wc, wo, ga, ub, vb, gf, bi, bo, bc = held
    first = at_ref[0] == 0
    where = at_ref[1]

    def spread(ref, size, width):
        row = lax.broadcasted_iota(jnp.int32, (size, width), 0)
        lane = lax.broadcasted_iota(jnp.int32, (size, width), 1)
        hot = (lane == size * where + row).astype(f32).astype(bf16)
        return ndot(ref[...], hot)

    for n, ref in enumerate((wq, wk, wv, wr)):
        left, right = ref[:, :512].astype(f32), ref[:, 512:].astype(f32)
        keep_ref[8 * n : 8 * n + 8, :] = jnp.where(first, left, right).astype(bf16)
        give_ref[8 * n : 8 * n + 8, :] = jnp.where(first, right, left).astype(bf16)
    for n in range(4):
        left, right = (win[:, 2048 * h + 512 * n : 2048 * h + 512 * n + 512].astype(f32) for h in range(2))
        keep_ref[32 + 8 * n : 40 + 8 * n, :] = jnp.where(first, left, right).astype(bf16)
        give_ref[32 + 8 * n : 40 + 8 * n, :] = jnp.where(first, right, left).astype(bf16)
    rows = []
    for ref in (ga, ub, vb, gf):
        wide = spread(ref, 8, D)
        rows += [wide[:, :512], wide[:, 512:]]
    wide = spread(bi, 32, 4 * D)
    halves = [jnp.concatenate([wide[:, 2048 * h + 512 * n : 2048 * h + 512 * n + 512] for n in range(4)], axis=0) for h in range(2)]
    tail = []
    for ref in (bo, bc):
        wide = spread(ref, 8, D)
        tail += [wide[:, :512], wide[:, 512:]]
    keep_ref[64:80, :] = jnp.concatenate(rows + [jnp.where(first, halves[0], halves[1])] + tail, axis=0).astype(bf16)
    give_ref[64:80, :] = jnp.concatenate(rows + [jnp.where(first, halves[1], halves[0])] + tail, axis=0).astype(bf16)
    blocks_ref[0] = wp[...]
    for q in range(3):
        blocks_ref[1 + q] = wc[8 * q : 8 * q + 8, :]
    for q in range(4):
        blocks_ref[4 + q] = wo[8 * q : 8 * q + 8, :]


def pack(at, *arrays):
    return pl.pallas_call(
        pack_kernel,
        in_specs=[SMEM] + [HBM] * len(arrays),
        out_specs=[VMEM] * 3,
        out_shape=[shape_of((8, 8, D), jnp.bfloat16)] + [shape_of((80, 512), jnp.bfloat16)] * 2,
        scratch_shapes=[pltpu.VMEM(shape, jnp.bfloat16) for shape in PACKED] + [pltpu.SemaphoreType.DMA((len(PACKED),))],
        compiler_params=params(60),
        name="pack_weights",
    )(at, *arrays)


def start_kernel(taps_ref, grad_ref, out_ref, stage, sem):
    stage[...] = cdot(taps_ref[...], grad_ref[...]).astype(jnp.bfloat16)
    run_copies([pltpu.make_async_copy(stage, out_ref.at[pl.ds(4096, 1536)], sem)])


def start_buffer(taps, grads):
    return pl.pallas_call(
        start_kernel,
        in_specs=[VMEM, VMEM],
        out_specs=HBM,
        out_shape=shape_of((BUFFER, D), jnp.bfloat16),
        scratch_shapes=[pltpu.VMEM((1536, D), jnp.bfloat16), pltpu.SemaphoreType.DMA],
        compiler_params=params(60),
        name="compression_gradient",
    )(taps, grads)


def normalize(rows):
    centred = rows - jnp.mean(rows, axis=1, keepdims=True)
    inverse = lax.rsqrt(jnp.mean(centred * centred, axis=1, keepdims=True) + EPSILON)
    return centred * inverse, inverse


ROWS = 256


def whole_spec(*shape):
    return pl.BlockSpec(shape, lambda i, c: (0,) * len(shape))


def rows_spec(lanes):
    return pl.BlockSpec((ROWS, lanes), lambda i, c: (i, 0))


def middle_kernel(core_ref, back_ref, got_ref, hidden_ref, gain_ref, gr_ref, proj_ref, hid_ref, branch_ref, att_ref, sum_ref):
    del core_ref
    back = back_ref[...].astype(jnp.float32) + got_ref[...].astype(jnp.float32)
    normed, inverse = normalize(hidden_ref[...])
    total = jnp.sum(back * normed, axis=0, keepdims=True)

    @pl.when(pl.program_id(0) == 0)
    def _():
        sum_ref[...] = total

    @pl.when(pl.program_id(0) > 0)
    def _():
        sum_ref[...] += total

    scaled = back * gain_ref[...]
    along = jnp.mean(scaled * normed, axis=1, keepdims=True)
    grad = gr_ref[...].astype(jnp.float32) + inverse * (
        scaled - jnp.mean(scaled, axis=1, keepdims=True) - normed * along
    )
    hid_ref[...] = grad
    branch = grad.astype(jnp.bfloat16)
    branch_ref[...] = branch
    att_ref[...] = tdot(branch, proj_ref[0]).astype(jnp.bfloat16)


def middle(core, back, got, hidden, gain, grad_res, large):
    return pl.pallas_call(
        middle_kernel,
        grid_spec=pltpu.PrefetchScalarGridSpec(
            num_scalar_prefetch=1,
            grid=(512 // ROWS,),
            in_specs=[
                rows_spec(D), rows_spec(D), rows_spec(D), whole_spec(1, D), rows_spec(D),
                pl.BlockSpec((1, 512, D), lambda i, c: (0, c[0], 0)),
            ],
            out_specs=[rows_spec(D), rows_spec(D), rows_spec(512), whole_spec(1, D)],
        ),
        out_shape=[
            shape_of((512, D)), shape_of((512, D), jnp.bfloat16), shape_of((512, 512), jnp.bfloat16), shape_of((1, D)),
        ],
        compiler_params=params(60),
        name="hidden_gradient",
    )(core, back, got, hidden, gain, grad_res, large)


LATE = ((512, 512), (512, D), (KTOT, D), (3, D, 512), (RELN, D))


def late_kernel(
    at_ref, p_ref, ga_ref, qu_ref, qv_ref, k_ref, v_ref, r_ref, gain_ref, small_ref, *rest
):
    f32, bf16 = jnp.float32, jnp.bfloat16
    count = len(LATE)
    sources, pieces, (gq_out, gk_out, gv_out) = rest[:count], rest[count : count + 5], rest[count + 5 : count + 8]
    ds_s, dw_s, qvr_s, gq_s, both_s, gr_s, sums_s = rest[count + 8 : count + 15]
    att_ref, branch_ref, joined_ref, mats_ref, table_ref = places = rest[count + 15 : -2]
    held, sems = rest[-2:]
    head = pl.program_id(0)

    def loads():
        out = []
        for k, (source, to) in enumerate(zip(sources, places)):
            source = source.at[pl.ds(0, 3)] if k == 3 else source
            out.append(pltpu.make_async_copy(source, to, sems.at[5 + k]))
        return out

    @pl.when(head == 0)
    def _():
        for load in loads():
            load.start()

    flip = (
        lax.broadcasted_iota(jnp.int32, (QB, QB), 0) + lax.broadcasted_iota(jnp.int32, (QB, QB), 1) == QB - 1
    ).astype(f32).astype(bf16)
    du = jnp.zeros((1, HEAD_DIM), f32)
    dv = du
    for b in range(SEG // QB):
        i0, nk, c0 = QB * b, COMP + MEM + QB * (b + 1), SEG - QB - QB * b
        wl = nk + QB
        rows = pl.ds(i0, QB)
        p = p_ref[0, rows, pl.ds(0, nk)].astype(f32)
        dp = tdot(ga_ref[rows, :], v_ref[pl.ds(0, nk), :])
        pd = p * dp
        delta = jnp.sum(pd, axis=1, keepdims=True)
        ds = (pd - p * delta).astype(bf16)
        ds_s[rows, pl.ds(0, nk)] = ds
        if nk < KTOT:
            ds_s[rows, pl.ds(nk, KTOT - nk)] = jnp.zeros((QB, KTOT - nk), bf16)
        wide = jnp.concatenate([ndot(flip, ds), jnp.zeros((QB, QB), f32)], axis=1)
        wide = pltpu.roll(wide, 0, 1, stride=1, stride_axis=0).astype(bf16)
        qvr_s[rows, :] = ndot(flip, qv_ref[rows, :]).astype(bf16)
        dw_s[rows, pl.ds(c0, wl)] = wide
        if c0:
            dw_s[rows, pl.ds(0, c0)] = jnp.zeros((QB, c0), bf16)
        dqu = ndot(ds, k_ref[pl.ds(0, nk), :]) * SCALE
        dqr = ndot(wide, r_ref[pl.ds(c0, wl), :]) * SCALE
        hi = dqr.astype(bf16)
        lo = (dqr - hi.astype(f32)).astype(bf16)
        dqv = ndot(flip, hi) + ndot(flip, lo)
        du += jnp.sum(dqu, axis=0, keepdims=True)
        dv += jnp.sum(dqv, axis=0, keepdims=True)
        gq_out[rows, :] = (dqu + dqv).astype(bf16)
    lanes = pl.ds(pl.multiple_of(HEAD_DIM * head, HEAD_DIM), HEAD_DIM)
    above = pl.ds(pl.multiple_of(512 + HEAD_DIM * head, HEAD_DIM), HEAD_DIM)
    sums_s[0:1, lanes] = du
    sums_s[1:2, lanes] = dv
    gq_s[:, lanes] = gq_out[...]
    grad = (cdot(ds_s[...], qu_ref[...]) * SCALE).astype(bf16)
    both_s[:, lanes] = grad
    gk_out[...] = grad[COMP + MEM :]
    grad = cdot(p_ref[0], ga_ref[...]).astype(bf16)
    both_s[:, above] = grad
    gv_out[...] = grad[COMP + MEM :]
    gr_s[:, lanes] = (cdot(dw_s[...], qvr_s[...]) * SCALE).astype(bf16)

    @pl.when(head == 3)
    def _():
        for load in loads():
            load.wait()
        proj = cdot(att_ref[...], branch_ref[...]).astype(bf16).reshape(4, 4, 4, 8, D)
        for h in range(2):
            held[:, :, :, 64 + 8 * h : 72 + 8 * h, :] = proj[..., 512 * h : 512 * h + 512]
        ones = jnp.ones((8, 512), bf16)

        def keep(m, grad):
            low = grad.astype(bf16)
            for h in range(2):
                held[m, :, :, 32 * h : 32 * h + 32, :] = low[512 * h : 512 * h + 512].reshape(4, 4, 32, 512)
            if m == 3:
                return jnp.zeros((8, D), f32)
            product = grad * mats_ref[m].astype(f32)
            high = product.astype(bf16)
            return tdot(ones, high) + tdot(ones, (product - high.astype(f32)).astype(bf16))

        keep(3, cdot(table_ref[...], gr_s[...]))
        total = keep(0, cdot(joined_ref[pl.ds(COMP + MEM, SEG), :], gq_s[...]))
        pair = cdot(joined_ref[...], both_s[...])
        total += keep(1, pair[:, :512])
        total += keep(2, pair[:, 512:])
        total = total[:1] / gain_ref[...]
        extra = jnp.concatenate([total[:, :512], total[:, 512:], sums_s[0:2, :], small_ref[4:, :]], axis=0)
        held[:, :, :, 80:, :] = jnp.zeros((4, 4, 4, 8, 512), bf16)
        held[0, 0, 0, 80:, :] = extra.astype(bf16)
        send_pieces("AB", 2, RING, at_ref, held, pieces, sems)


def late_gradients(at, probs, grad_att, query_u, query_v, keys, values, rel, gain, small, *arrays):
    f32, bf16 = jnp.float32, jnp.bfloat16
    col = lambda n: pl.BlockSpec((n, HEAD_DIM), lambda h: (0, h))
    const = lambda *shape: pl.BlockSpec(shape, lambda h: (0, 0))
    return pl.pallas_call(
        late_kernel,
        grid=(4,),
        in_specs=[
            SMEM, pl.BlockSpec((1, SEG, KTOT), lambda h: (h, 0, 0)),
            col(SEG), col(SEG), col(SEG), col(KTOT), col(KTOT), col(RELN), const(1, D), const(8, 512),
        ] + [HBM] * len(LATE),
        out_specs=[ANY] * 5 + [col(SEG)] * 3,
        out_shape=[shape_of((4 if part is None else 2, 4, 88, 512), bf16) for _, part in RING]
        + [shape_of((SEG, 512), bf16)] * 3,
        scratch_shapes=[
            pltpu.VMEM((SEG, KTOT), bf16),
            pltpu.VMEM((SEG, RELN), bf16),
            pltpu.VMEM((SEG, HEAD_DIM), bf16),
            pltpu.VMEM((SEG, 512), bf16),
            pltpu.VMEM((KTOT, D), bf16),
            pltpu.VMEM((RELN, 512), bf16),
            pltpu.VMEM((8, 512), f32),
        ]
        + [pltpu.VMEM(shape, bf16) for shape in LATE]
        + [pltpu.VMEM((4, 4, 4, 88, 512), bf16), pltpu.SemaphoreType.DMA((5 + len(LATE),))],
        compiler_params=params(60),
        cost_estimate=pl.CostEstimate(flops=20 << 30, bytes_accessed=30 << 20, transcendentals=0),
        name="attention_backward",
    )(at, probs, grad_att, query_u, query_v, keys, values, rel, gain, small, *arrays)


def ffn_kernel(at_ref, att_ref, got_ref, proj_ref, seg_ref, gain_ref, gr_ref, *rest):
    pieces, quarters, bias_ref, out_ref, back_ref, part_ref, hidden_ref = rest[:4], rest[4:8], rest[8], *rest[10:14]
    panels, act_ref, turned_ref, natural, stage_in, stage_out, sums, back_sum, part_sum, arrived, sems = rest[14:]
    p = pl.program_id(0)
    slot = lax.rem(p, 2)

    def panel_copies(core, m):
        rows = pl.ds(16 * m if isinstance(m, int) else pl.multiple_of(16 * m, 16), 16)
        return [
            pltpu.make_async_copy(
                piece.at[:, :, rows], panels.at[(m,) + spot_of("AB", core, 2, at_ref[k], part)], arrived.at[4 * m + j]
            )
            for j, ((k, part), piece) in enumerate(zip(DIRECT, pieces))
        ]

    for core in range(2):
        @pl.when((p == 0) & (at_ref[4] == core))
        def _():
            for m in range(4):
                for copy in panel_copies(core, m):
                    copy.start()

    @pl.when(p == 0)
    def _():
        core = at_ref[4]
        mine = proj_ref[0, pl.ds(pl.multiple_of(512 * core, 512), 512), :]
        other = proj_ref[0, pl.ds(pl.multiple_of(512 - 512 * core, 512), 512), :]
        hidden = seg_ref[...].astype(jnp.float32) + ndot(att_ref[...], mine) + ndot(got_ref[...], other)
        hidden_ref[...] = hidden
        act = (normalize(hidden)[0] * gain_ref[...]).astype(jnp.bfloat16)
        act_ref[...] = act
        turned_ref[...] = act.T

    for core in range(2):
        @pl.when(at_ref[4] == core)
        def _():
            for copy in panel_copies(core, p):
                copy.wait()

    def sending(step, buffer):
        rows = pl.ds(pl.multiple_of(1024 * (step // 2), 1024), 1024)
        lanes = pl.ds(pl.multiple_of(512 * lax.rem(step, 2), 512), 512)
        below = pl.ds(pl.multiple_of(2048 + 512 * step, 512), 512)
        return [
            pltpu.make_async_copy(stage_in.at[buffer], out_ref.at[rows, lanes], sems.at[buffer]),
            pltpu.make_async_copy(stage_out.at[buffer], out_ref.at[below], sems.at[2 + buffer]),
        ]

    @pl.when(p >= 2)
    def _():
        for copy in sending(p - 2, slot):
            copy.wait()

    act, grad, w_one = act_ref[...], gr_ref[...], panels[p].reshape(D, 512)
    for q in range(4):
        for shard in range(16):
            natural[32 * shard + 8 * q : 32 * shard + 8 * q + 8, :] = quarters[q][0, 8 * shard : 8 * shard + 8, :]
    w_two = natural[...]
    pre = ndot(act, w_one) + bias_ref[0]
    inner = math.sqrt(2.0 / math.pi)
    square = pre * pre
    tanh = jnp.tanh(inner * pre * (1.0 + 0.044715 * square))
    act_low = (0.5 * pre * (1.0 + tanh)).astype(jnp.bfloat16)
    slope = 0.5 * (1.0 + tanh) + (0.5 * inner) * pre * (1.0 - tanh * tanh) * (1.0 + (3.0 * 0.044715) * square)
    grad_act = tdot(grad, w_two)
    grad_pre = (grad_act * slope).astype(jnp.bfloat16)
    stage_in[slot] = ndot(turned_ref[...], grad_pre).astype(jnp.bfloat16)
    stage_out[slot] = cdot(act_low, grad).astype(jnp.bfloat16)
    for copy in sending(p, slot):
        copy.start()
    total = jnp.sum(grad_pre.astype(jnp.float32), axis=0, keepdims=True)
    total = jnp.concatenate([total, total], axis=1)
    row = lax.broadcasted_iota(jnp.int32, (16, D), 0)
    lane = lax.broadcasted_iota(jnp.int32, (16, D), 1)
    mine = (row == p // 2) & (lane // 512 == lax.rem(p, 2))

    @pl.when(p == 0)
    def _():
        sums[...] = jnp.zeros_like(sums)
        back_sum[...] = tdot(grad_pre, w_one)
        part_sum[...] = ndot(act_low, w_two)

    @pl.when((p > 0) & (p < 3))
    def _():
        back_sum[...] += tdot(grad_pre, w_one)
        part_sum[...] += ndot(act_low, w_two)

    @pl.when(p == 3)
    def _():
        back_ref[...] = (back_sum[...] + tdot(grad_pre, w_one)).astype(jnp.bfloat16)
        part_ref[...] = (part_sum[...] + ndot(act_low, w_two)).astype(jnp.bfloat16)

    sums[...] = jnp.where(mine, total, sums[...].astype(jnp.float32)).astype(jnp.bfloat16)

    @pl.when(p == 3)
    def _():
        last = pltpu.make_async_copy(sums, out_ref.at[pl.ds(5632, 16)], sems.at[4])
        last.start()
        for copy in sending(p - 1, 1 - slot) + sending(p, slot):
            copy.wait()
        last.wait()


def ffn(at, att, got, seg, gain, grad, pieces, large, bias, buffer):
    f32, bf16 = jnp.float32, jnp.bfloat16
    whole = pl.BlockSpec((512, D), lambda p, c: (0, 0))
    quarter = lambda q: pl.BlockSpec((1, 128, D), lambda p, c: (4 + q, 4 * c[4] + p, 0))
    return pl.pallas_call(
        ffn_kernel,
        grid_spec=pltpu.PrefetchScalarGridSpec(
            num_scalar_prefetch=1,
            grid=(4,),
            in_specs=[
                whole_spec(512, 512),
                whole_spec(512, 512),
                whole_spec(1, D, D),
                whole,
                whole_spec(1, D),
                whole,
                *([ANY] * 4),
                *(quarter(q) for q in range(4)),
                pl.BlockSpec((1, 1, 512), lambda p, c: (p, 0, 0)),
                HBM,
            ],
            out_specs=[HBM, whole, whole, whole],
            scratch_shapes=[
                pltpu.VMEM(MATS, bf16),
                pltpu.VMEM((512, D), bf16),
                pltpu.VMEM((D, 512), bf16),
                pltpu.VMEM((512, D), bf16),
                pltpu.VMEM((2, D, 512), bf16),
                pltpu.VMEM((2, 512, D), bf16),
                pltpu.VMEM((16, D), bf16),
                pltpu.VMEM((512, D), f32),
                pltpu.VMEM((512, D), f32),
                pltpu.SemaphoreType.DMA((16,)),
                pltpu.SemaphoreType.DMA((5,)),
            ],
        ),
        out_shape=[shape_of((BUFFER, D), bf16), shape_of((512, D), bf16), shape_of((512, D), bf16), shape_of((512, D))],
        input_output_aliases={16: 0},
        compiler_params=params(60),
        cost_estimate=pl.CostEstimate(flops=12 * 512 * 1024 * 2048, bytes_accessed=24 << 20, transcendentals=512 * 2048),
        name="feed_forward",
    )(at, att, got, large, seg, gain, grad, *pieces, large, large, large, large, bias, buffer)


STEP = 128
SLOTS = 8


def widen_kernel(core_ref, second, deps, *refs):
    core = core_ref[0]
    source, outs = refs[0], refs[1 + deps : -4]
    low, high, loads, stores = refs[-4:]
    jobs = []
    if second:
        for q in range(2):
            for r in range(512 // STEP):
                rows = pl.ds(512 * q + STEP * r, STEP)
                lanes = pl.ds(pl.multiple_of(D * (2 * (1 - core) + q), D), D)
                jobs.append((rows, outs[0].at[pl.ds(STEP * r, STEP), lanes]))
    else:
        for r in range(2048 // STEP):
            jobs.append((pl.ds(2048 + STEP * r, STEP), outs[1].at[pl.ds(STEP * r, STEP)]))
        for r in range(1536 // STEP):
            jobs.append((pl.ds(4096 + STEP * r, STEP), outs[2].at[pl.ds(STEP * r, STEP)]))
        for q in range(2):
            for r in range(512 // STEP):
                rows = pl.ds(pl.multiple_of(D * q + 512 * core + STEP * r, STEP), STEP)
                lanes = pl.ds(pl.multiple_of(D * (2 * core + q), D), D)
                jobs.append((rows, outs[0].at[pl.ds(STEP * r, STEP), lanes]))

    def load(k):
        return pltpu.make_async_copy(source.at[jobs[k][0]], low.at[k % SLOTS], loads.at[k % SLOTS])

    def store(k):
        return pltpu.make_async_copy(high.at[k % SLOTS], jobs[k][1], stores.at[k % SLOTS])

    for k in range(SLOTS):
        load(k).start()
    for k in range(len(jobs)):
        load(k).wait()
        if k >= SLOTS:
            store(k - SLOTS).wait()
        high[k % SLOTS] = low[k % SLOTS].astype(jnp.float32)
        store(k).start()
        if k + SLOTS < len(jobs):
            load(k + SLOTS).start()
    for k in range(len(jobs) - SLOTS, len(jobs)):
        store(k).wait()
    if not second:
        run_copies([pltpu.make_async_copy(source.at[pl.ds(5632, 16)], low.at[0, pl.ds(0, 16)], loads.at[0])])
        high[0, :16, :] = low[0, :16, :].astype(jnp.float32)
        run_copies([pltpu.make_async_copy(high.at[0, pl.ds(0, 16)], outs[3], stores.at[0])])


def widen(core, source, deps, into=None):
    shapes = [(512, FF)] if into is not None else [(512, FF), (2048, D), (1536, D), (16, D)]
    deps = tuple(deps) + (() if into is None else (into,))

    def body(core_ref, *refs):
        widen_kernel(core_ref, into is not None, len(deps), *refs)

    return pl.pallas_call(
        body,
        in_specs=[SMEM, HBM] + [ANY] * len(deps),
        out_specs=[HBM] * len(shapes),
        out_shape=[shape_of(shape) for shape in shapes],
        input_output_aliases={} if into is None else {1 + len(deps): 0},
        scratch_shapes=[
            pltpu.VMEM((SLOTS, STEP, D), jnp.bfloat16),
            pltpu.VMEM((SLOTS, STEP, D), jnp.float32),
            pltpu.SemaphoreType.DMA((SLOTS,)),
            pltpu.SemaphoreType.DMA((SLOTS,)),
        ],
        compiler_params=params(60),
        name="widen_gradients",
    )(core, source, *deps)


def pick_kernel(core_ref, source_ref, *rest):
    del core_ref
    rest[-1][...] = source_ref[...]


def pick_halves(core, buffer, deps):
    return pl.pallas_call(
        pick_kernel,
        grid_spec=pltpu.PrefetchScalarGridSpec(
            num_scalar_prefetch=1,
            grid=(2,),
            in_specs=[pl.BlockSpec((512, D), lambda q, c: (2 * q + 1 - c[0], 0))] + [ANY] * len(deps),
            out_specs=pl.BlockSpec((512, D), lambda q, c: (q, 0)),
        ),
        out_shape=shape_of((D, D), jnp.bfloat16),
        compiler_params=params(60),
        name="other_half",
    )(core, buffer, *deps)


def on_device(
    segment, memory, compressed, mem_count, comp_count, attn_gain, w_query, w_key, w_value, u_bias, v_bias,
    w_rel, w_proj, ffn_gain, w_in, b_in, w_out, b_out, w_comp, b_comp, out_grad, comp_grad,
):
    f32, bf16 = jnp.float32, jnp.bfloat16
    core, chip = lax.axis_index("blk"), lax.axis_index("dp")
    first = core == 0
    core_at = core.reshape(1).astype(jnp.int32)
    coords = {"y": chip // 16, "z": (chip // 4) % 4, "x": chip % 4}
    spots = {}
    for chain in ("AB",):
        spots[chain] = []
        for phase in range(3):
            at = jnp.where(first, coords[PATHS[chain[0]][phase]], coords[PATHS[chain[1]][phase]])
            spots[chain].append(jnp.stack([(at + k) % 4 for k in range(4)] + [core]).astype(jnp.int32))

    def both(own, other, axis=0):
        return jnp.where(first, jnp.concatenate([own, other], axis), jnp.concatenate([other, own], axis))

    def half(array, which, axis):
        size = array.shape[axis] // 2
        return lax.dynamic_slice_in_dim(array, which * size, size, axis)

    where_at = jnp.stack([core, 2 * chip + core]).astype(jnp.int32)
    row = lambda vector: vector.reshape(1, -1)
    blocks, keep, give = pack(
        where_at, w_query, w_key, w_value, w_rel, w_in, w_proj, w_comp, w_out,
        row(attn_gain), row(u_bias), row(v_bias), row(ffn_gain), row(b_in), row(b_out), row(b_comp),
    )
    large = lax.all_gather(blocks, ALL_AXES, axis=1, tiled=True)
    got = swap(give)
    chunk = jnp.concatenate(
        [both(keep[8 * n : 8 * n + 8], got[8 * n : 8 * n + 8]) for n in range(8)] + [keep[64:] + got[64:]]
    )

    pieces = [both(array[0], swap(array[0])) for array in (compressed, memory, segment, out_grad, comp_grad)]
    seg_at = COMP + MEM
    grad_res, comp_flat = pieces[3], pieces[4]
    all_rows = jnp.concatenate(pieces[:3])

    def centre(rows):
        mean = jnp.mean(rows, axis=-1, keepdims=True)
        centred = rows - mean
        return mean, lax.rsqrt(jnp.mean(centred * centred, axis=-1, keepdims=True) + EPSILON)

    mean_one, inverse_one = centre(all_rows.astype(f32))

    distance = (KTOT - 1) - jnp.arange(RELN, dtype=f32)
    frequency = jnp.exp(jnp.arange(D // 2, dtype=f32) * (-2.0 * math.log(10000.0) / D))
    coarse = distance[::32, None] * frequency[None, :]
    fine = jnp.arange(32, dtype=f32)[:, None] * frequency[None, :]
    sin_a, cos_a = (trig(coarse)[:, None, :] for trig in (jnp.sin, jnp.cos))
    sin_b, cos_b = (trig(fine)[None, :, :] for trig in (jnp.sin, jnp.cos))
    sines, cosines = sin_a * cos_b - cos_a * sin_b, cos_a * cos_b + sin_a * sin_b
    table = jnp.concatenate([sines.reshape(RELN, 512), cosines.reshape(RELN, 512)], axis=1)
    table = jnp.where(distance[:, None] >= 0.0, table, 0.0).astype(bf16)

    slot = jnp.arange(MEM, dtype=jnp.int32)
    masked = jnp.where((slot >= MEM - mem_count[0])[:, None], pieces[1], jnp.zeros_like(pieces[1]))
    windows = masked.reshape(MEM // RATE, RATE * D)
    buffer = start_buffer(half(windows, core, 1), comp_flat)

    mats, vecs, panels = gather_steps("AB", chunk, spots["AB"], (mean_one, inverse_one, all_rows, table, buffer))
    vecs = jnp.sum(vecs.astype(f32), axis=(0, 1, 2))
    gain_one, gain_two = vecs[:2].reshape(1, D), vecs[6:8].reshape(1, D)
    bias_u = jnp.where(first, vecs[2], vecs[3])
    bias_v = jnp.where(first, vecs[4], vecs[5])
    joined = ((all_rows.astype(f32) - mean_one) * inverse_one * gain_one).astype(bf16)
    query_rows = ndot(joined[seg_at:], mats[0])
    key_rows = ndot(joined, mats[1]).astype(bf16)
    value_rows = ndot(joined, mats[2]).astype(bf16)
    rel_rows = ndot(table, mats[3]).astype(bf16)
    query_u = (query_rows + bias_u).astype(bf16)
    query_v = (query_rows + bias_v).astype(bf16)
    counts = jnp.concatenate([mem_count, comp_count])
    attended, probs = attn_fwd(counts, query_u, query_v, key_rows, value_rows, rel_rows)

    ffn_bias = vecs[8:12].reshape(4, 1, 512)
    out_bias, comp_bias = vecs[12:14].reshape(1, D), vecs[14:16].reshape(1, D)
    buffer, back, partial, hidden = ffn(
        spots["AB"][2], attended, swap(attended), pieces[2], gain_two, grad_res, panels, large, ffn_bias, buffer
    )
    buffer = lax.psum(buffer, "dp")
    grad_hidden, grad_branch, grad_att, d_gain_two = middle(
        core_at, back, swap(back), hidden, gain_two, grad_res, large
    )

    d_b_out = jnp.sum(half(grad_res, core, 1).astype(f32), axis=0, keepdims=True)
    d_b_comp = jnp.sum(half(comp_flat, core, 1).astype(f32), axis=0, keepdims=True)
    small = jnp.concatenate(
        [jnp.zeros((4, 512), f32), half(d_gain_two, core, 1), d_b_out, d_b_comp, jnp.zeros((1, 512), f32)]
    )
    *pieces_late, grad_query, grad_keys, grad_values = late_gradients(
        spots["AB"][2], probs, grad_att, query_u, query_v, key_rows, value_rows, rel_rows, gain_one, small,
        attended, grad_branch, joined, mats, table,
    )
    share = scatter_steps("AB", pieces_late, spots["AB"])
    keep = half(share[:64], core, 0).astype(bf16)
    mail = swap(jnp.concatenate([half(share[:64], 1 - core, 0), share[80:]]).astype(bf16))
    gains = jnp.where(jnp.arange(8)[:, None] < 2, share[80:] + mail[32:].astype(f32), share[80:])
    late = jnp.concatenate([both(keep, mail[:32]), share[64:80].astype(bf16), gains.astype(bf16)])
    received = regather_steps("AB", late, spots["AB"])

    partial_sum = half(partial, core, 0).astype(f32) + swap(half(partial, 1 - core, 0)).astype(f32)
    result = half(hidden, core, 0) + partial_sum + out_bias
    output = result.astype(bf16)

    comp_proj = large[1:4].reshape(3, 128, 8, D).transpose(1, 0, 2, 3).reshape(RATE * D, D)
    new_compressed = (ndot(half(windows, core, 0), comp_proj) + comp_bias).astype(bf16)

    grad_seg = (
        tdot(grad_query, mats[0]) + tdot(grad_keys, mats[1]) + tdot(grad_values, mats[2])
    )
    grad_seg = half(grad_seg, core, 0) + swap(half(grad_seg, 1 - core, 0))
    scaled_one = grad_seg * gain_one
    own_segment = segment[0].astype(f32)
    mean_seg, inverse_seg = centre(own_segment)
    normed_seg = (own_segment - mean_seg) * inverse_seg
    d_segment = half(grad_hidden, core, 0) + inverse_seg * (
        scaled_one
        - jnp.mean(scaled_one, axis=-1, keepdims=True)
        - normed_seg * jnp.mean(scaled_one * normed_seg, axis=-1, keepdims=True)
    )

    deps = (received[1], received[4], output, new_compressed, d_segment)
    others = pick_halves(core_at, buffer, deps)
    d_in, d_out, d_comp, sums = widen(core_at, buffer, deps + (others,))
    *late, d_proj, extra = finish("AB", spots["AB"][2], received, d_out)
    (d_in,) = widen(core_at, swap(others), (late[0],), d_in)
    d_b_in = sums[:2].reshape(2048)
    return (
        output[None],
        new_compressed[None],
        d_segment[None],
        jnp.where(first, extra[0], extra[1]),
        late[0],
        late[1],
        late[2],
        extra[2],
        extra[3],
        late[3],
        d_proj,
        extra[4],
        d_in,
        d_b_in,
        d_out,
        extra[5],
        d_comp,
        extra[6],
    )


def solution(mesh):
    rows, weight, vector = P("dp", "blk", None), P(("dp", "blk"), None), P(("dp", "blk"))
    placed = (
        rows, rows, rows, P("dp"), P("dp"), vector, weight, weight, weight, vector, vector,
        weight, weight, vector, weight, vector, weight, vector, weight, vector, rows, rows,
    )
    half_one, half_two = P("blk"), P("blk", None)
    return jax.shard_map(
        on_device,
        mesh=mesh,
        in_specs=placed,
        out_specs=(
            rows, rows, rows, half_one, half_two, half_two, half_two, half_one, half_one,
            half_two, half_two, half_one, half_two, half_one, half_two, half_one, half_two, half_one,
        ),
        check_vma=False,
    )
```

```python
import math, functools
import jax, jax.numpy as jnp
from jax import lax
from jax.sharding import PartitionSpec as P
from jax.experimental import pallas as pl
from jax.experimental.pallas import tpu as pltpu
D=1024
FF=4096
HEAD_DIM=128
SEG=512
MEM=384
COMP=512
RATE=3
KTOT=1408
RELN=1536
QB=128
EPSILON=1e-05
SCALE=1.0/math.sqrt(HEAD_DIM); NEG=-1e30
def tdot(a,b):
    return lax.dot_general(a,b,(((1,),(1,)),((),())),preferred_element_type=jnp.float32)
def ndot(a,b):
    return lax.dot_general(a,b,(((1,),(0,)),((),())),preferred_element_type=jnp.float32)
def cdot(a,b):
    return lax.dot_general(a,b,(((0,),(0,)),((),())),preferred_element_type=jnp.float32)

def attn_fwd_kernel(cnt_ref, qu_ref, qv_ref, k_ref, v_ref, r_ref, att_ref, p_ref):
    mc = cnt_ref[0]; cc = cnt_ref[1]
    kp = lax.broadcasted_iota(jnp.int32,(1,COMP+MEM),1)
    ok = ((kp < COMP) & (kp >= COMP-cc)) | ((kp>=COMP)&(kp>=COMP+MEM-mc))
    old_bias = jnp.where(ok, 0.0, NEG)
    tri = jnp.where(lax.broadcasted_iota(jnp.int32,(QB,QB),1) <= lax.broadcasted_iota(jnp.int32,(QB,QB),0), 0.0, NEG)
    for b in range(SEG//QB):
        i0=QB*b; nk=COMP+MEM+QB*(b+1); c0=SEG-QB-QB*b; wl=nk+QB
        s = tdot(qu_ref[pl.ds(i0,QB),:], k_ref[pl.ds(0,nk),:])
        w = tdot(qv_ref[pl.ds(i0,QB),:], r_ref[pl.ds(c0,wl),:])
        w = pltpu.roll(w, wl-(QB-1), 1, stride=1, stride_axis=0)[:,:nk]
        s = (s+w)*SCALE
        parts=[s[:,:COMP+MEM]+old_bias]
        if b: parts.append(s[:,COMP+MEM:nk-QB])
        parts.append(s[:,nk-QB:]+tri)
        s=jnp.concatenate(parts,axis=1)
        m=jnp.max(s,axis=1,keepdims=True)
        e=jnp.exp(s-m)
        l=jnp.sum(e,axis=1,keepdims=True)
        p=(e*(1.0/l)).astype(jnp.bfloat16)
        p_ref[0,pl.ds(i0,QB),pl.ds(0,nk)]=p
        if nk<KTOT: p_ref[0,pl.ds(i0,QB),pl.ds(nk,KTOT-nk)]=jnp.zeros((QB,KTOT-nk),jnp.bfloat16)
        att_ref[pl.ds(i0,QB),:]=ndot(p,v_ref[pl.ds(0,nk),:]).astype(jnp.bfloat16)

def attn_fwd(cnt,qu,qv,k,v,r):
    nh=qu.shape[1]//HEAD_DIM
    col=lambda n: pl.BlockSpec((n,HEAD_DIM),lambda h:(0,h))
    return pl.pallas_call(attn_fwd_kernel, grid=(nh,),
        in_specs=[pl.BlockSpec(memory_space=pltpu.SMEM),col(SEG),col(SEG),col(KTOT),col(KTOT),col(RELN)],
        out_specs=[col(SEG),pl.BlockSpec((1,SEG,KTOT),lambda h:(h,0,0))],
        out_shape=[jax.ShapeDtypeStruct((SEG,nh*HEAD_DIM),jnp.bfloat16),jax.ShapeDtypeStruct((nh,SEG,KTOT),jnp.bfloat16)],
        compiler_params=pltpu.CompilerParams(vmem_limit_bytes=40<<20),
        cost_estimate=pl.CostEstimate(flops=6*nh*SEG*KTOT*HEAD_DIM,bytes_accessed=12<<20,transcendentals=nh*SEG*KTOT),
        name="attention_forward")(cnt,qu,qv,k,v,r)


PATHS = {"A": ("x", "z", "y"), "B": ("y", "x", "z"), "C": ("z", "y", "x")}
SPOT = {
    name: tuple(sorted(path[: phase + 1], key="yzx".index).index(path[phase]) for phase in range(3))
    for name, path in PATHS.items()
}
STRIDE = {"y": 16, "z": 4, "x": 1}
ALL_AXES = ("dp", "blk")
BUFFER = 5648
ANY = pl.BlockSpec(memory_space=pl.ANY)
SMEM = pl.BlockSpec(memory_space=pltpu.SMEM)
VMEM = pl.BlockSpec(memory_space=pltpu.VMEM)
HBM = pl.BlockSpec(memory_space=pltpu.HBM)


def params(mib=40):
    return pltpu.CompilerParams(vmem_limit_bytes=mib << 20)


def shape_of(shape, dtype=jnp.float32):
    return jax.ShapeDtypeStruct(shape, dtype)


def swap(array):
    return lax.ppermute(array, "blk", [(0, 1), (1, 0)])


def step_pairs(chain, phase, delta):
    pairs = []
    for chip in range(64):
        for core in range(2):
            stride = STRIDE[PATHS[chain[core]][phase]]
            at = (chip // stride) % 4
            pairs.append((2 * chip + core, 2 * (chip + ((at + delta) % 4 - at) * stride) + core))
    return pairs


def send(array, chain, phase, delta):
    return lax.ppermute(array, ALL_AXES, step_pairs(chain, phase, delta))


def run_copies(copies):
    for copy in copies:
        copy.start()
    for copy in copies:
        copy.wait()


def spot_of(chain, core, phase, index, part=None):
    where = [slice(None)] * phase
    if part is not None:
        where[0] = pl.ds(2 * part, 2)
    where.insert(SPOT[chain[core]][phase], index)
    return tuple(where)


DIRECT = ((0, None), (1, None), (2, None), (3, None))
RING = ((0, None), (1, None), (2, 0), (2, 1), (3, None))


def place_kernel(chain, phase, moves, deps, ways, at_ref, *rest):
    pieces, outs, sems = rest[: len(ways)], rest[len(ways) + deps : -1], rest[-1]
    lead = (slice(None),) * phase
    for core in range(2):
        @pl.when(at_ref[4] == core)
        def _():
            copies = []
            for j, ((k, part), piece) in enumerate(zip(ways, pieces)):
                where = spot_of(chain, core, phase, at_ref[k], part)
                for n, (start, size, out, head, to) in enumerate(moves):
                    source = piece.at[lead + (pl.ds(start, size),)]
                    target = outs[out].at[head + where]
                    if to is not None:
                        target = target.at[lead + (pl.ds(to, size),)]
                    copies.append(pltpu.make_async_copy(source, target, sems.at[j * len(moves) + n]))
            run_copies(copies)


def place(chain, phase, at, pieces, shapes, moves, deps=(), mib=32):
    ways = RING if len(pieces) == 5 else DIRECT
    out = pl.pallas_call(
        functools.partial(place_kernel, chain, phase, moves, len(deps), ways),
        in_specs=[SMEM] + [ANY] * (len(ways) + len(deps)),
        out_specs=[VMEM] * len(shapes),
        out_shape=[shape_of(shape, jnp.bfloat16) for shape in shapes],
        scratch_shapes=[pltpu.SemaphoreType.DMA((len(ways) * len(moves),))],
        compiler_params=params(mib),
        name="place_pieces",
    )(at, *pieces, *deps)
    return out if len(shapes) > 1 else out[0]


def grow(chain, phase, at, pieces):
    rows, lanes = pieces[0].shape[-2:]
    return place(chain, phase, at, pieces, [(4,) * (phase + 1) + (rows, lanes)], ((0, rows, 0, (), None),))


def send_pieces(chain, phase, ways, at_ref, held, pieces, sems):
    for core in range(2):
        @pl.when(at_ref[4] == core)
        def _():
            copies = []
            for j, ((k, part), piece) in enumerate(zip(ways, pieces)):
                where = spot_of(chain, core, phase, at_ref[k], part)
                copies.append(pltpu.make_async_copy(held.at[where], piece, sems.at[j]))
            run_copies(copies)


def split_kernel(chain, phase, count, at_ref, *rest):
    parts, pieces, held, sems = rest[:count], rest[count : count + 4], rest[-2], rest[-1]
    held[...] = sum(ref[...].astype(jnp.float32) for ref in parts).astype(jnp.bfloat16)
    send_pieces(chain, phase, DIRECT, at_ref, held, pieces, sems)


def add_split(chain, phase, at, parts):
    shape = parts[0].shape
    return pl.pallas_call(
        functools.partial(split_kernel, chain, phase, len(parts)),
        in_specs=[SMEM] + [VMEM] * len(parts),
        out_specs=[ANY] * 4,
        out_shape=[shape_of(shape[1:], jnp.bfloat16)] * 4,
        scratch_shapes=[pltpu.VMEM(shape, jnp.bfloat16), pltpu.SemaphoreType.DMA((4,))],
        compiler_params=params(32),
        name="add_pieces",
    )(at, *parts)


def halves_kernel(next_ref, prev_ref, low_ref, high_ref, next_out, prev_out):
    f32, bf16 = jnp.float32, jnp.bfloat16
    next_out[:2] = (next_ref[:2].astype(f32) + low_ref[...].astype(f32)).astype(bf16)
    next_out[2:] = next_ref[2:]
    prev_out[:2] = prev_ref[:2]
    prev_out[2:] = (prev_ref[2:].astype(f32) + high_ref[...].astype(f32)).astype(bf16)


def add_halves(*arrays):
    return pl.pallas_call(
        halves_kernel,
        in_specs=[VMEM] * 4,
        out_specs=[VMEM] * 2,
        out_shape=[shape_of(arrays[0].shape, jnp.bfloat16)] * 2,
        compiler_params=params(32),
        name="add_halves",
    )(*arrays)


def finish_kernel(chain, at_ref, *rest):
    received, (*outs, proj_ref, o1, o2, o3, o4, o5, o6, held, sems) = rest[:5], rest[6:]
    for core in range(2):
        @pl.when(at_ref[4] == core)
        def _():
            copies = []
            for j, ((k, part), piece) in enumerate(zip(RING, received)):
                where = spot_of(chain, core, 2, at_ref[k], part)
                copies.append(pltpu.make_async_copy(piece, held.at[where], sems.at[j]))
            run_copies(copies)
    extra = held[0, 0, 0, 80:, :].astype(jnp.float32)
    rows = [jnp.where(at_ref[4] == 0, extra[0:1], extra[1:2])] + [extra[k : k + 1] for k in range(2, 7)]
    for ref, row in zip((o1, o2, o3, o4, o5, o6), rows):
        for t in range(4):
            ref[t : t + 1, :] = row[:, 128 * t : 128 * t + 128]
    for chip in range(64):
        y, z, x = chip // 16, (chip // 4) % 4, chip % 4
        for h in range(2):
            block = held[y, z, x, 32 * h : 32 * h + 32, :].astype(jnp.float32)
            outs[y][pl.ds(32 * (chip % 16), 32), pl.ds(512 * h, 512)] = block
            block = held[y, z, x, 64 + 8 * h : 72 + 8 * h, :].astype(jnp.float32)
            proj_ref[pl.ds(8 * chip, 8), pl.ds(512 * h, 512)] = block


def finish(chain, at, pieces, after):
    return pl.pallas_call(
        functools.partial(finish_kernel, chain),
        in_specs=[SMEM] + [ANY] * 6,
        out_specs=[VMEM] * 11,
        out_shape=[shape_of((512, D))] * 5 + [shape_of((4, 128))] * 6,
        scratch_shapes=[pltpu.VMEM((4, 4, 4, 88, 512), jnp.bfloat16), pltpu.SemaphoreType.DMA((5,))],
        compiler_params=params(60),
        name="finish_gradients",
    )(at, *pieces, after)


def three_ways(chain, phase, chunk):
    prev, nxt, across = send(chunk, chain, phase, 1), send(chunk, chain, phase, -1), send(chunk, chain, phase, 2)
    return chunk, nxt, across, prev


def ring_ways(chain, chunk):
    prev, nxt = send(chunk, chain, 2, 1), send(chunk, chain, 2, -1)
    low, high = nxt[:2], prev[2:]
    return (chunk, nxt, send(low, chain, 2, -1), send(high, chain, 2, 1), prev), (low, high)


MATS = (4, 4, 4, 4, 16, 512)


def gather_steps(chain, chunk, spots, deps):
    chunk = grow(chain, 0, spots[0], three_ways(chain, 0, chunk))
    pieces = three_ways(chain, 1, chunk)
    near = place(chain, 1, spots[1], pieces, [(4, 4, 80, 512)], ((0, 64, 0, (), 0), (128, 16, 0, (), 64)))
    each = tuple((16 * m, 16, 0, (m,), None) for m in range(4))
    mats, vecs = place(
        chain, 2, spots[2], three_ways(chain, 2, near), [MATS, (4, 4, 4, 16, 512)], each + ((64, 16, 1, (), None),), deps
    )
    far = place(chain, 1, spots[1], pieces, [(4, 4, 64, 512)], ((64, 64, 0, (), None),), (mats,))
    return mats.reshape(4, D, 512), vecs, three_ways(chain, 2, far)


def scatter_steps(chain, pieces, spots):
    own, nxt, low, high, prev = pieces
    nxt, prev = add_halves(nxt, prev, send(low, chain, 2, 1), send(high, chain, 2, -1))
    parts = (own, send(nxt, chain, 2, 1), send(prev, chain, 2, -1))
    for phase in (1, 0):
        own, nxt, across, prev = add_split(chain, phase, spots[phase], parts)
        parts = (own, send(nxt, chain, phase, 1), send(prev, chain, phase, -1), send(across, chain, phase, 2))
    return sum(part.astype(jnp.float32) for part in parts)


def regather_steps(chain, chunk, spots):
    for phase in range(2):
        chunk = grow(chain, phase, spots[phase], three_ways(chain, phase, chunk))
    return ring_ways(chain, chunk)


PACKED = ((8, D),) * 4 + ((8, FF), (8, D), (24, D), (32, D)) + ((1, 8),) * 4 + ((1, 32), (1, 8), (1, 8))


def pack_kernel(at_ref, *refs):
    f32, bf16 = jnp.float32, jnp.bfloat16
    count = len(PACKED)
    sources, (blocks_ref, keep_ref, give_ref), held, sems = refs[:count], refs[count : count + 3], refs[count + 3 : -1], refs[-1]
    run_copies([pltpu.make_async_copy(source, place, sems.at[k]) for k, (source, place) in enumerate(zip(sources, held))])
    wq, wk, wv, wr, win, wp, wc, wo, ga, ub, vb, gf, bi, bo, bc = held
    first = at_ref[0] == 0
    where = at_ref[1]

    def spread(ref, size, width):
        row = lax.broadcasted_iota(jnp.int32, (size, width), 0)
        lane = lax.broadcasted_iota(jnp.int32, (size, width), 1)
        hot = (lane == size * where + row).astype(f32).astype(bf16)
        return ndot(ref[...], hot)

    for n, ref in enumerate((wq, wk, wv, wr)):
        left, right = ref[:, :512].astype(f32), ref[:, 512:].astype(f32)
        keep_ref[8 * n : 8 * n + 8, :] = jnp.where(first, left, right).astype(bf16)
        give_ref[8 * n : 8 * n + 8, :] = jnp.where(first, right, left).astype(bf16)
    for n in range(4):
        left, right = (win[:, 2048 * h + 512 * n : 2048 * h + 512 * n + 512].astype(f32) for h in range(2))
        keep_ref[32 + 8 * n : 40 + 8 * n, :] = jnp.where(first, left, right).astype(bf16)
        give_ref[32 + 8 * n : 40 + 8 * n, :] = jnp.where(first, right, left).astype(bf16)
    rows = []
    for ref in (ga, ub, vb, gf):
        wide = spread(ref, 8, D)
        rows += [wide[:, :512], wide[:, 512:]]
    wide = spread(bi, 32, 4 * D)
    halves = [jnp.concatenate([wide[:, 2048 * h + 512 * n : 2048 * h + 512 * n + 512] for n in range(4)], axis=0) for h in range(2)]
    tail = []
    for ref in (bo, bc):
        wide = spread(ref, 8, D)
        tail += [wide[:, :512], wide[:, 512:]]
    keep_ref[64:80, :] = jnp.concatenate(rows + [jnp.where(first, halves[0], halves[1])] + tail, axis=0).astype(bf16)
    give_ref[64:80, :] = jnp.concatenate(rows + [jnp.where(first, halves[1], halves[0])] + tail, axis=0).astype(bf16)
    blocks_ref[0] = wp[...]
    for q in range(3):
        blocks_ref[1 + q] = wc[8 * q : 8 * q + 8, :]
    for q in range(4):
        blocks_ref[4 + q] = wo[8 * q : 8 * q + 8, :]


def pack(at, *arrays):
    return pl.pallas_call(
        pack_kernel,
        in_specs=[SMEM] + [HBM] * len(arrays),
        out_specs=[VMEM] * 3,
        out_shape=[shape_of((8, 8, D), jnp.bfloat16)] + [shape_of((80, 512), jnp.bfloat16)] * 2,
        scratch_shapes=[pltpu.VMEM(shape, jnp.bfloat16) for shape in PACKED] + [pltpu.SemaphoreType.DMA((len(PACKED),))],
        compiler_params=params(60),
        name="pack_weights",
    )(at, *arrays)


def start_kernel(taps_ref, grad_ref, out_ref, stage, sem):
    stage[...] = cdot(taps_ref[...], grad_ref[...]).astype(jnp.bfloat16)
    run_copies([pltpu.make_async_copy(stage, out_ref.at[pl.ds(4096, 1536)], sem)])


def start_buffer(taps, grads):
    return pl.pallas_call(
        start_kernel,
        in_specs=[VMEM, VMEM],
        out_specs=HBM,
        out_shape=shape_of((BUFFER, D), jnp.bfloat16),
        scratch_shapes=[pltpu.VMEM((1536, D), jnp.bfloat16), pltpu.SemaphoreType.DMA],
        compiler_params=params(60),
        name="compression_gradient",
    )(taps, grads)


def normalize(rows):
    centred = rows - jnp.mean(rows, axis=1, keepdims=True)
    inverse = lax.rsqrt(jnp.mean(centred * centred, axis=1, keepdims=True) + EPSILON)
    return centred * inverse, inverse


ROWS = 256


def whole_spec(*shape):
    return pl.BlockSpec(shape, lambda i, c: (0,) * len(shape))


def rows_spec(lanes):
    return pl.BlockSpec((ROWS, lanes), lambda i, c: (i, 0))


def middle_kernel(core_ref, back_ref, got_ref, hidden_ref, gain_ref, gr_ref, proj_ref, hid_ref, branch_ref, att_ref, sum_ref):
    del core_ref
    back = back_ref[...].astype(jnp.float32) + got_ref[...].astype(jnp.float32)
    normed, inverse = normalize(hidden_ref[...])
    total = jnp.sum(back * normed, axis=0, keepdims=True)

    @pl.when(pl.program_id(0) == 0)
    def _():
        sum_ref[...] = total

    @pl.when(pl.program_id(0) > 0)
    def _():
        sum_ref[...] += total

    scaled = back * gain_ref[...]
    along = jnp.mean(scaled * normed, axis=1, keepdims=True)
    grad = gr_ref[...].astype(jnp.float32) + inverse * (
        scaled - jnp.mean(scaled, axis=1, keepdims=True) - normed * along
    )
    hid_ref[...] = grad
    branch = grad.astype(jnp.bfloat16)
    branch_ref[...] = branch
    att_ref[...] = tdot(branch, proj_ref[0]).astype(jnp.bfloat16)


def middle(core, back, got, hidden, gain, grad_res, large):
    return pl.pallas_call(
        middle_kernel,
        grid_spec=pltpu.PrefetchScalarGridSpec(
            num_scalar_prefetch=1,
            grid=(512 // ROWS,),
            in_specs=[
                rows_spec(D), rows_spec(D), rows_spec(D), whole_spec(1, D), rows_spec(D),
                pl.BlockSpec((1, 512, D), lambda i, c: (0, c[0], 0)),
            ],
            out_specs=[rows_spec(D), rows_spec(D), rows_spec(512), whole_spec(1, D)],
        ),
        out_shape=[
            shape_of((512, D)), shape_of((512, D), jnp.bfloat16), shape_of((512, 512), jnp.bfloat16), shape_of((1, D)),
        ],
        compiler_params=params(60),
        name="hidden_gradient",
    )(core, back, got, hidden, gain, grad_res, large)


LATE = ((512, 512), (512, D), (KTOT, D), (3, D, 512), (RELN, D))


def late_kernel(
    at_ref, p_ref, ga_ref, qu_ref, qv_ref, k_ref, v_ref, r_ref, gain_ref, small_ref, *rest
):
    f32, bf16 = jnp.float32, jnp.bfloat16
    count = len(LATE)
    sources, pieces, (gq_out, gk_out, gv_out) = rest[:count], rest[count : count + 5], rest[count + 5 : count + 8]
    ds_s, dw_s, qvr_s, gq_s, both_s, gr_s, sums_s = rest[count + 8 : count + 15]
    att_ref, branch_ref, joined_ref, mats_ref, table_ref = places = rest[count + 15 : -2]
    held, sems = rest[-2:]
    head = pl.program_id(0)

    def loads():
        out = []
        for k, (source, to) in enumerate(zip(sources, places)):
            source = source.at[pl.ds(0, 3)] if k == 3 else source
            out.append(pltpu.make_async_copy(source, to, sems.at[5 + k]))
        return out

    @pl.when(head == 0)
    def _():
        for load in loads():
            load.start()

    flip = (
        lax.broadcasted_iota(jnp.int32, (QB, QB), 0) + lax.broadcasted_iota(jnp.int32, (QB, QB), 1) == QB - 1
    ).astype(f32).astype(bf16)
    du = jnp.zeros((1, HEAD_DIM), f32)
    dv = du
    for b in range(SEG // QB):
        i0, nk, c0 = QB * b, COMP + MEM + QB * (b + 1), SEG - QB - QB * b
        wl = nk + QB
        rows = pl.ds(i0, QB)
        p = p_ref[0, rows, pl.ds(0, nk)].astype(f32)
        dp = tdot(ga_ref[rows, :], v_ref[pl.ds(0, nk), :])
        pd = p * dp
        delta = jnp.sum(pd, axis=1, keepdims=True)
        ds = (pd - p * delta).astype(bf16)
        ds_s[rows, pl.ds(0, nk)] = ds
        if nk < KTOT:
            ds_s[rows, pl.ds(nk, KTOT - nk)] = jnp.zeros((QB, KTOT - nk), bf16)
        wide = jnp.concatenate([ndot(flip, ds), jnp.zeros((QB, QB), f32)], axis=1)
        wide = pltpu.roll(wide, 0, 1, stride=1, stride_axis=0).astype(bf16)
        qvr_s[rows, :] = ndot(flip, qv_ref[rows, :]).astype(bf16)
        dw_s[rows, pl.ds(c0, wl)] = wide
        if c0:
            dw_s[rows, pl.ds(0, c0)] = jnp.zeros((QB, c0), bf16)
        dqu = ndot(ds, k_ref[pl.ds(0, nk), :]) * SCALE
        dqr = ndot(wide, r_ref[pl.ds(c0, wl), :]) * SCALE
        hi = dqr.astype(bf16)
        lo = (dqr - hi.astype(f32)).astype(bf16)
        dqv = ndot(flip, hi) + ndot(flip, lo)
        du += jnp.sum(dqu, axis=0, keepdims=True)
        dv += jnp.sum(dqv, axis=0, keepdims=True)
        gq_out[rows, :] = (dqu + dqv).astype(bf16)
    lanes = pl.ds(pl.multiple_of(HEAD_DIM * head, HEAD_DIM), HEAD_DIM)
    above = pl.ds(pl.multiple_of(512 + HEAD_DIM * head, HEAD_DIM), HEAD_DIM)
    sums_s[0:1, lanes] = du
    sums_s[1:2, lanes] = dv
    gq_s[:, lanes] = gq_out[...]
    grad = (cdot(ds_s[...], qu_ref[...]) * SCALE).astype(bf16)
    both_s[:, lanes] = grad
    gk_out[...] = grad[COMP + MEM :]
    grad = cdot(p_ref[0], ga_ref[...]).astype(bf16)
    both_s[:, above] = grad
    gv_out[...] = grad[COMP + MEM :]
    gr_s[:, lanes] = (cdot(dw_s[...], qvr_s[...]) * SCALE).astype(bf16)

    @pl.when(head == 3)
    def _():
        for load in loads():
            load.wait()
        proj = cdot(att_ref[...], branch_ref[...]).astype(bf16).reshape(4, 4, 4, 8, D)
        for h in range(2):
            held[:, :, :, 64 + 8 * h : 72 + 8 * h, :] = proj[..., 512 * h : 512 * h + 512]
        ones = jnp.ones((8, 512), bf16)

        def keep(m, grad):
            low = grad.astype(bf16)
            for h in range(2):
                held[m, :, :, 32 * h : 32 * h + 32, :] = low[512 * h : 512 * h + 512].reshape(4, 4, 32, 512)
            if m == 3:
                return jnp.zeros((8, D), f32)
            product = grad * mats_ref[m].astype(f32)
            high = product.astype(bf16)
            return tdot(ones, high) + tdot(ones, (product - high.astype(f32)).astype(bf16))

        keep(3, cdot(table_ref[...], gr_s[...]))
        total = keep(0, cdot(joined_ref[pl.ds(COMP + MEM, SEG), :], gq_s[...]))
        pair = cdot(joined_ref[...], both_s[...])
        total += keep(1, pair[:, :512])
        total += keep(2, pair[:, 512:])
        total = total[:1] / gain_ref[...]
        extra = jnp.concatenate([total[:, :512], total[:, 512:], sums_s[0:2, :], small_ref[4:, :]], axis=0)
        held[:, :, :, 80:, :] = jnp.zeros((4, 4, 4, 8, 512), bf16)
        held[0, 0, 0, 80:, :] = extra.astype(bf16)
        send_pieces("AB", 2, RING, at_ref, held, pieces, sems)


def late_gradients(at, probs, grad_att, query_u, query_v, keys, values, rel, gain, small, *arrays):
    f32, bf16 = jnp.float32, jnp.bfloat16
    col = lambda n: pl.BlockSpec((n, HEAD_DIM), lambda h: (0, h))
    const = lambda *shape: pl.BlockSpec(shape, lambda h: (0, 0))
    return pl.pallas_call(
        late_kernel,
        grid=(4,),
        in_specs=[
            SMEM, pl.BlockSpec((1, SEG, KTOT), lambda h: (h, 0, 0)),
            col(SEG), col(SEG), col(SEG), col(KTOT), col(KTOT), col(RELN), const(1, D), const(8, 512),
        ] + [HBM] * len(LATE),
        out_specs=[ANY] * 5 + [col(SEG)] * 3,
        out_shape=[shape_of((4 if part is None else 2, 4, 88, 512), bf16) for _, part in RING]
        + [shape_of((SEG, 512), bf16)] * 3,
        scratch_shapes=[
            pltpu.VMEM((SEG, KTOT), bf16),
            pltpu.VMEM((SEG, RELN), bf16),
            pltpu.VMEM((SEG, HEAD_DIM), bf16),
            pltpu.VMEM((SEG, 512), bf16),
            pltpu.VMEM((KTOT, D), bf16),
            pltpu.VMEM((RELN, 512), bf16),
            pltpu.VMEM((8, 512), f32),
        ]
        + [pltpu.VMEM(shape, bf16) for shape in LATE]
        + [pltpu.VMEM((4, 4, 4, 88, 512), bf16), pltpu.SemaphoreType.DMA((5 + len(LATE),))],
        compiler_params=params(60),
        cost_estimate=pl.CostEstimate(flops=20 << 30, bytes_accessed=30 << 20, transcendentals=0),
        name="attention_backward",
    )(at, probs, grad_att, query_u, query_v, keys, values, rel, gain, small, *arrays)


def ffn_kernel(at_ref, att_ref, got_ref, proj_ref, seg_ref, gain_ref, gr_ref, *rest):
    pieces, quarters, bias_ref, out_ref, back_ref, part_ref, hidden_ref = rest[:4], rest[4:8], rest[8], *rest[10:14]
    panels, act_ref, turned_ref, natural, stage_in, stage_out, sums, back_sum, part_sum, arrived, sems = rest[14:]
    p = pl.program_id(0)
    slot = lax.rem(p, 2)

    def panel_copies(core, m):
        rows = pl.ds(16 * m if isinstance(m, int) else pl.multiple_of(16 * m, 16), 16)
        return [
            pltpu.make_async_copy(
                piece.at[:, :, rows], panels.at[(m,) + spot_of("AB", core, 2, at_ref[k], part)], arrived.at[4 * m + j]
            )
            for j, ((k, part), piece) in enumerate(zip(DIRECT, pieces))
        ]

    for core in range(2):
        @pl.when((p == 0) & (at_ref[4] == core))
        def _():
            for m in range(4):
                for copy in panel_copies(core, m):
                    copy.start()

    @pl.when(p == 0)
    def _():
        core = at_ref[4]
        mine = proj_ref[0, pl.ds(pl.multiple_of(512 * core, 512), 512), :]
        other = proj_ref[0, pl.ds(pl.multiple_of(512 - 512 * core, 512), 512), :]
        hidden = seg_ref[...].astype(jnp.float32) + ndot(att_ref[...], mine) + ndot(got_ref[...], other)
        hidden_ref[...] = hidden
        act = (normalize(hidden)[0] * gain_ref[...]).astype(jnp.bfloat16)
        act_ref[...] = act
        turned_ref[...] = act.T

    for core in range(2):
        @pl.when(at_ref[4] == core)
        def _():
            for copy in panel_copies(core, p):
                copy.wait()

    def sending(step, buffer):
        rows = pl.ds(pl.multiple_of(1024 * (step // 2), 1024), 1024)
        lanes = pl.ds(pl.multiple_of(512 * lax.rem(step, 2), 512), 512)
        below = pl.ds(pl.multiple_of(2048 + 512 * step, 512), 512)
        return [
            pltpu.make_async_copy(stage_in.at[buffer], out_ref.at[rows, lanes], sems.at[buffer]),
            pltpu.make_async_copy(stage_out.at[buffer], out_ref.at[below], sems.at[2 + buffer]),
        ]

    @pl.when(p >= 2)
    def _():
        for copy in sending(p - 2, slot):
            copy.wait()

    act, grad, w_one = act_ref[...], gr_ref[...], panels[p].reshape(D, 512)
    for q in range(4):
        for shard in range(16):
            natural[32 * shard + 8 * q : 32 * shard + 8 * q + 8, :] = quarters[q][0, 8 * shard : 8 * shard + 8, :]
    w_two = natural[...]
    pre = ndot(act, w_one) + bias_ref[0]
    inner = math.sqrt(2.0 / math.pi)
    square = pre * pre
    tanh = jnp.tanh(inner * pre * (1.0 + 0.044715 * square))
    act_low = (0.5 * pre * (1.0 + tanh)).astype(jnp.bfloat16)
    slope = 0.5 * (1.0 + tanh) + (0.5 * inner) * pre * (1.0 - tanh * tanh) * (1.0 + (3.0 * 0.044715) * square)
    grad_act = tdot(grad, w_two)
    grad_pre = (grad_act * slope).astype(jnp.bfloat16)
    stage_in[slot] = ndot(turned_ref[...], grad_pre).astype(jnp.bfloat16)
    stage_out[slot] = cdot(act_low, grad).astype(jnp.bfloat16)
    for copy in sending(p, slot):
        copy.start()
    total = jnp.sum(grad_pre.astype(jnp.float32), axis=0, keepdims=True)
    total = jnp.concatenate([total, total], axis=1)
    row = lax.broadcasted_iota(jnp.int32, (16, D), 0)
    lane = lax.broadcasted_iota(jnp.int32, (16, D), 1)
    mine = (row == p // 2) & (lane // 512 == lax.rem(p, 2))

    @pl.when(p == 0)
    def _():
        sums[...] = jnp.zeros_like(sums)
        back_sum[...] = tdot(grad_pre, w_one)
        part_sum[...] = ndot(act_low, w_two)

    @pl.when((p > 0) & (p < 3))
    def _():
        back_sum[...] += tdot(grad_pre, w_one)
        part_sum[...] += ndot(act_low, w_two)

    @pl.when(p == 3)
    def _():
        back_ref[...] = (back_sum[...] + tdot(grad_pre, w_one)).astype(jnp.bfloat16)
        part_ref[...] = (part_sum[...] + ndot(act_low, w_two)).astype(jnp.bfloat16)

    sums[...] = jnp.where(mine, total, sums[...].astype(jnp.float32)).astype(jnp.bfloat16)

    @pl.when(p == 3)
    def _():
        last = pltpu.make_async_copy(sums, out_ref.at[pl.ds(5632, 16)], sems.at[4])
        last.start()
        for copy in sending(p - 1, 1 - slot) + sending(p, slot):
            copy.wait()
        last.wait()


def ffn(at, att, got, seg, gain, grad, pieces, large, bias, buffer):
    f32, bf16 = jnp.float32, jnp.bfloat16
    whole = pl.BlockSpec((512, D), lambda p, c: (0, 0))
    quarter = lambda q: pl.BlockSpec((1, 128, D), lambda p, c: (4 + q, 4 * c[4] + p, 0))
    return pl.pallas_call(
        ffn_kernel,
        grid_spec=pltpu.PrefetchScalarGridSpec(
            num_scalar_prefetch=1,
            grid=(4,),
            in_specs=[
                whole_spec(512, 512),
                whole_spec(512, 512),
                whole_spec(1, D, D),
                whole,
                whole_spec(1, D),
                whole,
                *([ANY] * 4),
                *(quarter(q) for q in range(4)),
                pl.BlockSpec((1, 1, 512), lambda p, c: (p, 0, 0)),
                HBM,
            ],
            out_specs=[HBM, whole, whole, whole],
            scratch_shapes=[
                pltpu.VMEM(MATS, bf16),
                pltpu.VMEM((512, D), bf16),
                pltpu.VMEM((D, 512), bf16),
                pltpu.VMEM((512, D), bf16),
                pltpu.VMEM((2, D, 512), bf16),
                pltpu.VMEM((2, 512, D), bf16),
                pltpu.VMEM((16, D), bf16),
                pltpu.VMEM((512, D), f32),
                pltpu.VMEM((512, D), f32),
                pltpu.SemaphoreType.DMA((16,)),
                pltpu.SemaphoreType.DMA((5,)),
            ],
        ),
        out_shape=[shape_of((BUFFER, D), bf16), shape_of((512, D), bf16), shape_of((512, D), bf16), shape_of((512, D))],
        input_output_aliases={16: 0},
        compiler_params=params(60),
        cost_estimate=pl.CostEstimate(flops=12 * 512 * 1024 * 2048, bytes_accessed=24 << 20, transcendentals=512 * 2048),
        name="feed_forward",
    )(at, att, got, large, seg, gain, grad, *pieces, large, large, large, large, bias, buffer)


STEP = 128
SLOTS = 8


def widen_kernel(core_ref, second, deps, *refs):
    core = core_ref[0]
    source, outs = refs[0], refs[1 + deps : -4]
    low, high, loads, stores = refs[-4:]
    jobs = []
    if second:
        for q in range(2):
            for r in range(512 // STEP):
                rows = pl.ds(512 * q + STEP * r, STEP)
                lanes = pl.ds(pl.multiple_of(D * (2 * (1 - core) + q), D), D)
                jobs.append((rows, outs[0].at[pl.ds(STEP * r, STEP), lanes]))
    else:
        for r in range(2048 // STEP):
            jobs.append((pl.ds(2048 + STEP * r, STEP), outs[1].at[pl.ds(STEP * r, STEP)]))
        for r in range(1536 // STEP):
            jobs.append((pl.ds(4096 + STEP * r, STEP), outs[2].at[pl.ds(STEP * r, STEP)]))
        for q in range(2):
            for r in range(512 // STEP):
                rows = pl.ds(pl.multiple_of(D * q + 512 * core + STEP * r, STEP), STEP)
                lanes = pl.ds(pl.multiple_of(D * (2 * core + q), D), D)
                jobs.append((rows, outs[0].at[pl.ds(STEP * r, STEP), lanes]))

    def load(k):
        return pltpu.make_async_copy(source.at[jobs[k][0]], low.at[k % SLOTS], loads.at[k % SLOTS])

    def store(k):
        return pltpu.make_async_copy(high.at[k % SLOTS], jobs[k][1], stores.at[k % SLOTS])

    for k in range(SLOTS):
        load(k).start()
    for k in range(len(jobs)):
        load(k).wait()
        if k >= SLOTS:
            store(k - SLOTS).wait()
        high[k % SLOTS] = low[k % SLOTS].astype(jnp.float32)
        store(k).start()
        if k + SLOTS < len(jobs):
            load(k + SLOTS).start()
    for k in range(len(jobs) - SLOTS, len(jobs)):
        store(k).wait()
    if not second:
        run_copies([pltpu.make_async_copy(source.at[pl.ds(5632, 16)], low.at[0, pl.ds(0, 16)], loads.at[0])])
        sums = low[0, :16, :].astype(jnp.float32)
        for t in range(16):
            outs[3][t : t + 1, :] = sums[t // 8 : t // 8 + 1, 128 * (t % 8) : 128 * (t % 8) + 128]


def widen(core, source, deps, into=None):
    shapes = [(512, FF)] if into is not None else [(512, FF), (2048, D), (1536, D), (16, 128)]
    deps = tuple(deps) + (() if into is None else (into,))

    def body(core_ref, *refs):
        widen_kernel(core_ref, into is not None, len(deps), *refs)

    return pl.pallas_call(
        body,
        in_specs=[SMEM, HBM] + [ANY] * len(deps),
        out_specs=[HBM] * min(len(shapes), 3) + [VMEM] * (len(shapes) - 3),
        out_shape=[shape_of(shape) for shape in shapes],
        input_output_aliases={} if into is None else {1 + len(deps): 0},
        scratch_shapes=[
            pltpu.VMEM((SLOTS, STEP, D), jnp.bfloat16),
            pltpu.VMEM((SLOTS, STEP, D), jnp.float32),
            pltpu.SemaphoreType.DMA((SLOTS,)),
            pltpu.SemaphoreType.DMA((SLOTS,)),
        ],
        compiler_params=params(60 if into is None else 20),
        name="widen_gradients",
    )(core, source, *deps)


def pick_kernel(core_ref, source_ref, *rest):
    del core_ref
    rest[-1][...] = source_ref[...]


def pick_halves(core, buffer, deps):
    return pl.pallas_call(
        pick_kernel,
        grid_spec=pltpu.PrefetchScalarGridSpec(
            num_scalar_prefetch=1,
            grid=(2,),
            in_specs=[pl.BlockSpec((512, D), lambda q, c: (2 * q + 1 - c[0], 0))] + [ANY] * len(deps),
            out_specs=pl.BlockSpec((512, D), lambda q, c: (q, 0)),
        ),
        out_shape=shape_of((D, D), jnp.bfloat16),
        compiler_params=params(60),
        name="other_half",
    )(core, buffer, *deps)


def on_device(
    segment, memory, compressed, mem_count, comp_count, attn_gain, w_query, w_key, w_value, u_bias, v_bias,
    w_rel, w_proj, ffn_gain, w_in, b_in, w_out, b_out, w_comp, b_comp, out_grad, comp_grad,
):
    f32, bf16 = jnp.float32, jnp.bfloat16
    core, chip = lax.axis_index("blk"), lax.axis_index("dp")
    first = core == 0
    core_at = core.reshape(1).astype(jnp.int32)
    coords = {"y": chip // 16, "z": (chip // 4) % 4, "x": chip % 4}
    spots = {}
    for chain in ("AB",):
        spots[chain] = []
        for phase in range(3):
            at = jnp.where(first, coords[PATHS[chain[0]][phase]], coords[PATHS[chain[1]][phase]])
            spots[chain].append(jnp.stack([(at + k) % 4 for k in range(4)] + [core]).astype(jnp.int32))

    def both(own, other, axis=0):
        return jnp.where(first, jnp.concatenate([own, other], axis), jnp.concatenate([other, own], axis))

    def half(array, which, axis):
        size = array.shape[axis] // 2
        return lax.dynamic_slice_in_dim(array, which * size, size, axis)

    where_at = jnp.stack([core, 2 * chip + core]).astype(jnp.int32)
    row = lambda vector: vector.reshape(1, -1)
    blocks, keep, give = pack(
        where_at, w_query, w_key, w_value, w_rel, w_in, w_proj, w_comp, w_out,
        row(attn_gain), row(u_bias), row(v_bias), row(ffn_gain), row(b_in), row(b_out), row(b_comp),
    )
    large = lax.all_gather(blocks, ALL_AXES, axis=1, tiled=True)
    got = swap(give)
    chunk = jnp.concatenate(
        [both(keep[8 * n : 8 * n + 8], got[8 * n : 8 * n + 8]) for n in range(8)] + [keep[64:] + got[64:]]
    )

    pieces = [both(array[0], swap(array[0])) for array in (compressed, memory, segment, out_grad, comp_grad)]
    seg_at = COMP + MEM
    grad_res, comp_flat = pieces[3], pieces[4]
    all_rows = jnp.concatenate(pieces[:3])

    def centre(rows):
        mean = jnp.mean(rows, axis=-1, keepdims=True)
        centred = rows - mean
        return mean, lax.rsqrt(jnp.mean(centred * centred, axis=-1, keepdims=True) + EPSILON)

    mean_one, inverse_one = centre(all_rows.astype(f32))

    distance = (KTOT - 1) - jnp.arange(RELN, dtype=f32)
    frequency = jnp.exp(jnp.arange(D // 2, dtype=f32) * (-2.0 * math.log(10000.0) / D))
    coarse = distance[::32, None] * frequency[None, :]
    fine = jnp.arange(32, dtype=f32)[:, None] * frequency[None, :]
    sin_a, cos_a = (trig(coarse)[:, None, :] for trig in (jnp.sin, jnp.cos))
    sin_b, cos_b = (trig(fine)[None, :, :] for trig in (jnp.sin, jnp.cos))
    sines, cosines = sin_a * cos_b - cos_a * sin_b, cos_a * cos_b + sin_a * sin_b
    table = jnp.concatenate([sines.reshape(RELN, 512), cosines.reshape(RELN, 512)], axis=1)
    table = jnp.where(distance[:, None] >= 0.0, table, 0.0).astype(bf16)

    slot = jnp.arange(MEM, dtype=jnp.int32)
    masked = jnp.where((slot >= MEM - mem_count[0])[:, None], pieces[1], jnp.zeros_like(pieces[1]))
    windows = masked.reshape(MEM // RATE, RATE * D)
    buffer = start_buffer(half(windows, core, 1), comp_flat)

    mats, vecs, panels = gather_steps("AB", chunk, spots["AB"], (mean_one, inverse_one, all_rows, table, buffer))
    vecs = jnp.sum(vecs.astype(f32), axis=(0, 1, 2))
    gain_one, gain_two = vecs[:2].reshape(1, D), vecs[6:8].reshape(1, D)
    bias_u = jnp.where(first, vecs[2], vecs[3])
    bias_v = jnp.where(first, vecs[4], vecs[5])
    joined = ((all_rows.astype(f32) - mean_one) * inverse_one * gain_one).astype(bf16)
    query_rows = ndot(joined[seg_at:], mats[0])
    key_rows = ndot(joined, mats[1]).astype(bf16)
    value_rows = ndot(joined, mats[2]).astype(bf16)
    rel_rows = ndot(table, mats[3]).astype(bf16)
    query_u = (query_rows + bias_u).astype(bf16)
    query_v = (query_rows + bias_v).astype(bf16)
    counts = jnp.concatenate([mem_count, comp_count])
    attended, probs = attn_fwd(counts, query_u, query_v, key_rows, value_rows, rel_rows)

    ffn_bias = vecs[8:12].reshape(4, 1, 512)
    out_bias, comp_bias = vecs[12:14].reshape(1, D), vecs[14:16].reshape(1, D)
    buffer, back, partial, hidden = ffn(
        spots["AB"][2], attended, swap(attended), pieces[2], gain_two, grad_res, panels, large, ffn_bias, buffer
    )
    buffer = lax.psum(buffer, "dp")
    grad_hidden, grad_branch, grad_att, d_gain_two = middle(
        core_at, back, swap(back), hidden, gain_two, grad_res, large
    )

    d_b_out = jnp.sum(half(grad_res, core, 1).astype(f32), axis=0, keepdims=True)
    d_b_comp = jnp.sum(half(comp_flat, core, 1).astype(f32), axis=0, keepdims=True)
    small = jnp.concatenate(
        [jnp.zeros((4, 512), f32), half(d_gain_two, core, 1), d_b_out, d_b_comp, jnp.zeros((1, 512), f32)]
    )
    *pieces_late, grad_query, grad_keys, grad_values = late_gradients(
        spots["AB"][2], probs, grad_att, query_u, query_v, key_rows, value_rows, rel_rows, gain_one, small,
        attended, grad_branch, joined, mats, table,
    )
    share = scatter_steps("AB", pieces_late, spots["AB"])
    keep = half(share[:64], core, 0).astype(bf16)
    mail = swap(jnp.concatenate([half(share[:64], 1 - core, 0), share[80:]]).astype(bf16))
    gains = jnp.where(jnp.arange(8)[:, None] < 2, share[80:] + mail[32:].astype(f32), share[80:])
    late = jnp.concatenate([both(keep, mail[:32]), share[64:80].astype(bf16), gains.astype(bf16)])
    received, passed_on = regather_steps("AB", late, spots["AB"])

    partial_sum = half(partial, core, 0).astype(f32) + swap(half(partial, 1 - core, 0)).astype(f32)
    result = half(hidden, core, 0) + partial_sum + out_bias
    output = result.astype(bf16)

    comp_proj = large[1:4].reshape(3, 128, 8, D).transpose(1, 0, 2, 3).reshape(RATE * D, D)
    new_compressed = (ndot(half(windows, core, 0), comp_proj) + comp_bias).astype(bf16)

    grad_seg = (
        tdot(grad_query, mats[0]) + tdot(grad_keys, mats[1]) + tdot(grad_values, mats[2])
    )
    grad_seg = half(grad_seg, core, 0) + swap(half(grad_seg, 1 - core, 0))
    scaled_one = grad_seg * gain_one
    own_segment = segment[0].astype(f32)
    mean_seg, inverse_seg = centre(own_segment)
    normed_seg = (own_segment - mean_seg) * inverse_seg
    d_segment = half(grad_hidden, core, 0) + inverse_seg * (
        scaled_one
        - jnp.mean(scaled_one, axis=-1, keepdims=True)
        - normed_seg * jnp.mean(scaled_one * normed_seg, axis=-1, keepdims=True)
    )

    deps = passed_on + (output, new_compressed, d_segment)
    others = pick_halves(core_at, buffer, deps)
    d_in, d_out, d_comp, sums = widen(core_at, buffer, deps + (others,))
    *late, d_proj, g1, g2, g3, g4, g5, g6 = finish("AB", spots["AB"][2], received, d_out)
    extra = [array.reshape(512) for array in (g1, g2, g3, g4, g5, g6)]
    (d_in,) = widen(core_at, swap(others), (late[0],), d_in)
    d_b_in = sums.reshape(2048)
    return (
        output[None],
        new_compressed[None],
        d_segment[None],
        extra[0],
        late[0],
        late[1],
        late[2],
        extra[1],
        extra[2],
        late[3],
        d_proj,
        extra[3],
        d_in,
        d_b_in,
        d_out,
        extra[4],
        d_comp,
        extra[5],
    )


def solution(mesh):
    rows, weight, vector = P("dp", "blk", None), P(("dp", "blk"), None), P(("dp", "blk"))
    placed = (
        rows, rows, rows, P("dp"), P("dp"), vector, weight, weight, weight, vector, vector,
        weight, weight, vector, weight, vector, weight, vector, weight, vector, rows, rows,
    )
    half_one, half_two = P("blk"), P("blk", None)
    return jax.shard_map(
        on_device,
        mesh=mesh,
        in_specs=placed,
        out_specs=(
            rows, rows, rows, half_one, half_two, half_two, half_two, half_one, half_one,
            half_two, half_two, half_one, half_two, half_one, half_two, half_one, half_two, half_one,
        ),
        check_vma=False,
    )
```

```python
import math, functools
import jax, jax.numpy as jnp
from jax import lax
from jax.sharding import PartitionSpec as P
from jax.experimental import pallas as pl
from jax.experimental.pallas import tpu as pltpu
D=1024
FF=4096
HEAD_DIM=128
SEG=512
MEM=384
COMP=512
RATE=3
KTOT=1408
RELN=1536
QB=128
EPSILON=1e-05
SCALE=1.0/math.sqrt(HEAD_DIM); NEG=-1e30
def tdot(a,b):
    return lax.dot_general(a,b,(((1,),(1,)),((),())),preferred_element_type=jnp.float32)
def ndot(a,b):
    return lax.dot_general(a,b,(((1,),(0,)),((),())),preferred_element_type=jnp.float32)
def cdot(a,b):
    return lax.dot_general(a,b,(((0,),(0,)),((),())),preferred_element_type=jnp.float32)

def attn_fwd_kernel(cnt_ref, qu_ref, qv_ref, k_ref, v_ref, r_ref, att_ref, p_ref):
    mc = cnt_ref[0]; cc = cnt_ref[1]
    kp = lax.broadcasted_iota(jnp.int32,(1,COMP+MEM),1)
    ok = ((kp < COMP) & (kp >= COMP-cc)) | ((kp>=COMP)&(kp>=COMP+MEM-mc))
    old_bias = jnp.where(ok, 0.0, NEG)
    tri = jnp.where(lax.broadcasted_iota(jnp.int32,(QB,QB),1) <= lax.broadcasted_iota(jnp.int32,(QB,QB),0), 0.0, NEG)
    for b in range(SEG//QB):
        i0=QB*b; nk=COMP+MEM+QB*(b+1); c0=SEG-QB-QB*b; wl=nk+QB
        s = tdot(qu_ref[pl.ds(i0,QB),:], k_ref[pl.ds(0,nk),:])
        w = tdot(qv_ref[pl.ds(i0,QB),:], r_ref[pl.ds(c0,wl),:])
        w = pltpu.roll(w, wl-(QB-1), 1, stride=1, stride_axis=0)[:,:nk]
        s = (s+w)*SCALE
        parts=[s[:,:COMP+MEM]+old_bias]
        if b: parts.append(s[:,COMP+MEM:nk-QB])
        parts.append(s[:,nk-QB:]+tri)
        s=jnp.concatenate(parts,axis=1)
        m=jnp.max(s,axis=1,keepdims=True)
        e=jnp.exp(s-m)
        l=jnp.sum(e,axis=1,keepdims=True)
        p=(e*(1.0/l)).astype(jnp.bfloat16)
        p_ref[0,pl.ds(i0,QB),pl.ds(0,nk)]=p
        if nk<KTOT: p_ref[0,pl.ds(i0,QB),pl.ds(nk,KTOT-nk)]=jnp.zeros((QB,KTOT-nk),jnp.bfloat16)
        att_ref[pl.ds(i0,QB),:]=ndot(p,v_ref[pl.ds(0,nk),:]).astype(jnp.bfloat16)

def attn_fwd(cnt,qu,qv,k,v,r):
    nh=qu.shape[1]//HEAD_DIM
    col=lambda n: pl.BlockSpec((n,HEAD_DIM),lambda h:(0,h))
    return pl.pallas_call(attn_fwd_kernel, grid=(nh,),
        in_specs=[pl.BlockSpec(memory_space=pltpu.SMEM),col(SEG),col(SEG),col(KTOT),col(KTOT),col(RELN)],
        out_specs=[col(SEG),pl.BlockSpec((1,SEG,KTOT),lambda h:(h,0,0))],
        out_shape=[jax.ShapeDtypeStruct((SEG,nh*HEAD_DIM),jnp.bfloat16),jax.ShapeDtypeStruct((nh,SEG,KTOT),jnp.bfloat16)],
        compiler_params=pltpu.CompilerParams(vmem_limit_bytes=40<<20),
        cost_estimate=pl.CostEstimate(flops=6*nh*SEG*KTOT*HEAD_DIM,bytes_accessed=12<<20,transcendentals=nh*SEG*KTOT),
        name="attention_forward")(cnt,qu,qv,k,v,r)


PATHS = {"A": ("x", "z", "y"), "B": ("y", "x", "z"), "C": ("z", "y", "x")}
SPOT = {
    name: tuple(sorted(path[: phase + 1], key="yzx".index).index(path[phase]) for phase in range(3))
    for name, path in PATHS.items()
}
STRIDE = {"y": 16, "z": 4, "x": 1}
ALL_AXES = ("dp", "blk")
BUFFER = 5648
ANY = pl.BlockSpec(memory_space=pl.ANY)
SMEM = pl.BlockSpec(memory_space=pltpu.SMEM)
VMEM = pl.BlockSpec(memory_space=pltpu.VMEM)
HBM = pl.BlockSpec(memory_space=pltpu.HBM)


def params(mib=40):
    return pltpu.CompilerParams(vmem_limit_bytes=mib << 20)


def shape_of(shape, dtype=jnp.float32):
    return jax.ShapeDtypeStruct(shape, dtype)


def swap(array):
    return lax.ppermute(array, "blk", [(0, 1), (1, 0)])


def step_pairs(chain, phase, delta):
    pairs = []
    for chip in range(64):
        for core in range(2):
            stride = STRIDE[PATHS[chain[core]][phase]]
            at = (chip // stride) % 4
            pairs.append((2 * chip + core, 2 * (chip + ((at + delta) % 4 - at) * stride) + core))
    return pairs


def send(array, chain, phase, delta):
    return lax.ppermute(array, ALL_AXES, step_pairs(chain, phase, delta))


def run_copies(copies):
    for copy in copies:
        copy.start()
    for copy in copies:
        copy.wait()


def spot_of(chain, core, phase, index, part=None):
    where = [slice(None)] * phase
    if part is not None:
        where[0] = pl.ds(2 * part, 2)
    where.insert(SPOT[chain[core]][phase], index)
    return tuple(where)


DIRECT = ((0, None), (1, None), (2, None), (3, None))
RING = ((0, None), (1, None), (2, 0), (2, 1), (3, None))


def place_kernel(chain, phase, moves, deps, ways, at_ref, *rest):
    pieces, outs, sems = rest[: len(ways)], rest[len(ways) + deps : -1], rest[-1]
    lead = (slice(None),) * phase
    for core in range(2):
        @pl.when(at_ref[4] == core)
        def _():
            copies = []
            for j, ((k, part), piece) in enumerate(zip(ways, pieces)):
                where = spot_of(chain, core, phase, at_ref[k], part)
                for n, (start, size, out, head, to) in enumerate(moves):
                    source = piece.at[lead + (pl.ds(start, size),)]
                    target = outs[out].at[head + where]
                    if to is not None:
                        target = target.at[lead + (pl.ds(to, size),)]
                    copies.append(pltpu.make_async_copy(source, target, sems.at[j * len(moves) + n]))
            run_copies(copies)


def place(chain, phase, at, pieces, shapes, moves, deps=(), mib=32):
    ways = RING if len(pieces) == 5 else DIRECT
    out = pl.pallas_call(
        functools.partial(place_kernel, chain, phase, moves, len(deps), ways),
        in_specs=[SMEM] + [ANY] * (len(ways) + len(deps)),
        out_specs=[VMEM] * len(shapes),
        out_shape=[shape_of(shape, jnp.bfloat16) for shape in shapes],
        scratch_shapes=[pltpu.SemaphoreType.DMA((len(ways) * len(moves),))],
        compiler_params=params(mib),
        name="place_pieces",
    )(at, *pieces, *deps)
    return out if len(shapes) > 1 else out[0]


def grow(chain, phase, at, pieces):
    rows, lanes = pieces[0].shape[-2:]
    return place(chain, phase, at, pieces, [(4,) * (phase + 1) + (rows, lanes)], ((0, rows, 0, (), None),))


def send_pieces(chain, phase, ways, at_ref, held, pieces, sems):
    for core in range(2):
        @pl.when(at_ref[4] == core)
        def _():
            copies = []
            for j, ((k, part), piece) in enumerate(zip(ways, pieces)):
                where = spot_of(chain, core, phase, at_ref[k], part)
                copies.append(pltpu.make_async_copy(held.at[where], piece, sems.at[j]))
            run_copies(copies)


def split_kernel(chain, phase, count, at_ref, *rest):
    parts, pieces, held, sems = rest[:count], rest[count : count + 4], rest[-2], rest[-1]
    held[...] = sum(ref[...].astype(jnp.float32) for ref in parts).astype(jnp.bfloat16)
    send_pieces(chain, phase, DIRECT, at_ref, held, pieces, sems)


def add_split(chain, phase, at, parts):
    shape = parts[0].shape
    return pl.pallas_call(
        functools.partial(split_kernel, chain, phase, len(parts)),
        in_specs=[SMEM] + [VMEM] * len(parts),
        out_specs=[ANY] * 4,
        out_shape=[shape_of(shape[1:], jnp.bfloat16)] * 4,
        scratch_shapes=[pltpu.VMEM(shape, jnp.bfloat16), pltpu.SemaphoreType.DMA((4,))],
        compiler_params=params(32),
        name="add_pieces",
    )(at, *parts)


def halves_kernel(next_ref, prev_ref, low_ref, high_ref, next_out, prev_out):
    f32, bf16 = jnp.float32, jnp.bfloat16
    next_out[:2] = (next_ref[:2].astype(f32) + low_ref[...].astype(f32)).astype(bf16)
    next_out[2:] = next_ref[2:]
    prev_out[:2] = prev_ref[:2]
    prev_out[2:] = (prev_ref[2:].astype(f32) + high_ref[...].astype(f32)).astype(bf16)


def add_halves(*arrays):
    return pl.pallas_call(
        halves_kernel,
        in_specs=[VMEM] * 4,
        out_specs=[VMEM] * 2,
        out_shape=[shape_of(arrays[0].shape, jnp.bfloat16)] * 2,
        compiler_params=params(32),
        name="add_halves",
    )(*arrays)


def finish_kernel(chain, at_ref, *rest):
    received, (*outs, proj_ref, o1, o2, o3, o4, o5, o6, held, sems) = rest[:5], rest[6:]
    for core in range(2):
        @pl.when(at_ref[4] == core)
        def _():
            copies = []
            for j, ((k, part), piece) in enumerate(zip(RING, received)):
                where = spot_of(chain, core, 2, at_ref[k], part)
                copies.append(pltpu.make_async_copy(piece, held.at[where], sems.at[j]))
            run_copies(copies)
    extra = held[0, 0, 0, 80:, :].astype(jnp.float32)
    rows = [jnp.where(at_ref[4] == 0, extra[0:1], extra[1:2])] + [extra[k : k + 1] for k in range(2, 7)]
    for ref, row in zip((o1, o2, o3, o4, o5, o6), rows):
        for t in range(4):
            ref[t : t + 1, :] = row[:, 128 * t : 128 * t + 128]
    for chip in range(64):
        y, z, x = chip // 16, (chip // 4) % 4, chip % 4
        for h in range(2):
            block = held[y, z, x, 32 * h : 32 * h + 32, :].astype(jnp.float32)
            outs[y][pl.ds(32 * (chip % 16), 32), pl.ds(512 * h, 512)] = block
            block = held[y, z, x, 64 + 8 * h : 72 + 8 * h, :].astype(jnp.float32)
            proj_ref[pl.ds(8 * chip, 8), pl.ds(512 * h, 512)] = block


def finish(chain, at, pieces, after):
    return pl.pallas_call(
        functools.partial(finish_kernel, chain),
        in_specs=[SMEM] + [ANY] * 6,
        out_specs=[VMEM] * 11,
        out_shape=[shape_of((512, D))] * 5 + [shape_of((4, 128))] * 6,
        scratch_shapes=[pltpu.VMEM((4, 4, 4, 88, 512), jnp.bfloat16), pltpu.SemaphoreType.DMA((5,))],
        compiler_params=params(60),
        name="finish_gradients",
    )(at, *pieces, after)


def three_ways(chain, phase, chunk):
    prev, nxt, across = send(chunk, chain, phase, 1), send(chunk, chain, phase, -1), send(chunk, chain, phase, 2)
    return chunk, nxt, across, prev


def ring_ways(chain, chunk):
    prev, nxt = send(chunk, chain, 2, 1), send(chunk, chain, 2, -1)
    low, high = nxt[:2], prev[2:]
    return (chunk, nxt, send(low, chain, 2, -1), send(high, chain, 2, 1), prev), (low, high)


MATS = (4, 4, 4, 4, 16, 512)


def gather_steps(chain, chunk, spots, deps):
    chunk = grow(chain, 0, spots[0], three_ways(chain, 0, chunk))
    pieces = three_ways(chain, 1, chunk)
    near = place(chain, 1, spots[1], pieces, [(4, 4, 80, 512)], ((0, 64, 0, (), 0), (128, 16, 0, (), 64)))
    each = tuple((16 * m, 16, 0, (m,), None) for m in range(4))
    mats, vecs = place(
        chain, 2, spots[2], three_ways(chain, 2, near), [MATS, (4, 4, 4, 16, 512)], each + ((64, 16, 1, (), None),), deps
    )
    far = place(chain, 1, spots[1], pieces, [(4, 4, 64, 512)], ((64, 64, 0, (), None),), (mats,))
    return mats.reshape(4, D, 512), vecs, three_ways(chain, 2, far)


def scatter_steps(chain, pieces, spots):
    own, nxt, low, high, prev = pieces
    nxt, prev = add_halves(nxt, prev, send(low, chain, 2, 1), send(high, chain, 2, -1))
    parts = (own, send(nxt, chain, 2, 1), send(prev, chain, 2, -1))
    for phase in (1, 0):
        own, nxt, across, prev = add_split(chain, phase, spots[phase], parts)
        parts = (own, send(nxt, chain, phase, 1), send(prev, chain, phase, -1), send(across, chain, phase, 2))
    return sum(part.astype(jnp.float32) for part in parts)


def regather_steps(chain, chunk, spots):
    for phase in range(2):
        chunk = grow(chain, phase, spots[phase], three_ways(chain, phase, chunk))
    return ring_ways(chain, chunk)


PACKED = ((8, D),) * 4 + ((8, FF), (8, D), (24, D), (32, D)) + ((1, 8),) * 4 + ((1, 32), (1, 8), (1, 8))


def pack_kernel(at_ref, *refs):
    f32, bf16 = jnp.float32, jnp.bfloat16
    count = len(PACKED)
    sources, (blocks_ref, keep_ref, give_ref), held, sems = refs[:count], refs[count : count + 3], refs[count + 3 : -1], refs[-1]
    run_copies([pltpu.make_async_copy(source, place, sems.at[k]) for k, (source, place) in enumerate(zip(sources, held))])
    wq, wk, wv, wr, win, wp, wc, wo, ga, ub, vb, gf, bi, bo, bc = held
    first = at_ref[0] == 0
    where = at_ref[1]

    def spread(ref, size, width):
        row = lax.broadcasted_iota(jnp.int32, (size, width), 0)
        lane = lax.broadcasted_iota(jnp.int32, (size, width), 1)
        hot = (lane == size * where + row).astype(f32).astype(bf16)
        return ndot(ref[...], hot)

    for n, ref in enumerate((wq, wk, wv, wr)):
        left, right = ref[:, :512].astype(f32), ref[:, 512:].astype(f32)
        keep_ref[8 * n : 8 * n + 8, :] = jnp.where(first, left, right).astype(bf16)
        give_ref[8 * n : 8 * n + 8, :] = jnp.where(first, right, left).astype(bf16)
    for n in range(4):
        left, right = (win[:, 2048 * h + 512 * n : 2048 * h + 512 * n + 512].astype(f32) for h in range(2))
        keep_ref[32 + 8 * n : 40 + 8 * n, :] = jnp.where(first, left, right).astype(bf16)
        give_ref[32 + 8 * n : 40 + 8 * n, :] = jnp.where(first, right, left).astype(bf16)
    rows = []
    for ref in (ga, ub, vb, gf):
        wide = spread(ref, 8, D)
        rows += [wide[:, :512], wide[:, 512:]]
    wide = spread(bi, 32, 4 * D)
    halves = [jnp.concatenate([wide[:, 2048 * h + 512 * n : 2048 * h + 512 * n + 512] for n in range(4)], axis=0) for h in range(2)]
    tail = []
    for ref in (bo, bc):
        wide = spread(ref, 8, D)
        tail += [wide[:, :512], wide[:, 512:]]
    keep_ref[64:80, :] = jnp.concatenate(rows + [jnp.where(first, halves[0], halves[1])] + tail, axis=0).astype(bf16)
    give_ref[64:80, :] = jnp.concatenate(rows + [jnp.where(first, halves[1], halves[0])] + tail, axis=0).astype(bf16)
    blocks_ref[0] = wp[...]
    for q in range(3):
        blocks_ref[1 + q] = wc[8 * q : 8 * q + 8, :]
    for q in range(4):
        blocks_ref[4 + q] = wo[8 * q : 8 * q + 8, :]


def pack(at, *arrays):
    return pl.pallas_call(
        pack_kernel,
        in_specs=[SMEM] + [HBM] * len(arrays),
        out_specs=[VMEM] * 3,
        out_shape=[shape_of((8, 8, D), jnp.bfloat16)] + [shape_of((80, 512), jnp.bfloat16)] * 2,
        scratch_shapes=[pltpu.VMEM(shape, jnp.bfloat16) for shape in PACKED] + [pltpu.SemaphoreType.DMA((len(PACKED),))],
        compiler_params=params(60),
        name="pack_weights",
    )(at, *arrays)


def start_kernel(taps_ref, grad_ref, out_ref, stage, sem):
    stage[...] = cdot(taps_ref[...], grad_ref[...]).astype(jnp.bfloat16)
    run_copies([pltpu.make_async_copy(stage, out_ref.at[pl.ds(4096, 1536)], sem)])


def start_buffer(taps, grads):
    return pl.pallas_call(
        start_kernel,
        in_specs=[VMEM, VMEM],
        out_specs=HBM,
        out_shape=shape_of((BUFFER, D), jnp.bfloat16),
        scratch_shapes=[pltpu.VMEM((1536, D), jnp.bfloat16), pltpu.SemaphoreType.DMA],
        compiler_params=params(60),
        name="compression_gradient",
    )(taps, grads)


def normalize(rows):
    centred = rows - jnp.mean(rows, axis=1, keepdims=True)
    inverse = lax.rsqrt(jnp.mean(centred * centred, axis=1, keepdims=True) + EPSILON)
    return centred * inverse, inverse


ROWS = 256


def whole_spec(*shape):
    return pl.BlockSpec(shape, lambda i, c: (0,) * len(shape))


def rows_spec(lanes):
    return pl.BlockSpec((ROWS, lanes), lambda i, c: (i, 0))


def middle_kernel(core_ref, back_ref, got_ref, hidden_ref, gain_ref, gr_ref, proj_ref, hid_ref, branch_ref, att_ref, sum_ref):
    del core_ref
    back = back_ref[...].astype(jnp.float32) + got_ref[...].astype(jnp.float32)
    normed, inverse = normalize(hidden_ref[...])
    total = jnp.sum(back * normed, axis=0, keepdims=True)

    @pl.when(pl.program_id(0) == 0)
    def _():
        sum_ref[...] = total

    @pl.when(pl.program_id(0) > 0)
    def _():
        sum_ref[...] += total

    scaled = back * gain_ref[...]
    along = jnp.mean(scaled * normed, axis=1, keepdims=True)
    grad = gr_ref[...].astype(jnp.float32) + inverse * (
        scaled - jnp.mean(scaled, axis=1, keepdims=True) - normed * along
    )
    hid_ref[...] = grad
    branch = grad.astype(jnp.bfloat16)
    branch_ref[...] = branch
    att_ref[...] = tdot(branch, proj_ref[0]).astype(jnp.bfloat16)


def middle(core, back, got, hidden, gain, grad_res, large):
    return pl.pallas_call(
        middle_kernel,
        grid_spec=pltpu.PrefetchScalarGridSpec(
            num_scalar_prefetch=1,
            grid=(512 // ROWS,),
            in_specs=[
                rows_spec(D), rows_spec(D), rows_spec(D), whole_spec(1, D), rows_spec(D),
                pl.BlockSpec((1, 512, D), lambda i, c: (0, c[0], 0)),
            ],
            out_specs=[rows_spec(D), rows_spec(D), rows_spec(512), whole_spec(1, D)],
        ),
        out_shape=[
            shape_of((512, D)), shape_of((512, D), jnp.bfloat16), shape_of((512, 512), jnp.bfloat16), shape_of((1, D)),
        ],
        compiler_params=params(60),
        name="hidden_gradient",
    )(core, back, got, hidden, gain, grad_res, large)


LATE = ((512, 512), (512, D), (KTOT, D), (3, D, 512), (RELN, D))


def late_kernel(
    at_ref, p_ref, ga_ref, qu_ref, qv_ref, k_ref, v_ref, r_ref, gain_ref, small_ref, *rest
):
    f32, bf16 = jnp.float32, jnp.bfloat16
    count = len(LATE)
    sources, pieces, (gq_out, gk_out, gv_out) = rest[:count], rest[count : count + 5], rest[count + 5 : count + 8]
    ds_s, dw_s, qvr_s, gq_s, both_s, gr_s, sums_s = rest[count + 8 : count + 15]
    att_ref, branch_ref, joined_ref, mats_ref, table_ref = places = rest[count + 15 : -2]
    held, sems = rest[-2:]
    head = pl.program_id(0)

    def loads():
        out = []
        for k, (source, to) in enumerate(zip(sources, places)):
            source = source.at[pl.ds(0, 3)] if k == 3 else source
            out.append(pltpu.make_async_copy(source, to, sems.at[5 + k]))
        return out

    @pl.when(head == 0)
    def _():
        for load in loads():
            load.start()

    flip = (
        lax.broadcasted_iota(jnp.int32, (QB, QB), 0) + lax.broadcasted_iota(jnp.int32, (QB, QB), 1) == QB - 1
    ).astype(f32).astype(bf16)
    du = jnp.zeros((1, HEAD_DIM), f32)
    dv = du
    for b in range(SEG // QB):
        i0, nk, c0 = QB * b, COMP + MEM + QB * (b + 1), SEG - QB - QB * b
        wl = nk + QB
        rows = pl.ds(i0, QB)
        p = p_ref[0, rows, pl.ds(0, nk)].astype(f32)
        dp = tdot(ga_ref[rows, :], v_ref[pl.ds(0, nk), :])
        pd = p * dp
        delta = jnp.sum(pd, axis=1, keepdims=True)
        ds = (pd - p * delta).astype(bf16)
        ds_s[rows, pl.ds(0, nk)] = ds
        if nk < KTOT:
            ds_s[rows, pl.ds(nk, KTOT - nk)] = jnp.zeros((QB, KTOT - nk), bf16)
        wide = jnp.concatenate([ndot(flip, ds), jnp.zeros((QB, QB), f32)], axis=1)
        wide = pltpu.roll(wide, 0, 1, stride=1, stride_axis=0).astype(bf16)
        qvr_s[rows, :] = ndot(flip, qv_ref[rows, :]).astype(bf16)
        dw_s[rows, pl.ds(c0, wl)] = wide
        if c0:
            dw_s[rows, pl.ds(0, c0)] = jnp.zeros((QB, c0), bf16)
        dqu = ndot(ds, k_ref[pl.ds(0, nk), :]) * SCALE
        dqr = ndot(wide, r_ref[pl.ds(c0, wl), :]) * SCALE
        hi = dqr.astype(bf16)
        lo = (dqr - hi.astype(f32)).astype(bf16)
        dqv = ndot(flip, hi) + ndot(flip, lo)
        du += jnp.sum(dqu, axis=0, keepdims=True)
        dv += jnp.sum(dqv, axis=0, keepdims=True)
        gq_out[rows, :] = (dqu + dqv).astype(bf16)
    lanes = pl.ds(pl.multiple_of(HEAD_DIM * head, HEAD_DIM), HEAD_DIM)
    above = pl.ds(pl.multiple_of(512 + HEAD_DIM * head, HEAD_DIM), HEAD_DIM)
    sums_s[0:1, lanes] = du
    sums_s[1:2, lanes] = dv
    gq_s[:, lanes] = gq_out[...]
    grad = (cdot(ds_s[...], qu_ref[...]) * SCALE).astype(bf16)
    both_s[:, lanes] = grad
    gk_out[...] = grad[COMP + MEM :]
    grad = cdot(p_ref[0], ga_ref[...]).astype(bf16)
    both_s[:, above] = grad
    gv_out[...] = grad[COMP + MEM :]
    gr_s[:, lanes] = (cdot(dw_s[...], qvr_s[...]) * SCALE).astype(bf16)

    @pl.when(head == 3)
    def _():
        for load in loads():
            load.wait()
        proj = cdot(att_ref[...], branch_ref[...]).astype(bf16).reshape(4, 4, 4, 8, D)
        for h in range(2):
            held[:, :, :, 64 + 8 * h : 72 + 8 * h, :] = proj[..., 512 * h : 512 * h + 512]
        ones = jnp.ones((8, 512), bf16)

        def keep(m, grad):
            low = grad.astype(bf16)
            for h in range(2):
                held[m, :, :, 32 * h : 32 * h + 32, :] = low[512 * h : 512 * h + 512].reshape(4, 4, 32, 512)
            if m == 3:
                return jnp.zeros((8, D), f32)
            product = grad * mats_ref[m].astype(f32)
            high = product.astype(bf16)
            return tdot(ones, high) + tdot(ones, (product - high.astype(f32)).astype(bf16))

        keep(3, cdot(table_ref[...], gr_s[...]))
        total = keep(0, cdot(joined_ref[pl.ds(COMP + MEM, SEG), :], gq_s[...]))
        pair = cdot(joined_ref[...], both_s[...])
        total += keep(1, pair[:, :512])
        total += keep(2, pair[:, 512:])
        total = total[:1] / gain_ref[...]
        extra = jnp.concatenate([total[:, :512], total[:, 512:], sums_s[0:2, :], small_ref[4:, :]], axis=0)
        held[:, :, :, 80:, :] = jnp.zeros((4, 4, 4, 8, 512), bf16)
        held[0, 0, 0, 80:, :] = extra.astype(bf16)
        send_pieces("AB", 2, RING, at_ref, held, pieces, sems)


def late_gradients(at, probs, grad_att, query_u, query_v, keys, values, rel, gain, small, *arrays):
    f32, bf16 = jnp.float32, jnp.bfloat16
    col = lambda n: pl.BlockSpec((n, HEAD_DIM), lambda h: (0, h))
    const = lambda *shape: pl.BlockSpec(shape, lambda h: (0, 0))
    return pl.pallas_call(
        late_kernel,
        grid=(4,),
        in_specs=[
            SMEM, pl.BlockSpec((1, SEG, KTOT), lambda h: (h, 0, 0)),
            col(SEG), col(SEG), col(SEG), col(KTOT), col(KTOT), col(RELN), const(1, D), const(8, 512),
        ] + [HBM] * len(LATE),
        out_specs=[ANY] * 5 + [col(SEG)] * 3,
        out_shape=[shape_of((4 if part is None else 2, 4, 88, 512), bf16) for _, part in RING]
        + [shape_of((SEG, 512), bf16)] * 3,
        scratch_shapes=[
            pltpu.VMEM((SEG, KTOT), bf16),
            pltpu.VMEM((SEG, RELN), bf16),
            pltpu.VMEM((SEG, HEAD_DIM), bf16),
            pltpu.VMEM((SEG, 512), bf16),
            pltpu.VMEM((KTOT, D), bf16),
            pltpu.VMEM((RELN, 512), bf16),
            pltpu.VMEM((8, 512), f32),
        ]
        + [pltpu.VMEM(shape, bf16) for shape in LATE]
        + [pltpu.VMEM((4, 4, 4, 88, 512), bf16), pltpu.SemaphoreType.DMA((5 + len(LATE),))],
        compiler_params=params(60),
        cost_estimate=pl.CostEstimate(flops=20 << 30, bytes_accessed=30 << 20, transcendentals=0),
        name="attention_backward",
    )(at, probs, grad_att, query_u, query_v, keys, values, rel, gain, small, *arrays)


def ffn_kernel(at_ref, att_ref, got_ref, proj_ref, seg_ref, gain_ref, gr_ref, *rest):
    pieces, quarters, bias_ref, out_ref, back_ref, part_ref, hidden_ref = rest[:4], rest[4:8], rest[8], *rest[10:14]
    panels, act_ref, turned_ref, natural, stage_in, stage_out, sums, back_sum, part_sum, arrived, sems = rest[14:]
    p = pl.program_id(0)
    slot = lax.rem(p, 2)

    def panel_copies(core, m):
        rows = pl.ds(16 * m if isinstance(m, int) else pl.multiple_of(16 * m, 16), 16)
        return [
            pltpu.make_async_copy(
                piece.at[:, :, rows], panels.at[(m,) + spot_of("AB", core, 2, at_ref[k], part)], arrived.at[4 * m + j]
            )
            for j, ((k, part), piece) in enumerate(zip(DIRECT, pieces))
        ]

    for core in range(2):
        @pl.when((p == 0) & (at_ref[4] == core))
        def _():
            for m in range(4):
                for copy in panel_copies(core, m):
                    copy.start()

    @pl.when(p == 0)
    def _():
        core = at_ref[4]
        mine = proj_ref[0, pl.ds(pl.multiple_of(512 * core, 512), 512), :]
        other = proj_ref[0, pl.ds(pl.multiple_of(512 - 512 * core, 512), 512), :]
        hidden = seg_ref[...].astype(jnp.float32) + ndot(att_ref[...], mine) + ndot(got_ref[...], other)
        hidden_ref[...] = hidden
        act = (normalize(hidden)[0] * gain_ref[...]).astype(jnp.bfloat16)
        act_ref[...] = act
        turned_ref[...] = act.T

    for core in range(2):
        @pl.when(at_ref[4] == core)
        def _():
            for copy in panel_copies(core, p):
                copy.wait()

    def sending(step, buffer):
        rows = pl.ds(pl.multiple_of(1024 * (step // 2), 1024), 1024)
        lanes = pl.ds(pl.multiple_of(512 * lax.rem(step, 2), 512), 512)
        below = pl.ds(pl.multiple_of(2048 + 512 * step, 512), 512)
        return [
            pltpu.make_async_copy(stage_in.at[buffer], out_ref.at[rows, lanes], sems.at[buffer]),
            pltpu.make_async_copy(stage_out.at[buffer], out_ref.at[below], sems.at[2 + buffer]),
        ]

    @pl.when(p >= 2)
    def _():
        for copy in sending(p - 2, slot):
            copy.wait()

    act, grad, w_one = act_ref[...], gr_ref[...], panels[p].reshape(D, 512)
    for q in range(4):
        for shard in range(16):
            natural[32 * shard + 8 * q : 32 * shard + 8 * q + 8, :] = quarters[q][0, 8 * shard : 8 * shard + 8, :]
    w_two = natural[...]
    pre = ndot(act, w_one) + bias_ref[0]
    inner = math.sqrt(2.0 / math.pi)
    square = pre * pre
    tanh = jnp.tanh(inner * pre * (1.0 + 0.044715 * square))
    act_low = (0.5 * pre * (1.0 + tanh)).astype(jnp.bfloat16)
    slope = 0.5 * (1.0 + tanh) + (0.5 * inner) * pre * (1.0 - tanh * tanh) * (1.0 + (3.0 * 0.044715) * square)
    grad_act = tdot(grad, w_two)
    grad_pre = (grad_act * slope).astype(jnp.bfloat16)
    stage_in[slot] = ndot(turned_ref[...], grad_pre).astype(jnp.bfloat16)
    stage_out[slot] = cdot(act_low, grad).astype(jnp.bfloat16)
    for copy in sending(p, slot):
        copy.start()
    total = jnp.sum(grad_pre.astype(jnp.float32), axis=0, keepdims=True)
    total = jnp.concatenate([total, total], axis=1)
    row = lax.broadcasted_iota(jnp.int32, (16, D), 0)
    lane = lax.broadcasted_iota(jnp.int32, (16, D), 1)
    mine = (row == p // 2) & (lane // 512 == lax.rem(p, 2))

    @pl.when(p == 0)
    def _():
        sums[...] = jnp.zeros_like(sums)
        back_sum[...] = tdot(grad_pre, w_one)
        part_sum[...] = ndot(act_low, w_two)

    @pl.when((p > 0) & (p < 3))
    def _():
        back_sum[...] += tdot(grad_pre, w_one)
        part_sum[...] += ndot(act_low, w_two)

    @pl.when(p == 3)
    def _():
        back_ref[...] = (back_sum[...] + tdot(grad_pre, w_one)).astype(jnp.bfloat16)
        part_ref[...] = (part_sum[...] + ndot(act_low, w_two)).astype(jnp.bfloat16)

    sums[...] = jnp.where(mine, total, sums[...].astype(jnp.float32)).astype(jnp.bfloat16)

    @pl.when(p == 3)
    def _():
        last = pltpu.make_async_copy(sums, out_ref.at[pl.ds(5632, 16)], sems.at[4])
        last.start()
        for copy in sending(p - 1, 1 - slot) + sending(p, slot):
            copy.wait()
        last.wait()


def ffn(at, att, got, seg, gain, grad, pieces, large, bias, buffer):
    f32, bf16 = jnp.float32, jnp.bfloat16
    whole = pl.BlockSpec((512, D), lambda p, c: (0, 0))
    quarter = lambda q: pl.BlockSpec((1, 128, D), lambda p, c: (4 + q, 4 * c[4] + p, 0))
    return pl.pallas_call(
        ffn_kernel,
        grid_spec=pltpu.PrefetchScalarGridSpec(
            num_scalar_prefetch=1,
            grid=(4,),
            in_specs=[
                whole_spec(512, 512),
                whole_spec(512, 512),
                whole_spec(1, D, D),
                whole,
                whole_spec(1, D),
                whole,
                *([ANY] * 4),
                *(quarter(q) for q in range(4)),
                pl.BlockSpec((1, 1, 512), lambda p, c: (p, 0, 0)),
                HBM,
            ],
            out_specs=[HBM, whole, whole, whole],
            scratch_shapes=[
                pltpu.VMEM(MATS, bf16),
                pltpu.VMEM((512, D), bf16),
                pltpu.VMEM((D, 512), bf16),
                pltpu.VMEM((512, D), bf16),
                pltpu.VMEM((2, D, 512), bf16),
                pltpu.VMEM((2, 512, D), bf16),
                pltpu.VMEM((16, D), bf16),
                pltpu.VMEM((512, D), f32),
                pltpu.VMEM((512, D), f32),
                pltpu.SemaphoreType.DMA((16,)),
                pltpu.SemaphoreType.DMA((5,)),
            ],
        ),
        out_shape=[shape_of((BUFFER, D), bf16), shape_of((512, D), bf16), shape_of((512, D), bf16), shape_of((512, D))],
        input_output_aliases={16: 0},
        compiler_params=params(60),
        cost_estimate=pl.CostEstimate(flops=12 * 512 * 1024 * 2048, bytes_accessed=24 << 20, transcendentals=512 * 2048),
        name="feed_forward",
    )(at, att, got, large, seg, gain, grad, *pieces, large, large, large, large, bias, buffer)


STEP = 128
SLOTS = 16


def widen_kernel(core_ref, second, deps, *refs):
    core = core_ref[0]
    source, outs = refs[0], refs[1 + deps : -4]
    low, high, loads, stores = refs[-4:]
    jobs = []
    if second:
        for q in range(2):
            for r in range(512 // STEP):
                rows = pl.ds(512 * q + STEP * r, STEP)
                lanes = pl.ds(pl.multiple_of(D * (2 * (1 - core) + q), D), D)
                jobs.append((rows, outs[0].at[pl.ds(STEP * r, STEP), lanes]))
    else:
        for r in range(2048 // STEP):
            jobs.append((pl.ds(2048 + STEP * r, STEP), outs[1].at[pl.ds(STEP * r, STEP)]))
        for r in range(1536 // STEP):
            jobs.append((pl.ds(4096 + STEP * r, STEP), outs[2].at[pl.ds(STEP * r, STEP)]))
        for q in range(2):
            for r in range(512 // STEP):
                rows = pl.ds(pl.multiple_of(D * q + 512 * core + STEP * r, STEP), STEP)
                lanes = pl.ds(pl.multiple_of(D * (2 * core + q), D), D)
                jobs.append((rows, outs[0].at[pl.ds(STEP * r, STEP), lanes]))

    def load(k):
        return pltpu.make_async_copy(source.at[jobs[k][0]], low.at[k % SLOTS], loads.at[k % SLOTS])

    def store(k):
        return pltpu.make_async_copy(high.at[k % SLOTS], jobs[k][1], stores.at[k % SLOTS])

    for k in range(min(SLOTS, len(jobs))):
        load(k).start()
    for k in range(len(jobs)):
        load(k).wait()
        if k >= SLOTS:
            store(k - SLOTS).wait()
        high[k % SLOTS] = low[k % SLOTS].astype(jnp.float32)
        store(k).start()
        if k + SLOTS < len(jobs):
            load(k + SLOTS).start()
    for k in range(max(0, len(jobs) - SLOTS), len(jobs)):
        store(k).wait()
    if not second:
        run_copies([pltpu.make_async_copy(source.at[pl.ds(5632, 16)], low.at[0, pl.ds(0, 16)], loads.at[0])])
        sums = low[0, :16, :].astype(jnp.float32)
        for t in range(16):
            outs[3][t : t + 1, :] = sums[t // 8 : t // 8 + 1, 128 * (t % 8) : 128 * (t % 8) + 128]


def widen(core, source, deps, into=None):
    shapes = [(512, FF)] if into is not None else [(512, FF), (2048, D), (1536, D), (16, 128)]
    deps = tuple(deps) + (() if into is None else (into,))

    def body(core_ref, *refs):
        widen_kernel(core_ref, into is not None, len(deps), *refs)

    return pl.pallas_call(
        body,
        in_specs=[SMEM, HBM] + [ANY] * len(deps),
        out_specs=[HBM] * min(len(shapes), 3) + [VMEM] * (len(shapes) - 3),
        out_shape=[shape_of(shape) for shape in shapes],
        input_output_aliases={} if into is None else {1 + len(deps): 0},
        scratch_shapes=[
            pltpu.VMEM((SLOTS, STEP, D), jnp.bfloat16),
            pltpu.VMEM((SLOTS, STEP, D), jnp.float32),
            pltpu.SemaphoreType.DMA((SLOTS,)),
            pltpu.SemaphoreType.DMA((SLOTS,)),
        ],
        compiler_params=params(60 if into is None else 20),
        name="widen_gradients",
    )(core, source, *deps)


def pick_kernel(core_ref, source_ref, *rest):
    del core_ref
    rest[-1][...] = source_ref[...]


def pick_halves(core, buffer, deps):
    return pl.pallas_call(
        pick_kernel,
        grid_spec=pltpu.PrefetchScalarGridSpec(
            num_scalar_prefetch=1,
            grid=(2,),
            in_specs=[pl.BlockSpec((512, D), lambda q, c: (2 * q + 1 - c[0], 0))] + [ANY] * len(deps),
            out_specs=pl.BlockSpec((512, D), lambda q, c: (q, 0)),
        ),
        out_shape=shape_of((D, D), jnp.bfloat16),
        compiler_params=params(60),
        name="other_half",
    )(core, buffer, *deps)


def on_device(
    segment, memory, compressed, mem_count, comp_count, attn_gain, w_query, w_key, w_value, u_bias, v_bias,
    w_rel, w_proj, ffn_gain, w_in, b_in, w_out, b_out, w_comp, b_comp, out_grad, comp_grad,
):
    f32, bf16 = jnp.float32, jnp.bfloat16
    core, chip = lax.axis_index("blk"), lax.axis_index("dp")
    first = core == 0
    core_at = core.reshape(1).astype(jnp.int32)
    coords = {"y": chip // 16, "z": (chip // 4) % 4, "x": chip % 4}
    spots = {}
    for chain in ("AB",):
        spots[chain] = []
        for phase in range(3):
            at = jnp.where(first, coords[PATHS[chain[0]][phase]], coords[PATHS[chain[1]][phase]])
            spots[chain].append(jnp.stack([(at + k) % 4 for k in range(4)] + [core]).astype(jnp.int32))

    def both(own, other, axis=0):
        return jnp.where(first, jnp.concatenate([own, other], axis), jnp.concatenate([other, own], axis))

    def half(array, which, axis):
        size = array.shape[axis] // 2
        return lax.dynamic_slice_in_dim(array, which * size, size, axis)

    where_at = jnp.stack([core, 2 * chip + core]).astype(jnp.int32)
    row = lambda vector: vector.reshape(1, -1)
    blocks, keep, give = pack(
        where_at, w_query, w_key, w_value, w_rel, w_in, w_proj, w_comp, w_out,
        row(attn_gain), row(u_bias), row(v_bias), row(ffn_gain), row(b_in), row(b_out), row(b_comp),
    )
    large = lax.all_gather(blocks, ALL_AXES, axis=1, tiled=True)
    got = swap(give)
    chunk = jnp.concatenate(
        [both(keep[8 * n : 8 * n + 8], got[8 * n : 8 * n + 8]) for n in range(8)] + [keep[64:] + got[64:]]
    )

    pieces = [both(array[0], swap(array[0])) for array in (compressed, memory, segment, out_grad, comp_grad)]
    seg_at = COMP + MEM
    grad_res, comp_flat = pieces[3], pieces[4]
    all_rows = jnp.concatenate(pieces[:3])

    def centre(rows):
        mean = jnp.mean(rows, axis=-1, keepdims=True)
        centred = rows - mean
        return mean, lax.rsqrt(jnp.mean(centred * centred, axis=-1, keepdims=True) + EPSILON)

    mean_one, inverse_one = centre(all_rows.astype(f32))

    distance = (KTOT - 1) - jnp.arange(RELN, dtype=f32)
    frequency = jnp.exp(jnp.arange(D // 2, dtype=f32) * (-2.0 * math.log(10000.0) / D))
    coarse = distance[::32, None] * frequency[None, :]
    fine = jnp.arange(32, dtype=f32)[:, None] * frequency[None, :]
    sin_a, cos_a = (trig(coarse)[:, None, :] for trig in (jnp.sin, jnp.cos))
    sin_b, cos_b = (trig(fine)[None, :, :] for trig in (jnp.sin, jnp.cos))
    sines, cosines = sin_a * cos_b - cos_a * sin_b, cos_a * cos_b + sin_a * sin_b
    table = jnp.concatenate([sines.reshape(RELN, 512), cosines.reshape(RELN, 512)], axis=1)
    table = jnp.where(distance[:, None] >= 0.0, table, 0.0).astype(bf16)

    slot = jnp.arange(MEM, dtype=jnp.int32)
    masked = jnp.where((slot >= MEM - mem_count[0])[:, None], pieces[1], jnp.zeros_like(pieces[1]))
    windows = masked.reshape(MEM // RATE, RATE * D)
    buffer = start_buffer(half(windows, core, 1), comp_flat)

    mats, vecs, panels = gather_steps("AB", chunk, spots["AB"], (mean_one, inverse_one, all_rows, table, buffer))
    vecs = jnp.sum(vecs.astype(f32), axis=(0, 1, 2))
    gain_one, gain_two = vecs[:2].reshape(1, D), vecs[6:8].reshape(1, D)
    bias_u = jnp.where(first, vecs[2], vecs[3])
    bias_v = jnp.where(first, vecs[4], vecs[5])
    joined = ((all_rows.astype(f32) - mean_one) * inverse_one * gain_one).astype(bf16)
    query_rows = ndot(joined[seg_at:], mats[0])
    key_rows = ndot(joined, mats[1]).astype(bf16)
    value_rows = ndot(joined, mats[2]).astype(bf16)
    rel_rows = ndot(table, mats[3]).astype(bf16)
    query_u = (query_rows + bias_u).astype(bf16)
    query_v = (query_rows + bias_v).astype(bf16)
    counts = jnp.concatenate([mem_count, comp_count])
    attended, probs = attn_fwd(counts, query_u, query_v, key_rows, value_rows, rel_rows)

    ffn_bias = vecs[8:12].reshape(4, 1, 512)
    out_bias, comp_bias = vecs[12:14].reshape(1, D), vecs[14:16].reshape(1, D)
    buffer, back, partial, hidden = ffn(
        spots["AB"][2], attended, swap(attended), pieces[2], gain_two, grad_res, panels, large, ffn_bias, buffer
    )
    buffer = lax.psum(buffer, "dp")
    grad_hidden, grad_branch, grad_att, d_gain_two = middle(
        core_at, back, swap(back), hidden, gain_two, grad_res, large
    )

    d_b_out = jnp.sum(half(grad_res, core, 1).astype(f32), axis=0, keepdims=True)
    d_b_comp = jnp.sum(half(comp_flat, core, 1).astype(f32), axis=0, keepdims=True)
    small = jnp.concatenate(
        [jnp.zeros((4, 512), f32), half(d_gain_two, core, 1), d_b_out, d_b_comp, jnp.zeros((1, 512), f32)]
    )
    *pieces_late, grad_query, grad_keys, grad_values = late_gradients(
        spots["AB"][2], probs, grad_att, query_u, query_v, key_rows, value_rows, rel_rows, gain_one, small,
        attended, grad_branch, joined, mats, table,
    )
    share = scatter_steps("AB", pieces_late, spots["AB"])
    keep = half(share[:64], core, 0).astype(bf16)
    mail = swap(jnp.concatenate([half(share[:64], 1 - core, 0), share[80:]]).astype(bf16))
    gains = jnp.where(jnp.arange(8)[:, None] < 2, share[80:] + mail[32:].astype(f32), share[80:])
    late = jnp.concatenate([both(keep, mail[:32]), share[64:80].astype(bf16), gains.astype(bf16)])
    received, passed_on = regather_steps("AB", late, spots["AB"])

    partial_sum = half(partial, core, 0).astype(f32) + swap(half(partial, 1 - core, 0)).astype(f32)
    result = half(hidden, core, 0) + partial_sum + out_bias
    output = result.astype(bf16)

    comp_proj = large[1:4].reshape(3, 128, 8, D).transpose(1, 0, 2, 3).reshape(RATE * D, D)
    new_compressed = (ndot(half(windows, core, 0), comp_proj) + comp_bias).astype(bf16)

    grad_seg = (
        tdot(grad_query, mats[0]) + tdot(grad_keys, mats[1]) + tdot(grad_values, mats[2])
    )
    grad_seg = half(grad_seg, core, 0) + swap(half(grad_seg, 1 - core, 0))
    scaled_one = grad_seg * gain_one
    own_segment = segment[0].astype(f32)
    mean_seg, inverse_seg = centre(own_segment)
    normed_seg = (own_segment - mean_seg) * inverse_seg
    d_segment = half(grad_hidden, core, 0) + inverse_seg * (
        scaled_one
        - jnp.mean(scaled_one, axis=-1, keepdims=True)
        - normed_seg * jnp.mean(scaled_one * normed_seg, axis=-1, keepdims=True)
    )

    deps = passed_on + (output, new_compressed, d_segment)
    others = pick_halves(core_at, buffer, deps)
    d_in, d_out, d_comp, sums = widen(core_at, buffer, deps + (others,))
    *late, d_proj, g1, g2, g3, g4, g5, g6 = finish("AB", spots["AB"][2], received, d_out)
    extra = [array.reshape(512) for array in (g1, g2, g3, g4, g5, g6)]
    (d_in,) = widen(core_at, swap(others), (late[0],), d_in)
    d_b_in = sums.reshape(2048)
    return (
        output[None],
        new_compressed[None],
        d_segment[None],
        extra[0],
        late[0],
        late[1],
        late[2],
        extra[1],
        extra[2],
        late[3],
        d_proj,
        extra[3],
        d_in,
        d_b_in,
        d_out,
        extra[4],
        d_comp,
        extra[5],
    )


def solution(mesh):
    rows, weight, vector = P("dp", "blk", None), P(("dp", "blk"), None), P(("dp", "blk"))
    placed = (
        rows, rows, rows, P("dp"), P("dp"), vector, weight, weight, weight, vector, vector,
        weight, weight, vector, weight, vector, weight, vector, weight, vector, rows, rows,
    )
    half_one, half_two = P("blk"), P("blk", None)
    return jax.shard_map(
        on_device,
        mesh=mesh,
        in_specs=placed,
        out_specs=(
            rows, rows, rows, half_one, half_two, half_two, half_two, half_one, half_one,
            half_two, half_two, half_one, half_two, half_one, half_two, half_one, half_two, half_one,
        ),
        check_vma=False,
    )
```
